32 devices in a mesh: dp: 16 (over z, y, x), chan: 2 (over core).
Axes of the slice: x: 2, y: 2, z: 4, core: 2. Of those that a mesh axis runs over, the one named last changes fastest.
Arguments:
- frames_in: bfloat16 [2, 16, 1024, 512], P(None, 'dp', None, 'chan'), may hold values from -6 to 6
- utter_lengths: int32 [2, 16, 4], P(None, 'dp'), may hold values from 1 to 64, 128 in all within a row
- code_ids: int32 [2, 16, 128], P(None, 'dp'), may hold values from 0 to 8191
- alpha_first: float32 [3, 512], P(None, 'chan'), may hold values from 0.3 to 2
- alpha_second: float32 [3, 512], P(None, 'chan'), may hold values from 0.3 to 2
- alpha_last: float32 [512], P('chan'), may hold values from 0.3 to 2
- w_dilated: bfloat16 [3, 7, 512, 512], P(None, None, None, 'chan'), may hold values from -0.09375 to 0.09375
- w_point: bfloat16 [3, 512, 512], P(None, None, 'chan'), may hold values from -0.25 to 0.25
- w_down: bfloat16 [16, 512, 1024], P(None, None, 'chan'), may hold values from -0.0625 to 0.0625
- w_latent: bfloat16 [1024, 8], P('chan'), may hold values from -0.0390625 to 0.0390625
- w_expand: bfloat16 [8, 1024], P(None, 'chan'), may hold values from -3 to 3
- codebook: float32 [8, 8192], replicated, may hold values from -6 to 6
- out_grad: bfloat16 [2, 16, 128, 1024], P(None, 'dp', None, 'chan'), may hold values from -6 to 6
Outputs:
- block_out: bfloat16 [2, 16, 128, 1024], P(None, 'dp', None, 'chan')
- grad_frames: float32 [2, 16, 1024, 512], P(None, 'dp', None, 'chan')
- grad_alpha_first: float32 [3, 512], P(None, 'chan')
- grad_alpha_second: float32 [3, 512], P(None, 'chan')
- grad_alpha_last: float32 [512], P('chan')
- grad_w_dilated: float32 [3, 7, 512, 512], P(None, None, None, 'chan')
- grad_w_point: float32 [3, 512, 512], P(None, None, 'chan')
- grad_w_down: float32 [16, 512, 1024], P(None, None, 'chan')
- grad_w_latent: float32 [1024, 8], P('chan')
- grad_w_expand: float32 [8, 1024], P(None, 'chan')
- grad_codebook: float32 [8, 8192], replicated
The draws below stay inside these ranges and needn't reach their ends.
Inputs may be any that keep to these rules, and one draw needn't show every extreme that they name: `utter_lengths`: each row's 4 utterance lengths count output frames and sum to 128; the longest of each row has exactly 64.
All inputs are finite; a program needn't handle non-finite values.
Results may differ from the reference program's by a relative error of at most 0.035.
Values may be sent and summed in bfloat16 or wider, within the bound.
No kernel may reach another device: no remote copies, remote signals or barrier semaphores. Data moves between devices by JAX's collectives and lax.ppermute only.
A program may use at most 256 MiB of HBM per device.

```python
import math
import jax
import jax.numpy as jnp
import numpy as np
from jax import lax

C = 512
C2 = 1024
LATENT = 8
CODES = 8192
K = 7
STRIDE = 8
KS = 16
UTTS = 4
MICRO = 2
FRAMES = 1024
ROWS = 16
OUT = 128
MOST = 64


def draw_codebook(key, part):
    key = jax.random.fold_in(key, 17)
    entry_key, scale_key = jax.random.split(key)
    entries = jnp.clip(jax.random.normal(entry_key, (LATENT, CODES), jnp.float32), -4.0, 4.0)
    column_scale = jnp.exp(jax.random.uniform(scale_key, (1, CODES), jnp.float32, math.log(0.15), math.log(1.5)))
    return (entries * column_scale).astype(jnp.float32)


def place_ends(array, key, least, high):
    longest = array.shape.index(max(array.shape))
    spots = []
    for shift in (0, 1):
        where = [jax.random.randint(jax.random.fold_in(key, axis), (), 0, length) for axis, length in enumerate(array.shape)]
        where[longest] = (where[longest] + shift) % array.shape[longest]
        spots.append(tuple(where))
    return array.at[spots[0]].set(least).at[spots[1]].set(high)


def shard_levels(rng, extent, cuts, least, largest):
    gain = 1.0
    for dim, parts in cuts:
        draws = jax.random.uniform(jax.random.fold_in(jax.random.fold_in(rng, 6), dim), (parts,), jnp.float32, least / len(cuts), largest / len(cuts))
        gain = gain * jnp.repeat(jnp.exp(draws), extent[dim] // parts).reshape((-1,) + (1,) * (len(extent) - 1 - dim))
    return gain


def profile(number_of, total, most, lean):
    portions = [(1 << 20) // math.isqrt(grade ** lean) + 1 for grade in range(2, number_of + 1)]
    surplus, given = total - most - (number_of - 1), [1] * (number_of - 1)
    while surplus > 0:
        movable = [i for i in range(number_of - 1) if given[i] < most]
        whole, remaining = sum([portions[i] for i in movable]), surplus
        for i in movable:
            extra = min(most - given[i], max(1, remaining * portions[i] // whole), surplus)
            given[i] = given[i] + extra
            surplus = surplus - extra
    return np.array([most] + given)


def ragged(key, amount, total, bound, lean):
    if amount == 2:
        one = jax.random.randint(key, (), max(1, total - bound), min(bound, total - 1) + 1)
        return jnp.stack([one, total - one])
    sizes = jnp.asarray(profile(amount, total, bound, lean), jnp.int32)
    twos = (amount - 1) // 2
    donor, taker = sizes[1:1 + 2 * twos:2], sizes[2:2 + 2 * twos:2]
    room = jnp.minimum(donor - 1, bound - taker)
    passed = jax.random.randint(jax.random.fold_in(key, 1), (twos,), 0, 1 << 20) % (room + 1)
    sizes = sizes.at[1:1 + 2 * twos:2].set(donor - passed).at[2:2 + 2 * twos:2].set(taker + passed)
    return sizes[jax.random.permutation(jax.random.fold_in(key, 2), amount)]


def gaussian(rng, extent, deviation, most, cuts=(), kind=jnp.bfloat16):
    values = jax.random.normal(rng, extent, jnp.float32) * deviation
    if len(cuts) > 0:
        values = shard_levels(rng, extent, cuts, -0.22, 0.18) * values
    return jnp.clip(values, min=-most, max=most).astype(kind)


def setup_inputs(seed: int = 0) -> dict:
    key_of = jax.random.split(jax.random.key(seed), 14)
    frames_in = gaussian(key_of[0], (MICRO, ROWS, FRAMES, C), 1.0, 6.0, ((1, 16), (3, 2)))
    utter_lengths = jax.vmap(lambda own: ragged(own, UTTS, OUT, MOST, 1))(jax.random.split(key_of[1], MICRO * ROWS)).reshape((MICRO, ROWS, UTTS)).astype(jnp.int32)
    code_ids = place_ends(jax.random.randint(key_of[2], (MICRO, ROWS, OUT), 0, CODES), jax.random.fold_in(key_of[2], 1), 0, CODES - 1).astype(jnp.int32)
    alpha_first = jnp.clip(jnp.exp(math.log(2.0) - 1.89712 * jax.random.uniform(key_of[3], (3, C), jnp.float32) ** shard_levels(key_of[3], (3, C), ((1, 2),), -0.2, 0.2)), 0.3, 2.0)
    alpha_second = jnp.clip(jnp.exp(math.log(2.0) - 1.89712 * jax.random.uniform(key_of[4], (3, C), jnp.float32) ** shard_levels(key_of[4], (3, C), ((1, 2),), -0.2, 0.2)), 0.3, 2.0)
    alpha_last = jnp.clip(jnp.exp(math.log(2.0) - 1.89712 * jax.random.uniform(key_of[5], (C,), jnp.float32) ** shard_levels(key_of[5], (C,), ((0, 2),), -0.2, 0.2)), 0.3, 2.0)
    w_dilated = gaussian(key_of[6], (3, K, C, C), (K * C) ** -0.5, 0.09375, ((3, 2),))
    w_point = gaussian(key_of[7], (3, C, C), C ** -0.5, 0.25, ((2, 2),))
    w_down = gaussian(key_of[8], (KS, C, C2), (KS * C) ** -0.5, 0.0625, ((2, 2),))
    w_latent = gaussian(key_of[9], (C2, LATENT), (20 * C2) ** -0.5, 0.0390625, ((0, 2),))
    w_expand = gaussian(key_of[10], (LATENT, C2), (LATENT // 2) ** -0.5, 3.0, ((1, 2),))
    codebook = draw_codebook(jax.random.fold_in(key_of[13], 71), 0)
    out_grad = gaussian(key_of[12], (MICRO, ROWS, OUT, C2), 1.0, 6.0, ((1, 16), (3, 2)))
    return {"frames_in": frames_in, "utter_lengths": utter_lengths, "code_ids": code_ids, "alpha_first": alpha_first, "alpha_second": alpha_second, "alpha_last": alpha_last, "w_dilated": w_dilated, "w_point": w_point, "w_down": w_down, "w_latent": w_latent, "w_expand": w_expand, "codebook": codebook, "out_grad": out_grad}


DILATIONS = (1, 3, 9)
HIGHEST_PRECISION = lax.Precision.HIGHEST

@jax.custom_vjp
def low(v):
    return lax.optimization_barrier(v.astype(jnp.bfloat16)).astype(jnp.float32)

@jax.custom_vjp
def low_back(v):
    return v

def low_keep(v):
    return (low(v), None)

def low_pass(kept, grad):
    return (grad,)

def back_keep(v):
    return (v, None)

def back_low(kept, grad):
    return (low(grad),)
low.defvjp(low_keep, low_pass)
low_back.defvjp(back_keep, back_low)

def matmul(left, right):
    return jnp.dot(left, right, precision=HIGHEST_PRECISION, preferred_element_type=jnp.float32)

def shift_rows(signal, offset):
    if offset > 0:
        zero_rows = jnp.zeros((offset,) + signal.shape[1:], signal.dtype)
        return jnp.concatenate([signal[offset:], zero_rows], axis=0)
    if offset < 0:
        zero_rows = jnp.zeros((-offset,) + signal.shape[1:], signal.dtype)
        return jnp.concatenate([zero_rows, signal[:offset]], axis=0)
    return signal

def utterance_ids(lengths, frames):
    utt_ends = jnp.cumsum(lengths).astype(jnp.int32) * STRIDE
    places = jnp.arange(frames, dtype=jnp.int32)
    return (1 + lax.optimization_barrier(jnp.sum((places[:, None] >= utt_ends[None, :]).astype(jnp.int32), axis=1))).astype(jnp.int32)

def dilated_taps(signal, labels, dilation):
    pieces = []
    for tap_index in range(K):
        offset = dilation * (tap_index - K // 2)
        same_utt = (shift_rows(labels, offset) == labels).astype(signal.dtype)
        pieces.append(shift_rows(signal, offset) * same_utt[:, None])
    return jnp.concatenate(pieces, axis=1)

def stride_taps(signal, labels):
    frames, channels = signal.shape
    blocks = signal.reshape(frames // STRIDE, STRIDE, channels)
    block_marks = labels[::STRIDE]
    same_before = (shift_rows(block_marks, -1) == block_marks).astype(signal.dtype)
    same_following = (shift_rows(block_marks, 1) == block_marks).astype(signal.dtype)
    before = shift_rows(blocks, -1)[:, STRIDE // 2:] * same_before[:, None, None]
    following = shift_rows(blocks, 1)[:, :STRIDE // 2] * same_following[:, None, None]
    window = jnp.concatenate([before, blocks, following], axis=1)
    return window.reshape(frames // STRIDE, KS * channels)

def snake_act(signal, sharpness):
    return signal + jnp.square(jnp.sin(sharpness * signal)) / sharpness

def normalize(values, reduce_axis):
    return values * lax.rsqrt(lax.optimization_barrier(jnp.sum(values * values, axis=reduce_axis, keepdims=True)) + 1.0)

def forward(signal, labels, row_codes, alpha_first, alpha_second, alpha_last, w_dilated, w_point, w_down, w_latent, w_expand, codebook):
    running = signal
    for section_index in range(3):
        opened = low(snake_act(running, alpha_first[section_index]))
        stacked = dilated_taps(opened, labels, DILATIONS[section_index])
        dilated_out = low_back(matmul(stacked, w_dilated[section_index].reshape(K * C, C)))
        closed = low(snake_act(dilated_out, alpha_second[section_index]))
        running = running + low_back(matmul(closed, w_point[section_index]))
    opened_last = low(snake_act(running, alpha_last))
    hidden = low(low_back(matmul(stride_taps(opened_last, labels), w_down.reshape(KS * C, C2))))
    latent = matmul(hidden, w_latent)
    latent_unit = normalize(latent, 1)
    code_unit = normalize(codebook, 0)
    selector = (row_codes[:, None] == jnp.arange(CODES, dtype=jnp.int32)[None, :]).astype(jnp.float32)
    chosen = lax.dot_general(selector, code_unit, (((1,), (1,)), ((), ())), precision=HIGHEST_PRECISION, preferred_element_type=jnp.float32)
    mixed_code = low(latent_unit + chosen)
    return matmul(mixed_code, w_expand)

def reference(frames_in, utter_lengths, code_ids, alpha_first, alpha_second, alpha_last, w_dilated, w_point, w_down, w_latent, w_expand, codebook, out_grad):
    weights = tuple((weight.astype(jnp.float32) for weight in (alpha_first, alpha_second, alpha_last, w_dilated, w_point, w_down, w_latent, w_expand, codebook)))
    rows_in = frames_in.reshape(-1, FRAMES, C).astype(jnp.float32)
    lengths_all = utter_lengths.reshape(-1, UTTS)
    codes_all = code_ids.reshape(-1, OUT)
    grads_all = out_grad.reshape(-1, OUT, C2).astype(jnp.float32)

    def one_row(totals, row_data):
        signal, lengths, row_codes, cotangent = row_data
        labels = utterance_ids(lengths, FRAMES)

        def run(values, *params):
            return forward(values, labels, row_codes, *params)
        result, pullback = jax.vjp(run, signal, *weights)
        cotangents = pullback(cotangent)
        totals = tuple((total_grad + new_grad for total_grad, new_grad in zip(totals, cotangents[1:])))
        return (totals, (result.astype(jnp.bfloat16), cotangents[0]))
    zero_grads = tuple((jnp.zeros_like(weight) for weight in weights))
    totals, (outputs, input_grads) = lax.scan(one_row, zero_grads, (rows_in, lengths_all, codes_all, grads_all))
    return (outputs.reshape(MICRO, ROWS, OUT, C2), input_grads.reshape(MICRO, ROWS, FRAMES, C), totals[0], totals[1], totals[2], totals[3], totals[4], totals[5], totals[6], totals[7], totals[8])
```

```python
import jax
import jax.numpy as jnp
from jax import lax
from jax.sharding import PartitionSpec as P

K = 7
STRIDE = 8
KS = 16
DILATIONS = (1, 3, 9)
HIGHEST = lax.Precision.HIGHEST
BF = jnp.bfloat16
F32 = jnp.float32


def shift_rows(signal, offset):
    if offset > 0:
        zero_rows = jnp.zeros((offset,) + signal.shape[1:], signal.dtype)
        return jnp.concatenate([signal[offset:], zero_rows], axis=0)
    if offset < 0:
        zero_rows = jnp.zeros((-offset,) + signal.shape[1:], signal.dtype)
        return jnp.concatenate([zero_rows, signal[:offset]], axis=0)
    return signal


def utterance_ids(lengths, frames):
    utt_ends = jnp.cumsum(lengths) * STRIDE
    places = jnp.arange(frames, dtype=jnp.int32)
    return 1 + jnp.sum((places[:, None] >= utt_ends[None, :]).astype(jnp.int32), axis=1)


def stacked_taps(signal, labels, dilation, sign):
    pieces = []
    for tap_index in range(K):
        offset = sign * dilation * (tap_index - K // 2)
        same_utt = (shift_rows(labels, offset) == labels).astype(signal.dtype)
        pieces.append(shift_rows(signal, offset) * same_utt[:, None])
    return jnp.concatenate(pieces, axis=1)


def snake_parts(signal, sharpness):
    turns = signal * (sharpness * (1.0 / jnp.pi))
    turns = turns - jnp.round(turns)
    sine = jnp.sin(jnp.pi * turns)
    cosine = jnp.cos(jnp.pi * turns)
    return sine, cosine


def snake_act(signal, sharpness):
    return signal + jnp.square(jnp.sin(sharpness * signal)) / sharpness


def normalize(values, reduce_axis):
    return values * lax.rsqrt(jnp.sum(values * values, axis=reduce_axis, keepdims=True) + 1.0)


def contract_rows(left, right):
    return lax.dot_general(left, right, (((0,), (0,)), ((), ())), preferred_element_type=F32)


def contract_cols(left, right):
    return lax.dot_general(left, right, (((1,), (1,)), ((), ())), preferred_element_type=F32)


def chip_grid(count):
    bits = count.bit_length() - 1
    side = 1 << (bits // 3)
    return ((1, side), (side, side), (side * side, count // (side * side)))


def ring_pairs(count, step, size):
    pairs = []
    for index in range(count):
        place = (index // step) % size
        pairs.append((index, index + (((place + 1) % size) - place) * step))
    return pairs


def scatter_axis(part, count, step, size):
    place = (lax.axis_index("dp") // step) % size
    rows = part.shape[0] // size
    pairs = ring_pairs(count, step, size)

    def block(back):
        start = lax.rem(place + (2 * size - back), size) * rows
        return lax.dynamic_slice_in_dim(part, start, rows, 0)

    moving = block(1)
    for turn in range(size - 1):
        got = lax.ppermute(moving, "dp", pairs)
        moving = (got.astype(F32) + block(2 + turn).astype(F32)).astype(BF)
    return moving


def gather_axis(part, count, step, size):
    place = (lax.axis_index("dp") // step) % size
    rows = part.shape[0]
    pairs = ring_pairs(count, step, size)
    whole = jnp.zeros((size * rows,) + part.shape[1:], part.dtype)
    whole = lax.dynamic_update_slice_in_dim(whole, part, place * rows, 0)
    moving = part
    for turn in range(size - 1):
        moving = lax.ppermute(moving, "dp", pairs)
        start = lax.rem(place + (2 * size - 1 - turn), size) * rows
        whole = lax.dynamic_update_slice_in_dim(whole, moving, start, 0)
    return whole


def sum_over_chips(part, count, order):
    axes = [chip_grid(count)[index] for index in order]
    for step, size in axes:
        part = scatter_axis(part, count, step, size)
    for step, size in reversed(axes):
        part = gather_axis(part, count, step, size)
    return part


def sum_chunk(chunk, count):
    rows = chunk.shape[0] // 128
    third = rows // 3
    cuts = [0, (rows - third) // 2, 2 * ((rows - third) // 2), rows]
    orders = ((0, 1, 2), (1, 2, 0), (2, 0, 1))
    parts = []
    for index in range(3):
        piece = chunk[cuts[index] * 128 : cuts[index + 1] * 128]
        parts.append(sum_over_chips(piece, count, orders[index]))
    return jnp.concatenate(parts, axis=0)


def sum_small(values, count):
    for step, size in chip_grid(count):
        pairs = ring_pairs(count, step, size)
        moving = values
        total = values
        for _ in range(size - 1):
            moving = lax.ppermute(moving, "dp", pairs)
            total = total + moving
        values = total
    return values


def swap(values):
    return lax.ppermute(values, "chan", [(0, 1), (1, 0)])


def shards(
    frames_in,
    utter_lengths,
    code_ids,
    alpha_first,
    alpha_second,
    alpha_last,
    w_dilated,
    w_point,
    w_down,
    w_latent,
    w_expand,
    codebook,
    out_grad,
):
    count = lax.axis_size("dp")
    core = lax.axis_index("chan")
    frames = frames_in.shape[2]
    half = frames_in.shape[3]
    full = 2 * half
    out_frames = frames // STRIDE
    latent_width = codebook.shape[0]

    def join(mine, other, axis):
        return jnp.where(
            core == 0,
            jnp.concatenate([mine, other], axis=axis),
            jnp.concatenate([other, mine], axis=axis),
        )

    def own_half(values, axis):
        return lax.dynamic_slice_in_dim(values, core * half, half, axis)

    def other_half(values, axis):
        return lax.dynamic_slice_in_dim(values, (1 - core) * half, half, axis)

    def mine_of(values):
        return lax.dynamic_index_in_dim(values, core, 0, keepdims=False)

    def other_of(values):
        return lax.dynamic_index_in_dim(values, 1 - core, 0, keepdims=False)

    running = join(
        mine_of(frames_in)[0], swap(other_of(frames_in)[0]), 1
    ).astype(F32)
    lengths = mine_of(utter_lengths)[0]
    lengths_other = other_of(utter_lengths)[0]
    labels = utterance_ids(lengths, frames)
    labels_other = utterance_ids(lengths_other, frames)
    alphas = join(
        jnp.concatenate([alpha_first, alpha_second, alpha_last[None]], axis=0),
        swap(jnp.concatenate([alpha_first, alpha_second, alpha_last[None]], axis=0)),
        1,
    )
    w_full = [
        join(w_dilated[u], swap(w_dilated[u]), 2).reshape(K * full, full) for u in range(3)
    ]
    p_full = [join(w_point[u], swap(w_point[u]), 1) for u in range(3)]

    down_code = jnp.einsum("kco,ol->ckl", w_down, w_latent, preferred_element_type=F32)
    down_code = down_code.reshape(full, KS * latent_width)
    down_code = down_code + swap(down_code)

    ids = mine_of(code_ids)[0]
    code_range = jnp.arange(codebook.shape[1], dtype=jnp.int32)
    selector = (ids[:, None] == code_range[None, :]).astype(F32)
    code_unit, code_back = jax.vjp(lambda values: normalize(values, 0), codebook)
    chosen = lax.dot_general(
        selector, code_unit, (((1,), (1,)), ((), ())), precision=HIGHEST, preferred_element_type=F32
    )
    grad_parts = [contract_cols(out_grad[m, 0], w_expand) for m in range(2)]
    grad_parts = jnp.stack(grad_parts)
    grad_mixed = mine_of(grad_parts) + swap(other_of(grad_parts))
    code_sum = lax.dot_general(
        grad_mixed, selector, (((0,), (0,)), ((), ())), precision=HIGHEST, preferred_element_type=F32
    )

    kept = []
    for u in range(3):
        opened = snake_act(running, alphas[u]).astype(BF)
        opened_other = swap(opened)
        stacked = stacked_taps(opened, labels, DILATIONS[u], 1)
        dilated_out = jnp.dot(stacked, w_full[u], preferred_element_type=F32)
        closed = snake_act(dilated_out, alphas[3 + u]).astype(BF)
        closed_other = swap(closed)
        kept.append((running, opened, opened_other, dilated_out, closed, closed_other))
        running = running + jnp.dot(closed, p_full[u], preferred_element_type=F32)

    opened_last = snake_act(running, alphas[6]).astype(BF)
    width = KS * latent_width
    place = jnp.arange(frames, dtype=jnp.int32)[:, None] % STRIDE
    tap = jnp.arange(width, dtype=jnp.int32)[None, :] // latent_width
    pattern = (tap % STRIDE == (place + STRIDE // 2) % STRIDE).astype(F32)
    marks = labels[::STRIDE]
    same_before = (shift_rows(marks, -1) == marks).astype(F32)[:, None]
    same_after = (shift_rows(marks, 1) == marks).astype(F32)[:, None]
    lane = jnp.arange(width, dtype=jnp.int32)[None, :]
    early = lane < 4 * latent_width
    late = lane >= 12 * latent_width
    fold = (lane.T % latent_width == jnp.arange(latent_width)[None, :]).astype(F32)
    products = jnp.dot(opened_last.astype(F32), down_code, precision=HIGHEST)
    sums = jnp.sum((products * pattern).reshape(out_frames, STRIDE, width), axis=1)
    sums = jnp.where(
        early,
        same_before * shift_rows(sums, -1),
        jnp.where(late, same_after * shift_rows(sums, 1), sums),
    )
    latent = jnp.dot(sums, fold, precision=HIGHEST)
    latent_unit, latent_back = jax.vjp(lambda values: normalize(values, 1), latent)
    mixed_code = (latent_unit + chosen).astype(BF)
    mixed_other = swap(mixed_code)
    mixed_both = jnp.where(
        core == 0, jnp.stack([mixed_code, mixed_other]), jnp.stack([mixed_other, mixed_code])
    )
    block_out = jnp.einsum(
        "mjl,lo->mjo", mixed_both, w_expand, preferred_element_type=F32
    ).astype(BF)[:, None]
    expand_sum = jnp.einsum(
        "mjl,mjo->lo", mixed_both, out_grad[:, 0], preferred_element_type=F32
    )
    grad_latent = latent_back(grad_mixed)[0]
    spread = jnp.tile(grad_latent, (1, KS))
    spread = jnp.where(
        early,
        shift_rows(same_before * spread, 1),
        jnp.where(late, shift_rows(same_after * spread, -1), spread),
    )
    spread = jnp.repeat(spread, STRIDE, axis=0) * pattern
    down_sum = lax.dot_general(
        opened_last.astype(F32), spread, (((0,), (0,)), ((), ())), precision=HIGHEST
    )
    grad_last = lax.dot_general(
        spread, down_code, (((1,), (1,)), ((), ())), precision=HIGHEST
    )
    grad_running, grad_rate_last = jax.vjp(snake_act, running, alphas[6])[1](grad_last)

    rate_sums = [None] * 6 + [grad_rate_last]
    chunks = [None] * 3
    for u in (2, 1, 0):
        running_in, opened, opened_other, dilated_out, closed, closed_other = kept[u]
        grad_point = grad_running.astype(BF)
        grad_closed = contract_cols(grad_point, p_full[u])
        grad_dilated, rate = jax.vjp(snake_act, dilated_out, alphas[3 + u])[1](grad_closed)
        rate_sums[3 + u] = rate
        grad_dilated = grad_dilated.astype(BF)
        point_other = swap(other_half(grad_point, 1))
        dilated_other = swap(other_half(grad_dilated, 1))
        stacked = stacked_taps(grad_dilated, labels, DILATIONS[u], -1)
        grad_opened = contract_cols(
            stacked,
            jnp.transpose(w_full[u].reshape(K, full, full), (1, 0, 2)).reshape(full, K * full),
        )
        stacked_own = stacked_taps(own_half(grad_dilated, 1), labels, DILATIONS[u], -1)
        stacked_other = stacked_taps(dilated_other, labels_other, DILATIONS[u], -1)
        conv = contract_rows(opened, stacked_own) + contract_rows(opened_other, stacked_other)
        conv = jnp.transpose(conv.astype(BF).reshape(full, K, half), (1, 0, 2))
        point = contract_rows(closed, own_half(grad_point, 1)) + contract_rows(
            closed_other, point_other
        )
        pieces = [conv.reshape(K * full, half), point.astype(BF)]
        if u == 2:
            down_half = lax.dynamic_slice_in_dim(down_sum, core * half, half, 0) + swap(
                lax.dynamic_slice_in_dim(down_sum, (1 - core) * half, half, 0)
            )
            code_width = codebook.shape[1] // 2
            code_half = lax.dynamic_slice_in_dim(code_sum, core * code_width, code_width, 1) + swap(
                lax.dynamic_slice_in_dim(code_sum, (1 - core) * code_width, code_width, 1)
            )
            pieces += [
                down_half.astype(BF).reshape(-1, half),
                code_half.astype(BF).reshape(-1, half),
            ]
        chunks[u] = sum_chunk(jnp.concatenate(pieces, axis=0), count)
        grad_input, rate = jax.vjp(snake_act, running_in, alphas[u])[1](grad_opened)
        rate_sums[u] = rate
        grad_running = grad_running + grad_input

    rates = jnp.stack(rate_sums)
    rates = own_half(rates, 1) + swap(other_half(rates, 1))
    small = jnp.concatenate([rates, expand_sum.reshape(-1, half)], axis=0)
    small = sum_small(small, count)
    conv_rows = K * full
    w_rows = conv_rows + full
    down_rows = full * width // 2 // half
    down_half = chunks[2][w_rows : w_rows + down_rows].reshape(half, width)
    code_half = chunks[2][w_rows + down_rows :].reshape(latent_width, codebook.shape[1] // 2)
    down_total = join(down_half, swap(down_half), 0).astype(F32)
    code_total = join(code_half, swap(code_half), 1).astype(F32)
    down_taps = jnp.transpose(down_total.reshape(full, KS, latent_width), (1, 0, 2))
    grad_w_down = jnp.einsum(
        "kcl,ol->kco", down_taps, w_latent.astype(F32), preferred_element_type=F32
    )
    grad_w_latent = jnp.einsum(
        "kco,kcl->ol", w_down, down_taps.astype(BF), preferred_element_type=F32
    )
    grad_codebook = code_back(code_total)[0]

    sent = swap(other_half(grad_running, 1))
    kept_half = own_half(grad_running, 1)
    grad_frames = jnp.where(
        core == 0, jnp.stack([kept_half, sent]), jnp.stack([sent, kept_half])
    )[:, None]
    return (
        block_out,
        grad_frames,
        small[0:3],
        small[3:6],
        small[6],
        jnp.stack([chunks[u][:conv_rows] for u in range(3)])
        .astype(F32)
        .reshape(3, K, full, half),
        jnp.stack([chunks[u][conv_rows:w_rows] for u in range(3)]).astype(F32),
        grad_w_down,
        grad_w_latent,
        small[7:].reshape(latent_width, -1),
        grad_codebook,
    )


def solution(mesh):
    placed = (
        P(None, "dp", None, "chan"),
        P(None, "dp", None),
        P(None, "dp", None),
        P(None, "chan"),
        P(None, "chan"),
        P("chan"),
        P(None, None, None, "chan"),
        P(None, None, "chan"),
        P(None, None, "chan"),
        P("chan", None),
        P(None, "chan"),
        P(),
        P(None, "dp", None, "chan"),
    )
    return jax.shard_map(
        shards,
        mesh=mesh,
        in_specs=placed,
        out_specs=(
            P(None, "dp", None, "chan"),
            P(None, "dp", None, "chan"),
            P(None, "chan"),
            P(None, "chan"),
            P("chan"),
            P(None, None, None, "chan"),
            P(None, None, "chan"),
            P(None, None, "chan"),
            P("chan", None),
            P(None, "chan"),
            P(),
        ),
        check_vma=False,
    )
```

```python
import functools
import jax
import jax.numpy as jnp
from jax import lax
from jax.experimental import pallas as pl
from jax.experimental.pallas import tpu as pltpu
from jax.sharding import PartitionSpec as P

K = 7
STRIDE = 8
KS = 16
DILATIONS = (1, 3, 9)
BF = jnp.bfloat16
F32 = jnp.float32
HALO = 32
TILE = 256
LANES = 128
SINE = (3.141592580569316, -5.1677069002071025, 2.550031640919103, -0.5980464504720939, 0.0772222489218058)
COSINE = (0.9999999534666402, -4.934792858671753, 4.058411914096722, -1.3318801607983635, 0.2196967977026182)
VMEM_LIMIT = 60 * 1024 * 1024
ANY = pl.BlockSpec(memory_space=pl.ANY)
SMEM = pl.BlockSpec(memory_space=pltpu.SMEM)
VMEM = pl.BlockSpec(memory_space=pltpu.VMEM)


def dot(left, right):
    return jnp.dot(left, right, preferred_element_type=F32)


def dot_cols(left, right):
    return lax.dot_general(left, right, (((1,), (1,)), ((), ())), preferred_element_type=F32)


def poly(u, terms):
    total = terms[-1]
    for term in terms[-2::-1]:
        total = total * u + term
    return total


def half_turns(v, alpha):
    turns = v * (alpha * 0.3183098861837907)
    return turns - jnp.round(turns)


def snake(v, alpha):
    t = half_turns(v, alpha)
    u = t * t
    p = poly(u, SINE)
    return v + (u * (p * p)) * (1.0 / alpha)


def snake_slopes(v, alpha):
    t = half_turns(v, alpha)
    u = t * t
    sine = t * poly(u, SINE)
    double = 2.0 * sine * poly(u, COSINE)
    return sine * sine, double


def put_labels(label_ref, meta_ref, base, utts, frames):
    t = lax.broadcasted_iota(jnp.int32, label_ref.shape, 0) - HALO
    label = jnp.zeros(label_ref.shape, jnp.int32)
    for utt in range(utts):
        label = label + (t >= meta_ref[base + utt]).astype(jnp.int32)
    label_ref[...] = jnp.where((t < 0) | (t >= frames), -1, label)


def tap(padded_ref, label_ref, row, rows, offset):
    here = HALO + row
    width = padded_ref.shape[1]
    same = label_ref[here + offset : here + offset + rows, :] == label_ref[here : here + rows, :]
    pieces = []
    for lane in range(0, width, LANES):
        piece = padded_ref[here + offset : here + offset + rows, lane : lane + LANES]
        pieces.append(jnp.where(same, piece, 0.0).astype(BF))
    return jnp.concatenate(pieces, axis=1)


def column_half(core, half):
    return pl.ds(pl.multiple_of(core * half, half), half)


def forward_kernel(utts, dilation, first, *refs):
    if first:
        (meta, alpha_in, alpha_mid, mine, other, w_mine, w_other, p_mine, p_other,
         keep, opened_t, dilated, closed_t, after,
         mine_v, other_v, running_v, padded, label, taps, wm_v, wo_v, pm_v, po_v, mid_v, ot_v, ct_v, after_v, sem, out_sem) = refs
    else:
        (meta, alpha_in, alpha_mid, running, w_mine, w_other, p_mine, p_other,
         opened_t, dilated, closed_t, after,
         running_v, padded, label, taps, wm_v, wo_v, pm_v, po_v, mid_v, ot_v, ct_v, after_v, sem, out_sem) = refs
    frames, full = running_v.shape
    half = full // 2
    tiles = frames // TILE
    core = meta[2 * utts]
    own = column_half(core, half)
    oth = column_half(1 - core, half)
    outs = []

    def send(source, target):
        copy = pltpu.make_async_copy(source, target, out_sem.at[len(outs)])
        copy.start()
        outs.append(copy)

    loads = []
    if first:
        for place, (source, target) in enumerate(((mine, mine_v), (other, other_v))):
            loads.append(pltpu.make_async_copy(source, target, sem.at[place]))
    else:
        for tile in range(tiles):
            rows = pl.ds(tile * TILE, TILE)
            loads.append(pltpu.make_async_copy(running.at[rows], running_v.at[rows], sem.at[tile]))
    weights = []
    for place, (source, target) in enumerate(
        ((w_mine, wm_v), (w_other, wo_v), (p_mine, pm_v), (p_other, po_v))
    ):
        weights.append(pltpu.make_async_copy(source, target, sem.at[tiles + place]))
    for copy in loads + weights:
        copy.start()
    put_labels(label, meta, 0, utts, frames)
    edge = jnp.zeros((HALO, full), F32)
    padded[:HALO, :] = edge
    padded[HALO + frames :, :] = edge
    rate_in = alpha_in[...]
    rate_mid = alpha_mid[...]
    if first:
        for copy in loads:
            copy.wait()
    for tile in range(tiles):
        rows = slice(tile * TILE, (tile + 1) * TILE)
        if first:
            running_v[rows, own] = mine_v[rows, :].astype(F32)
            running_v[rows, oth] = other_v[rows, :].astype(F32)
            send(running_v.at[pl.ds(tile * TILE, TILE)], keep.at[pl.ds(tile * TILE, TILE)])
        else:
            loads[tile].wait()
        opened = snake(running_v[rows, :], rate_in)
        padded[HALO + tile * TILE : HALO + (tile + 1) * TILE, :] = opened
        ot_v[:, rows] = opened.T.astype(BF)
    send(ot_v, opened_t)
    for copy in weights:
        copy.wait()
    for tile in range(tiles):
        rows = slice(tile * TILE, (tile + 1) * TILE)
        there = pl.ds(tile * TILE, TILE)
        slot = tile % 2
        for index in range(K):
            offset = dilation * (index - K // 2)
            taps[slot, :, index * full : (index + 1) * full] = tap(
                padded, label, tile * TILE, TILE, offset
            )
        mid_v[rows, own] = dot(taps[slot], wm_v[...])
        mid_v[rows, oth] = dot(taps[slot], wo_v[...])
        send(mid_v.at[there], dilated.at[there])
        closed = snake(mid_v[rows, :], rate_mid)
        ct_v[:, rows] = closed.T.astype(BF)
        closed = closed.astype(BF)
        after_v[rows, own] = running_v[rows, own] + dot(closed, pm_v[...])
        after_v[rows, oth] = running_v[rows, oth] + dot(closed, po_v[...])
        send(after_v.at[there], after.at[there])
    send(ct_v, closed_t)
    for copy in outs:
        copy.wait()


def run_forward(unit, meta, alpha_in, alpha_mid, inputs, w_mine, w_other, p_mine, p_other, utts):
    first = len(inputs) == 2
    frames = inputs[0].shape[0]
    half = w_mine.shape[1]
    full = 2 * half
    tiles = frames // TILE
    outs = [
        jax.ShapeDtypeStruct((full, frames), BF),
        jax.ShapeDtypeStruct((frames, full), F32),
        jax.ShapeDtypeStruct((full, frames), BF),
        jax.ShapeDtypeStruct((frames, full), F32),
    ]
    scratch = [
        pltpu.VMEM((frames, full), F32),
        pltpu.VMEM((frames + 2 * HALO, full), F32),
        pltpu.VMEM((frames + 2 * HALO, LANES), jnp.int32),
        pltpu.VMEM((2, TILE, K * full), BF),
        pltpu.VMEM(w_mine.shape, BF),
        pltpu.VMEM(w_mine.shape, BF),
        pltpu.VMEM(p_mine.shape, BF),
        pltpu.VMEM(p_mine.shape, BF),
        pltpu.VMEM((frames, full), F32),
        pltpu.VMEM((full, frames), BF),
        pltpu.VMEM((full, frames), BF),
        pltpu.VMEM((frames, full), F32),
        pltpu.SemaphoreType.DMA((tiles + 4,)),
        pltpu.SemaphoreType.DMA((3 * tiles + 2,)),
    ]
    if first:
        outs = [jax.ShapeDtypeStruct((frames, full), F32)] + outs
        scratch = [pltpu.VMEM((frames, half), BF)] * 2 + scratch
    return pl.pallas_call(
        functools.partial(forward_kernel, utts, DILATIONS[unit], first),
        out_shape=outs,
        in_specs=[SMEM, VMEM, VMEM] + [ANY] * (len(inputs) + 4),
        out_specs=[ANY] * len(outs),
        scratch_shapes=scratch,
        compiler_params=pltpu.CompilerParams(vmem_limit_bytes=VMEM_LIMIT),
        cost_estimate=pl.CostEstimate(
            flops=2 * frames * (K + 1) * full * full, bytes_accessed=14 << 20, transcendentals=0
        ),
        name="forward",
    )(meta, alpha_in, alpha_mid, *inputs, w_mine, w_other, p_mine, p_other)


def closing_steps(tile, point, mid, alpha, core_cols, refs):
    gp_v, gd_v, pm_v, po_v = refs
    own, oth = core_cols
    rows = slice(tile * TILE, (tile + 1) * TILE)
    gp_v[rows, :] = point.astype(BF)
    grad = dot_cols(gp_v[rows, own], pm_v[...]) + dot_cols(gp_v[rows, oth], po_v[...])
    square, double = snake_slopes(mid, alpha)
    gd_v[rows, :] = (grad * (1.0 + double)).astype(BF)
    rate = grad * (mid * double - square * (1.0 / alpha))
    return jnp.sum(rate.reshape(TILE // 8, 8, rate.shape[1]), axis=0)


def closing_kernel(utts, meta, alpha, grad, mid, p_mine, p_other,
                   gp_mine, gp_other, gd_mine, gd_other, rates,
                   grad_v, mid_v, pm_v, po_v, gp_v, gd_v, sem, out_sem):
    frames, full = grad_v.shape
    half = full // 2
    tiles = frames // TILE
    core = meta[2 * utts]
    own = column_half(core, half)
    oth = column_half(1 - core, half)
    loads = [
        pltpu.make_async_copy(p_mine, pm_v, sem.at[2 * tiles]),
        pltpu.make_async_copy(p_other, po_v, sem.at[2 * tiles + 1]),
    ]
    for tile in range(tiles):
        there = pl.ds(tile * TILE, TILE)
        loads.append(pltpu.make_async_copy(grad.at[there], grad_v.at[there], sem.at[2 * tile]))
        loads.append(pltpu.make_async_copy(mid.at[there], mid_v.at[there], sem.at[2 * tile + 1]))
    for copy in loads:
        copy.start()
    loads[0].wait()
    loads[1].wait()
    value = alpha[...]
    total = jnp.zeros(rates.shape, F32)
    outs = []
    for tile in range(tiles):
        rows = slice(tile * TILE, (tile + 1) * TILE)
        loads[2 + 2 * tile].wait()
        loads[3 + 2 * tile].wait()
        total = total + closing_steps(
            tile, grad_v[rows, :], mid_v[rows, :], value, (own, oth), (gp_v, gd_v, pm_v, po_v)
        )
        there = pl.ds(tile * TILE, TILE)
        for source, target, cols in (
            (gp_v, gp_mine, own), (gp_v, gp_other, oth), (gd_v, gd_mine, own), (gd_v, gd_other, oth)
        ):
            copy = pltpu.make_async_copy(
                source.at[there, cols], target.at[there], out_sem.at[len(outs)]
            )
            copy.start()
            outs.append(copy)
    rates[...] = total * (1.0 / value)
    for copy in outs:
        copy.wait()


def run_closing(meta, alpha, grad, mid, p_mine, p_other, utts):
    frames, full = grad.shape
    half = full // 2
    tiles = frames // TILE
    part = jax.ShapeDtypeStruct((frames, half), BF)
    return pl.pallas_call(
        functools.partial(closing_kernel, utts),
        out_shape=[part, part, part, part, jax.ShapeDtypeStruct((8, full), F32)],
        in_specs=[SMEM, VMEM] + [ANY] * 4,
        out_specs=[ANY] * 4 + [VMEM],
        scratch_shapes=[
            pltpu.VMEM((frames, full), F32),
            pltpu.VMEM((frames, full), F32),
            pltpu.VMEM(p_mine.shape, BF),
            pltpu.VMEM(p_mine.shape, BF),
            pltpu.VMEM((frames, full), BF),
            pltpu.VMEM((frames, full), BF),
            pltpu.SemaphoreType.DMA((2 * tiles + 2,)),
            pltpu.SemaphoreType.DMA((4 * tiles,)),
        ],
        compiler_params=pltpu.CompilerParams(vmem_limit_bytes=VMEM_LIMIT),
        cost_estimate=pl.CostEstimate(
            flops=2 * frames * full * full, bytes_accessed=8 << 20, transcendentals=0
        ),
        name="closing",
    )(meta, alpha, grad, mid, p_mine, p_other)


def weight_kernel(utts, dilation, meta, ot_mine, ot_other, ct_mine, ct_other,
                  gd_mine, gd_other, gp_mine, gp_other, chunk,
                  ot_v, ct_v, gd_v, gp_v, padded, label, taps, out_v, sem, out_sem):
    frames, half = gd_mine.shape
    full = 2 * half
    loads = []
    for source, target in (
        (gd_mine, gd_v.at[pl.ds(0, frames)]),
        (gd_other, gd_v.at[pl.ds(frames, frames)]),
        (ot_mine, ot_v.at[:, pl.ds(0, frames)]),
        (ot_other, ot_v.at[:, pl.ds(frames, frames)]),
        (ct_mine, ct_v.at[:, pl.ds(0, frames)]),
        (ct_other, ct_v.at[:, pl.ds(frames, frames)]),
        (gp_mine, gp_v.at[pl.ds(0, frames)]),
        (gp_other, gp_v.at[pl.ds(frames, frames)]),
    ):
        loads.append(pltpu.make_async_copy(source, target, sem.at[len(loads)]))
    for copy in loads:
        copy.start()
    edge = jnp.zeros((HALO, half), F32)
    for row in range(2):
        put_labels(label.at[row], meta, row * utts, utts, frames)
        padded[row, :HALO, :] = edge
        padded[row, HALO + frames :, :] = edge
    for row in range(2):
        loads[row].wait()
        padded[row, HALO : HALO + frames, :] = gd_v[row * frames : (row + 1) * frames, :].astype(F32)
    outs = []

    def send(index):
        there = pl.ds(index * full, full)
        copy = pltpu.make_async_copy(out_v.at[there], chunk.at[there], out_sem.at[len(outs)])
        copy.start()
        outs.append(copy)

    loads[2].wait()
    loads[3].wait()
    for index in range(K):
        offset = -dilation * (index - K // 2)
        slot = index % 2
        for row in range(2):
            for start in range(0, frames, TILE):
                taps[slot, row * frames + start : row * frames + start + TILE, :] = tap(
                    padded.at[row], label.at[row], start, TILE, offset
                )
        out_v[index * full : (index + 1) * full, :] = dot(ot_v[...], taps[slot]).astype(BF)
        send(index)
    for copy in loads[4:]:
        copy.wait()
    out_v[K * full :, :] = dot(ct_v[...], gp_v[...]).astype(BF)
    send(K)
    for copy in outs:
        copy.wait()


def run_weight(unit, meta, ot_mine, ot_other, ct_mine, ct_other, gd_mine, gd_other, gp_mine, gp_other, utts):
    frames, half = gd_mine.shape
    full = 2 * half
    return pl.pallas_call(
        functools.partial(weight_kernel, utts, DILATIONS[unit]),
        out_shape=jax.ShapeDtypeStruct(((K + 1) * full, half), BF),
        in_specs=[SMEM] + [ANY] * 8,
        out_specs=ANY,
        scratch_shapes=[
            pltpu.VMEM((full, 2 * frames), BF),
            pltpu.VMEM((full, 2 * frames), BF),
            pltpu.VMEM((2 * frames, half), BF),
            pltpu.VMEM((2 * frames, half), BF),
            pltpu.VMEM((2, frames + 2 * HALO, half), F32),
            pltpu.VMEM((2, frames + 2 * HALO, LANES), jnp.int32),
            pltpu.VMEM((2, 2 * frames, half), BF),
            pltpu.VMEM(((K + 1) * full, half), BF),
            pltpu.SemaphoreType.DMA((8,)),
            pltpu.SemaphoreType.DMA((K + 1,)),
        ],
        compiler_params=pltpu.CompilerParams(vmem_limit_bytes=VMEM_LIMIT),
        cost_estimate=pl.CostEstimate(
            flops=4 * frames * (K + 1) * full * half, bytes_accessed=8 << 20, transcendentals=0
        ),
        name="weight_grads",
    )(meta, ot_mine, ot_other, ct_mine, ct_other, gd_mine, gd_other, gp_mine, gp_other)


def opening_kernel(utts, dilation, meta, alpha, gd_mine, gd_other, running, grad, w_mine, w_other,
                   after, rates,
                   gm_v, go_v, padded, label, taps, running_v, grad_v, wm_v, wo_v, after_v, sem, out_sem):
    frames, full = running_v.shape
    half = full // 2
    tiles = frames // TILE
    loads = []
    for source, target in ((gd_mine, gm_v), (gd_other, go_v), (w_mine, wm_v), (w_other, wo_v)):
        loads.append(pltpu.make_async_copy(source, target, sem.at[len(loads)]))
    for tile in range(tiles):
        there = pl.ds(tile * TILE, TILE)
        for source, target in ((running, running_v), (grad, grad_v)):
            loads.append(
                pltpu.make_async_copy(source.at[there], target.at[there], sem.at[len(loads)])
            )
    for copy in loads:
        copy.start()
    put_labels(label, meta, 0, utts, frames)
    edge = jnp.zeros((HALO, half), F32)
    for part, values in ((0, gm_v), (1, go_v)):
        padded[part, :HALO, :] = edge
        padded[part, HALO + frames :, :] = edge
        loads[part].wait()
        padded[part, HALO : HALO + frames, :] = values[...].astype(F32)
    loads[2].wait()
    loads[3].wait()
    value = alpha[...]
    total = jnp.zeros(rates.shape, F32)
    outs = []
    for tile in range(tiles):
        rows = slice(tile * TILE, (tile + 1) * TILE)
        there = pl.ds(tile * TILE, TILE)
        opened = jnp.zeros((TILE, full), F32)
        for index in range(K):
            offset = -dilation * (index - K // 2)
            for part, weight in ((0, wm_v), (1, wo_v)):
                piece = tap(padded.at[part], label, tile * TILE, TILE, offset)
                opened = opened + dot_cols(piece, weight[index * full : (index + 1) * full, :])
        loads[4 + 2 * tile].wait()
        loads[5 + 2 * tile].wait()
        v = running_v[rows, :]
        square, double = snake_slopes(v, value)
        after_v[rows, :] = grad_v[rows, :] + opened * (1.0 + double)
        rate = opened * (v * double - square * (1.0 / value))
        total = total + jnp.sum(rate.reshape(TILE // 8, 8, full), axis=0)
        copy = pltpu.make_async_copy(after_v.at[there], after.at[there], out_sem.at[tile])
        copy.start()
        outs.append(copy)
    rates[...] = total * (1.0 / value)
    for copy in outs:
        copy.wait()


def run_opening(unit, meta, alpha, gd_mine, gd_other, running, grad, w_mine, w_other, utts):
    frames, full = running.shape
    half = full // 2
    tiles = frames // TILE
    return pl.pallas_call(
        functools.partial(opening_kernel, utts, DILATIONS[unit]),
        out_shape=[
            jax.ShapeDtypeStruct((frames, full), F32),
            jax.ShapeDtypeStruct((8, full), F32),
        ],
        in_specs=[SMEM, VMEM] + [ANY] * 6,
        out_specs=[ANY, VMEM],
        scratch_shapes=[
            pltpu.VMEM((frames, half), BF),
            pltpu.VMEM((frames, half), BF),
            pltpu.VMEM((2, frames + 2 * HALO, half), F32),
            pltpu.VMEM((frames + 2 * HALO, LANES), jnp.int32),
            pltpu.VMEM((8, 128), BF),
            pltpu.VMEM((frames, full), F32),
            pltpu.VMEM((frames, full), F32),
            pltpu.VMEM(w_mine.shape, BF),
            pltpu.VMEM(w_mine.shape, BF),
            pltpu.VMEM((frames, full), F32),
            pltpu.SemaphoreType.DMA((4 + 2 * tiles,)),
            pltpu.SemaphoreType.DMA((tiles,)),
        ],
        compiler_params=pltpu.CompilerParams(vmem_limit_bytes=VMEM_LIMIT),
        cost_estimate=pl.CostEstimate(
            flops=2 * frames * K * full * full, bytes_accessed=11 << 20, transcendentals=0
        ),
        name="opening",
    )(meta, alpha, gd_mine, gd_other, running, grad, w_mine, w_other)


def split(values, terms):
    parts = []
    for _ in range(terms):
        part = values.astype(BF)
        parts.append(part)
        values = values - part.astype(F32)
    return parts


def code_kernel(utts, meta, alpha_last, alpha_mid, running, mid, p_mine, p_other, down, down_t, chosen, grad_code,
                grad_out, mixed, down_sum, last_rates, gp_mine, gp_other, gd_mine, gd_other, rates,
                running_v, mid_v, pm_v, po_v, opened_v, square_v, double_v, out_v, gp_v, gd_v, sem, out_sem):
    frames, full = running_v.shape
    half = full // 2
    tiles = frames // TILE
    blocks = frames // STRIDE
    core = meta[2 * utts]
    own = column_half(core, half)
    oth = column_half(1 - core, half)
    loads = []
    for tile in range(tiles):
        there = pl.ds(tile * TILE, TILE)
        loads.append(pltpu.make_async_copy(running.at[there], running_v.at[there], sem.at[tile]))
    for tile in range(tiles):
        there = pl.ds(tile * TILE, TILE)
        loads.append(pltpu.make_async_copy(mid.at[there], mid_v.at[there], sem.at[tiles + tile]))
    loads.append(pltpu.make_async_copy(p_mine, pm_v, sem.at[2 * tiles]))
    loads.append(pltpu.make_async_copy(p_other, po_v, sem.at[2 * tiles + 1]))
    for copy in loads:
        copy.start()
    value = alpha_last[...]
    inverse = 1.0 / value
    width = down.shape[1]
    code = width // KS
    lane = lax.broadcasted_iota(jnp.int32, (TILE, width), 1) // code
    place = lax.broadcasted_iota(jnp.int32, (TILE, width), 0) % STRIDE
    pattern = (lane % STRIDE == (place + STRIDE // 2) % STRIDE).astype(F32)
    down_parts = jnp.concatenate(split(down[...], 3), axis=1)
    sums = []
    for tile in range(tiles):
        rows = slice(tile * TILE, (tile + 1) * TILE)
        loads[tile].wait()
        v = running_v[rows, :]
        square, double = snake_slopes(v, value)
        square_v[rows, :] = square
        double_v[rows, :] = double
        opened = (v + square * inverse).astype(BF)
        opened_v[rows, :] = opened
        products = dot(opened, down_parts)
        products = products[:, :width] + products[:, width : 2 * width] + products[:, 2 * width :]
        products = (products * pattern).reshape(TILE // STRIDE, STRIDE, width)
        sums.append(jnp.sum(products, axis=1))
    sums = jnp.concatenate(sums, axis=0)
    block = lax.broadcasted_iota(jnp.int32, (blocks, width), 0)
    block_lane = lax.broadcasted_iota(jnp.int32, (blocks, width), 1)
    label = jnp.zeros((blocks, width), jnp.int32)
    for utt in range(utts):
        label = label + (block * STRIDE >= meta[utt]).astype(jnp.int32)

    def earlier(values):
        return pltpu.roll(values, 1, 0)

    def later(values):
        return pltpu.roll(values, blocks - 1, 0)

    same_before = jnp.where((block > 0) & (earlier(label) == label), 1.0, 0.0)
    same_after = jnp.where((block < blocks - 1) & (later(label) == label), 1.0, 0.0)
    early = block_lane < 4 * code
    late = block_lane >= 12 * code
    sums = jnp.where(
        early, same_before * earlier(sums), jnp.where(late, same_after * later(sums), sums)
    )
    fold = (
        lax.broadcasted_iota(jnp.int32, (width, width), 0) % code
        == lax.broadcasted_iota(jnp.int32, (width, width), 1) % code
    ).astype(BF)
    latent = dot(jnp.concatenate(split(sums, 3), axis=1), jnp.concatenate([fold] * 3, axis=0))
    scale = lax.rsqrt(jnp.sum(latent * latent, axis=1, keepdims=True) * (1.0 / KS) + 1.0)
    unit = latent * scale
    mixed[...] = (unit + chosen[...]).astype(BF)
    back = grad_code[...]
    along = jnp.sum(unit * back, axis=1, keepdims=True) * (1.0 / KS)
    spread = (back - unit * along) * scale
    spread = jnp.where(
        early,
        later(same_before * spread),
        jnp.where(late, earlier(same_after * spread), spread),
    )
    down_t_parts = split(down_t[...], 2)
    down_t_stack = jnp.concatenate([down_t_parts[0], down_t_parts[1], down_t_parts[0]], axis=0)
    loads[2 * tiles].wait()
    loads[2 * tiles + 1].wait()
    total = jnp.zeros(rates.shape, F32)
    last_total = jnp.zeros(rates.shape, F32)
    down_total = jnp.zeros(down_sum.shape, F32)
    mid_value = alpha_mid[...]
    outs = []
    for tile in range(tiles):
        rows = slice(tile * TILE, (tile + 1) * TILE)
        there = pl.ds(tile * TILE, TILE)
        own_blocks = spread[tile * (TILE // STRIDE) : (tile + 1) * (TILE // STRIDE), :]
        wide = jnp.broadcast_to(
            own_blocks[:, None, :], (TILE // STRIDE, STRIDE, width)
        ).reshape(TILE, width) * pattern
        parts = split(wide, 3)
        sums = lax.dot_general(
            opened_v[rows, :],
            jnp.concatenate(parts, axis=1),
            (((0,), (0,)), ((), ())),
            preferred_element_type=F32,
        )
        down_total = down_total + (sums[:, :width] + sums[:, width : 2 * width] + sums[:, 2 * width :])
        grad_last = dot(jnp.concatenate([parts[0], parts[0], parts[1]], axis=1), down_t_stack)
        v = running_v[rows, :]
        square = square_v[rows, :]
        double = double_v[rows, :]
        grad = grad_last * (1.0 + double)
        out_v[rows, :] = grad
        outs.append(pltpu.make_async_copy(out_v.at[there], grad_out.at[there], out_sem.at[len(outs)]))
        outs[-1].start()
        rate = grad_last * (v * double - square * inverse)
        last_total = last_total + jnp.sum(rate.reshape(TILE // 8, 8, full), axis=0)
        loads[tiles + tile].wait()
        total = total + closing_steps(
            tile, grad, mid_v[rows, :], mid_value, (own, oth), (gp_v, gd_v, pm_v, po_v)
        )
        for source, target, cols in (
            (gp_v, gp_mine, own), (gp_v, gp_other, oth), (gd_v, gd_mine, own), (gd_v, gd_other, oth)
        ):
            outs.append(
                pltpu.make_async_copy(source.at[there, cols], target.at[there], out_sem.at[len(outs)])
            )
            outs[-1].start()
    rates[...] = total * (1.0 / mid_value)
    last_rates[...] = last_total * inverse
    down_sum[...] = down_total
    for copy in outs:
        copy.wait()


def run_code(meta, alpha_last, alpha_mid, running, mid, p_mine, p_other, down, chosen, grad_code, utts):
    frames, full = running.shape
    half = full // 2
    tiles = frames // TILE
    width = down.shape[1]
    blocks = frames // STRIDE
    part = jax.ShapeDtypeStruct((frames, half), BF)
    return pl.pallas_call(
        functools.partial(code_kernel, utts),
        out_shape=[
            jax.ShapeDtypeStruct((frames, full), F32),
            jax.ShapeDtypeStruct((blocks, width), BF),
            jax.ShapeDtypeStruct((full, width), F32),
            jax.ShapeDtypeStruct((8, full), F32),
            part, part, part, part,
            jax.ShapeDtypeStruct((8, full), F32),
        ],
        in_specs=[SMEM, VMEM, VMEM] + [ANY] * 4 + [VMEM] * 4,
        out_specs=[ANY, VMEM, VMEM, VMEM] + [ANY] * 4 + [VMEM],
        scratch_shapes=[
            pltpu.VMEM((frames, full), F32),
            pltpu.VMEM((frames, full), F32),
            pltpu.VMEM(p_mine.shape, BF),
            pltpu.VMEM(p_mine.shape, BF),
            pltpu.VMEM((frames, full), BF),
            pltpu.VMEM((frames, full), F32),
            pltpu.VMEM((frames, full), F32),
            pltpu.VMEM((frames, full), F32),
            pltpu.VMEM((frames, full), BF),
            pltpu.VMEM((frames, full), BF),
            pltpu.SemaphoreType.DMA((2 * tiles + 2,)),
            pltpu.SemaphoreType.DMA((5 * tiles,)),
        ],
        compiler_params=pltpu.CompilerParams(vmem_limit_bytes=VMEM_LIMIT),
        cost_estimate=pl.CostEstimate(
            flops=4 * frames * full * full, bytes_accessed=12 << 20, transcendentals=0
        ),
        name="code_space",
    )(meta, alpha_last, alpha_mid, running, mid, p_mine, p_other, down, down.T, chosen, grad_code)


HIGHEST = lax.Precision.HIGHEST


def normalize(values, reduce_axis):
    return values * lax.rsqrt(jnp.sum(values * values, axis=reduce_axis, keepdims=True) + 1.0)


def chip_orders(count):
    bits = count.bit_length() - 1
    side = bits // 3
    axes = [list(range(side)), list(range(side, 2 * side)), list(range(2 * side, bits))]
    orders = []
    for turn in range(3):
        turned = axes[turn:] + axes[:turn]
        order = []
        for level in range(bits):
            order += [axis[level] for axis in turned if level < len(axis)]
        orders.append(tuple(order))
    return orders


def exchange(values, count, bits):
    pairs = []
    for chip in range(count):
        for core in range(2):
            pairs.append((2 * chip + core, 2 * (chip ^ (1 << bits[core])) + core))
    return lax.ppermute(values, ("dp", "chan"), pairs)


def side_of(bits):
    bit = jnp.where(lax.axis_index("chan") == 0, bits[0], bits[1])
    return lax.shift_right_logical(lax.axis_index("dp"), bit) & 1


def sum_over_chips(part, count, orders, last):
    steps = list(zip(*orders))
    for bits in steps:
        side = side_of(bits)
        rows = part.shape[0] // 2
        sent = lax.dynamic_slice_in_dim(part, (1 - side) * rows, rows, 0)
        kept = lax.dynamic_slice_in_dim(part, side * rows, rows, 0)
        part = (kept.astype(F32) + exchange(sent, count, bits).astype(F32)).astype(BF)
    for bits in reversed(steps):
        side = side_of(bits)
        got = exchange(part, count, bits)
        part = jnp.concatenate(
            [jnp.where(side == 0, part, got), jnp.where(side == 0, got, part)], axis=0
        )
    return part


def sum_chunk(chunk, count):
    orders = chip_orders(count)
    units = chunk.shape[0] // 256
    cut = (units - (3 * units) // 10) * 256
    one = sum_over_chips(chunk[:cut], count, (orders[0], orders[1]), None)
    two = sum_over_chips(chunk[cut:], count, (orders[2], orders[2]), None)
    return jnp.concatenate([one, two], axis=0)


def sum_small(values, count):
    for bit in range(count.bit_length() - 1):
        values = values + exchange(values, count, (bit, bit))
    return values


def swap(values):
    return lax.ppermute(values, "chan", [(0, 1), (1, 0)])


def shards(
    frames_in,
    utter_lengths,
    code_ids,
    alpha_first,
    alpha_second,
    alpha_last,
    w_dilated,
    w_point,
    w_down,
    w_latent,
    w_expand,
    codebook,
    out_grad,
):
    count = lax.axis_size("dp")
    core = lax.axis_index("chan")
    half = frames_in.shape[3]
    full = 2 * half
    utts = utter_lengths.shape[2]
    latent_width = codebook.shape[0]
    codes = codebook.shape[1]
    width = KS * latent_width

    def join(mine, other, axis):
        return jnp.where(
            core == 0,
            jnp.concatenate([mine, other], axis=axis),
            jnp.concatenate([other, mine], axis=axis),
        )

    def own_half(values, axis):
        size = values.shape[axis] // 2
        return lax.dynamic_slice_in_dim(values, core * size, size, axis)

    def other_half(values, axis):
        size = values.shape[axis] // 2
        return lax.dynamic_slice_in_dim(values, (1 - core) * size, size, axis)

    def mine_of(values):
        return lax.dynamic_index_in_dim(values, core, 0, keepdims=False)

    def other_of(values):
        return lax.dynamic_index_in_dim(values, 1 - core, 0, keepdims=False)

    frames_mine = mine_of(frames_in)[0]
    frames_other = swap(other_of(frames_in)[0])
    alpha_rows = jnp.concatenate([alpha_first, alpha_second, alpha_last[None]], axis=0)
    alphas = join(alpha_rows, swap(alpha_rows), 1)
    w_mine = [w_dilated[u].reshape(K * full, half) for u in range(3)]
    p_mine = [w_point[u] for u in range(3)]
    w_other = [swap(values) for values in w_mine]
    p_other = [swap(values) for values in p_mine]
    ends = jnp.cumsum(utter_lengths[:, 0], axis=1) * STRIDE
    meta = jnp.concatenate([mine_of(ends), other_of(ends), core[None]]).astype(jnp.int32)

    down_code = jnp.einsum("kco,ol->ckl", w_down, w_latent, preferred_element_type=F32)
    down_code = down_code.reshape(full, width)
    down_code = down_code + swap(down_code)

    ids = mine_of(code_ids)[0]
    selector = (ids[:, None] == jnp.arange(codes, dtype=jnp.int32)[None, :]).astype(F32)
    code_unit, code_back = jax.vjp(lambda values: normalize(values, 0), codebook)
    chosen = lax.dot_general(
        selector, code_unit, (((1,), (1,)), ((), ())), precision=HIGHEST, preferred_element_type=F32
    )
    grad_parts = jnp.stack([dot_cols(out_grad[m, 0], w_expand) for m in range(2)])
    grad_mixed = mine_of(grad_parts) + swap(other_of(grad_parts))
    code_sum = lax.dot_general(
        grad_mixed, selector, (((0,), (0,)), ((), ())), precision=HIGHEST, preferred_element_type=F32
    )

    kept = []
    inputs = (frames_mine, frames_other)
    for u in range(3):
        results = run_forward(
            u, meta, alphas[u][None], alphas[3 + u][None], inputs,
            w_mine[u], w_other[u], p_mine[u], p_other[u], utts,
        )
        if u == 0:
            running, *results = results
        opened_t, dilated, closed_t, after = results
        kept.append((running, opened_t, swap(opened_t), dilated, closed_t, swap(closed_t)))
        running = after
        inputs = (running,)

    (
        grad_running, mixed, down_sum, rate_last, gp_mine, gp_other, gd_mine, gd_other, rate,
    ) = run_code(
        meta, alphas[6][None], alphas[5][None], running, kept[2][3], p_mine[2], p_other[2],
        down_code, jnp.tile(chosen, (1, KS)), jnp.tile(grad_mixed, (1, KS)), utts,
    )
    rates = [None] * 7
    rates[6] = rate_last
    chunks = [None] * 3
    for u in (2, 1, 0):
        running, opened_t, opened_t_other, dilated, closed_t, closed_t_other = kept[u]
        if u < 2:
            gp_mine, gp_other, gd_mine, gd_other, rate = run_closing(
                meta, alphas[3 + u][None], grad_running, dilated, p_mine[u], p_other[u], utts
            )
        rates[3 + u] = rate
        chunk = run_weight(
            u, meta, opened_t, opened_t_other, closed_t, closed_t_other,
            gd_mine, swap(gd_other), gp_mine, swap(gp_other), utts,
        )
        if u == 2:
            down_half = own_half(down_sum, 0) + swap(other_half(down_sum, 0))
            code_half = own_half(code_sum, 1) + swap(other_half(code_sum, 1))
            chunk = jnp.concatenate(
                [chunk, down_half.astype(BF).reshape(-1, half), code_half.astype(BF).reshape(-1, half)],
                axis=0,
            )
        chunks[u] = sum_chunk(chunk, count)
        grad_running, rate = run_opening(
            u, meta, alphas[u][None], gd_mine, gd_other, running, grad_running,
            w_mine[u], w_other[u], utts,
        )
        rates[u] = rate

    mixed = mixed[:, :latent_width]
    mixed_other = swap(mixed)
    mixed_both = jnp.where(
        core == 0, jnp.stack([mixed, mixed_other]), jnp.stack([mixed_other, mixed])
    )
    block_out = jnp.einsum(
        "mjl,lo->mjo", mixed_both, w_expand, preferred_element_type=F32
    ).astype(BF)[:, None]
    expand_sum = jnp.einsum(
        "mjl,mjo->lo", mixed_both, out_grad[:, 0], preferred_element_type=F32
    )
    rates = jnp.sum(jnp.stack(rates), axis=1)
    rates = own_half(rates, 1) + swap(other_half(rates, 1))
    small = sum_small(jnp.concatenate([rates, expand_sum.reshape(-1, half)], axis=0), count)
    conv_rows = K * full
    w_rows = conv_rows + full
    down_rows = half * width // half
    down_half = chunks[2][w_rows : w_rows + down_rows].reshape(half, width)
    code_half = chunks[2][w_rows + down_rows :].reshape(latent_width, codes // 2)
    down_total = join(down_half, swap(down_half), 0).astype(F32)
    code_total = join(code_half, swap(code_half), 1).astype(F32)
    down_taps = jnp.transpose(down_total.reshape(full, KS, latent_width), (1, 0, 2))
    grad_w_down = jnp.einsum(
        "kcl,ol->kco", down_taps.astype(BF), w_latent, preferred_element_type=F32
    )
    grad_w_latent = jnp.einsum(
        "kco,kcl->ol", w_down, down_taps.astype(BF), preferred_element_type=F32
    )
    grad_codebook = code_back(code_total)[0]

    got = swap(other_half(grad_running, 1))
    own = own_half(grad_running, 1)
    grad_frames = jnp.where(core == 0, jnp.stack([own, got]), jnp.stack([got, own]))[:, None]
    return (
        block_out,
        grad_frames,
        small[0:3],
        small[3:6],
        small[6],
        jnp.stack([chunks[u][:conv_rows] for u in range(3)])
        .astype(F32)
        .reshape(3, K, full, half),
        jnp.stack([chunks[u][conv_rows:w_rows] for u in range(3)]).astype(F32),
        grad_w_down,
        grad_w_latent,
        small[7:].reshape(latent_width, -1),
        grad_codebook,
    )


def solution(mesh):
    placed = (
        P(None, "dp", None, "chan"),
        P(None, "dp", None),
        P(None, "dp", None),
        P(None, "chan"),
        P(None, "chan"),
        P("chan"),
        P(None, None, None, "chan"),
        P(None, None, "chan"),
        P(None, None, "chan"),
        P("chan", None),
        P(None, "chan"),
        P(),
        P(None, "dp", None, "chan"),
    )
    return jax.shard_map(
        shards,
        mesh=mesh,
        in_specs=placed,
        out_specs=(
            P(None, "dp", None, "chan"),
            P(None, "dp", None, "chan"),
            P(None, "chan"),
            P(None, "chan"),
            P("chan"),
            P(None, None, None, "chan"),
            P(None, None, "chan"),
            P(None, None, "chan"),
            P("chan", None),
            P(None, "chan"),
            P(),
        ),
        check_vma=False,
    )
```

```python
import functools
import types
import jax
import jax.numpy as jnp
from jax import lax
from jax.experimental import pallas as pl
from jax.experimental.pallas import tpu as pltpu
from jax.sharding import PartitionSpec as P

DP = "dp"
CHAN = "chan"
K = 7
STRIDE = 8
KS = 16
DILATIONS = (1, 3, 9)
BF = jnp.bfloat16
F32 = jnp.float32
HALO = 32
TILE = 256
LANES = 128
SINE = (3.141592580569316, -5.1677069002071025, 2.550031640919103, -0.5980464504720939, 0.0772222489218058)
COSINE = (0.9999999534666402, -4.934792858671753, 4.058411914096722, -1.3318801607983635, 0.2196967977026182)
VMEM_LIMIT = 60 * 1024 * 1024
SMALL_LIMIT = 16 * 1024 * 1024
COST = dict(
    prepare=9, forward=36, code_grads=3, weight_grads=10, opening=15, finish=5,
    down_grads=11, collect=3, place_rows=3, codebook_grads=3,
    sum_step=1, hold=1,
)
ANY = pl.BlockSpec(memory_space=pl.ANY)
SMEM = pl.BlockSpec(memory_space=pltpu.SMEM)
VMEM = pl.BlockSpec(memory_space=pltpu.VMEM)
DMA = pltpu.SemaphoreType.DMA


def shape(dims, kind):
    return jax.ShapeDtypeStruct(dims, kind)


class Order:
    def __init__(self):
        self.token = None
        self.before = []


def call(order, kernel, name, ins, outs, scratch, aliases=None, limit=VMEM_LIMIT):
    deps = ([] if order.token is None else [order.token]) + order.before
    order.before = []

    def body(*refs):
        refs = list(refs)
        named = dict(zip(ins, refs))
        refs = refs[len(ins) + len(deps) :]
        named.update(zip(outs, refs))
        refs[len(outs)][0] = jnp.int32(0)
        named.update(zip(scratch, refs[len(outs) + 1 :]))
        kernel(types.SimpleNamespace(**named))

    made = pl.pallas_call(
        body,
        out_shape=[out for _, out in outs.values()] + [shape((1,), jnp.int32)],
        in_specs=[spec for spec, _ in ins.values()] + [ANY] * len(deps),
        out_specs=[spec for spec, _ in outs.values()] + [SMEM],
        scratch_shapes=list(scratch.values()),
        input_output_aliases=aliases or {},
        compiler_params=pltpu.CompilerParams(vmem_limit_bytes=limit),
        cost_estimate=pl.CostEstimate(
            flops=COST[name] << 30, bytes_accessed=COST[name] * 3500000, transcendentals=0
        ),
        name=name,
    )(*[array for _, array in ins.values()], *deps)
    order.token = made[-1]
    return dict(zip(outs, made))


class Copies:
    def __init__(self, sem):
        self.sem = sem
        self.made = []
        self.done = set()

    def start(self, source, target):
        copy = pltpu.make_async_copy(source, target, self.sem.at[len(self.made)])
        copy.start()
        self.made.append(copy)
        return len(self.made) - 1

    def wait(self, *numbers):
        for number in numbers:
            if number not in self.done:
                self.done.add(number)
                self.made[number].wait()

    def wait_all(self):
        self.wait(*range(len(self.made)))


def dot(left, right):
    return jnp.dot(left, right, preferred_element_type=F32)


def dot_cols(left, right):
    return lax.dot_general(left, right, (((1,), (1,)), ((), ())), preferred_element_type=F32)


def poly(u, terms):
    total = terms[-1]
    for term in terms[-2::-1]:
        total = total * u + term
    return total


def half_turns(v, alpha):
    turns = v * (alpha * 0.3183098861837907)
    return turns - jnp.round(turns)


def snake(v, alpha):
    t = half_turns(v, alpha)
    u = t * t
    p = poly(u, SINE)
    return v + (u * (p * p)) * (1.0 / alpha)


def snake_slopes(v, alpha):
    t = half_turns(v, alpha)
    u = t * t
    sine = t * poly(u, SINE)
    double = 2.0 * sine * poly(u, COSINE)
    return sine * sine, double


def ends_of(lengths, row):
    ends = []
    total = 0
    for utt in range(lengths.shape[2]):
        total = total + lengths[row, 0, utt] * STRIDE
        ends.append(total)
    return ends


def put_labels(label_ref, ends, frames):
    t = lax.broadcasted_iota(jnp.int32, label_ref.shape, 0) - HALO
    label = jnp.zeros(label_ref.shape, jnp.int32)
    for end in ends:
        label = label + (t >= end).astype(jnp.int32)
    label_ref[...] = jnp.where((t < 0) | (t >= frames), -1, label)


def put_edges(padded_ref, frames):
    edge = jnp.zeros((HALO, padded_ref.shape[1]), F32)
    padded_ref[:HALO, :] = edge
    padded_ref[HALO + frames :, :] = edge


def tap(padded_ref, label_ref, row, rows, offset):
    here = HALO + row
    width = padded_ref.shape[1]
    same = label_ref[here + offset : here + offset + rows, :] == label_ref[here : here + rows, :]
    pieces = []
    for lane in range(0, width, LANES):
        piece = padded_ref[here + offset : here + offset + rows, lane : lane + LANES]
        pieces.append(jnp.where(same, piece, 0.0).astype(BF))
    return jnp.concatenate(pieces, axis=1)


def column_half(core, half):
    return pl.ds(pl.multiple_of(core * half, half), half)


def both_columns(half):
    core = lax.axis_index(CHAN)
    return column_half(core, half), column_half(1 - core, half)


def put_row(target, mine, other, index, own, oth):
    half = mine.shape[1]
    target[:, own] = jnp.broadcast_to(mine[index : index + 1, :], (8, half))
    target[:, oth] = jnp.broadcast_to(other[index : index + 1, :], (8, half))
    return target[0:1, :]


def split(values, terms):
    parts = []
    for _ in range(terms):
        part = values.astype(BF)
        parts.append(part)
        values = values - part.astype(F32)
    return parts


def row_sums(values):
    return jnp.sum(values.reshape(values.shape[0] // 8, 8, values.shape[1]), axis=0)


def tiles_of(frames):
    return [(slice(start, start + TILE), pl.ds(start, TILE)) for start in range(0, frames, TILE)]


def forward_kernel(r):
    frames, full = r.run_v.shape[1:]
    half = full // 2
    core = lax.axis_index(CHAN)
    own, oth = both_columns(half)
    copies = Copies(r.sem)
    tiles = tiles_of(frames)
    place = [
        copies.start(r.lengths, r.lengths_v),
        copies.start(r.alpha_mine, r.alpha_mv),
        copies.start(r.alpha_other, r.alpha_ov),
    ]
    loads = [copies.start(r.frames_in.at[core, 0], r.mine_v), copies.start(r.frames_got.at[core, 0], r.other_v)]

    def load_weights(unit):
        return [
            copies.start(r.w_mine.at[unit], r.w_v.at[unit % 2, 0]),
            copies.start(r.w_other.at[unit], r.w_v.at[unit % 2, 1]),
        ]

    weights = [load_weights(0)]
    points = [copies.start(r.p_mine, r.pm_v), copies.start(r.p_other, r.po_v)]
    weights.append(load_weights(1))
    small = [
        copies.start(source, target)
        for source, target in (
            (r.down_mine, r.dm_v), (r.down_other, r.do_v), (r.chosen, r.chosen_v),
            (r.back_mine, r.bm_v), (r.back_other, r.bo_v),
        )
    ]
    put_edges(r.padded, frames)
    copies.wait(*place)
    put_labels(r.label, ends_of(r.lengths_v, core), frames)
    copies.wait(*loads)
    leaving = {(kind, slot): [] for kind in ("run", "mid", "seen") for slot in range(2)}

    def settle(kind, slot):
        copies.wait(*leaving[kind, slot])
        leaving[kind, slot] = []

    for unit in range(3):
        now, later = r.run_v.at[unit % 2], r.run_v.at[(unit + 1) % 2]
        mid = r.mid_v.at[unit % 2]
        seen = r.seen_v.at[unit % 2]
        rate_in = put_row(r.rate_v.at[unit], r.alpha_mv, r.alpha_ov, unit, own, oth)
        rate_mid = put_row(r.rate_v.at[3 + unit], r.alpha_mv, r.alpha_ov, 3 + unit, own, oth)
        settle("seen", unit % 2)
        for rows, there in tiles:
            if unit == 0:
                now[rows, own] = r.mine_v[rows, :].astype(F32)
                now[rows, oth] = r.other_v[rows, :].astype(F32)
                leaving["run", 0].append(copies.start(now.at[there], r.running.at[unit, there]))
            opened = snake(now[rows, :], rate_in)
            r.padded[HALO + rows.start : HALO + rows.stop, :] = opened
            seen[:full, rows] = opened.T.astype(BF)
        seen_out = getattr(r, f"seen{unit}")
        leaving["seen", unit % 2].append(
            copies.start(seen.at[pl.ds(0, full)], seen_out.at[pl.ds(0, full)])
        )
        copies.wait(*weights[unit])
        if unit == 0:
            copies.wait(*points)
        settle("mid", unit % 2)
        settle("run", (unit + 1) % 2)
        for place_of, (rows, there) in enumerate(tiles):
            taps = r.taps.at[place_of % 2]
            for index in range(K):
                offset = DILATIONS[unit] * (index - K // 2)
                taps[:, index * full : (index + 1) * full] = tap(
                    r.padded, r.label, rows.start, TILE, offset
                )
            mid[rows, own] = dot(taps[...], r.w_v[unit % 2, 0])
            mid[rows, oth] = dot(taps[...], r.w_v[unit % 2, 1])
            if unit < 2:
                leaving["mid", unit % 2].append(copies.start(mid.at[there], r.dilated.at[unit, there]))
            closed = snake(mid[rows, :], rate_mid)
            seen[full:, rows] = closed.T.astype(BF)
            closed = closed.astype(BF)
            later[rows, own] = now[rows, own] + dot(closed, r.pm_v[unit])
            later[rows, oth] = now[rows, oth] + dot(closed, r.po_v[unit])
            if unit < 2:
                leaving["run", (unit + 1) % 2].append(
                    copies.start(later.at[there], r.running.at[unit + 1, there])
                )
        leaving["seen", unit % 2].append(
            copies.start(seen.at[pl.ds(full, full)], seen_out.at[pl.ds(full, full)])
        )
        if unit == 0:
            weights.append(load_weights(2))

    running, mid = r.run_v.at[1], r.mid_v.at[0]
    blocks = frames // STRIDE
    value = put_row(r.rate_v.at[6], r.alpha_mv, r.alpha_ov, 6, own, oth)
    mid_value = r.rate_v[5, 0:1, :]
    inverse = 1.0 / value
    copies.wait(*small)
    width = r.dm_v.shape[1]
    code = width // KS
    lane = lax.broadcasted_iota(jnp.int32, (TILE, width), 1) // code
    step = lax.broadcasted_iota(jnp.int32, (TILE, width), 0) % STRIDE
    pattern = (lane % STRIDE == (step + STRIDE // 2) % STRIDE).astype(F32)
    down = r.dm_v[...] + r.do_v[...]
    down_parts = jnp.concatenate(split(down, 3), axis=1)
    sums = []
    for rows, _ in tiles:
        v = running[rows, :]
        square, double = snake_slopes(v, value)
        r.square_v[rows, :] = square
        r.double_v[rows, :] = double
        opened = (v + square * inverse).astype(BF)
        r.opened_v[rows, :] = opened
        products = dot(opened, down_parts)
        products = products[:, :width] + products[:, width : 2 * width] + products[:, 2 * width :]
        products = (products * pattern).reshape(TILE // STRIDE, STRIDE, width)
        sums.append(jnp.sum(products, axis=1))
    sums = jnp.concatenate(sums, axis=0)
    block = lax.broadcasted_iota(jnp.int32, (blocks, width), 0)
    block_lane = lax.broadcasted_iota(jnp.int32, (blocks, width), 1)
    label = jnp.zeros((blocks, width), jnp.int32)
    for end in ends_of(r.lengths_v, core):
        label = label + (block * STRIDE >= end).astype(jnp.int32)

    def earlier(values):
        return pltpu.roll(values, 1, 0)

    def later_rows(values):
        return pltpu.roll(values, blocks - 1, 0)

    same_before = jnp.where((block > 0) & (earlier(label) == label), 1.0, 0.0)
    same_after = jnp.where((block < blocks - 1) & (later_rows(label) == label), 1.0, 0.0)
    early = block_lane < 4 * code
    late = block_lane >= 12 * code
    sums = jnp.where(
        early, same_before * earlier(sums), jnp.where(late, same_after * later_rows(sums), sums)
    )
    fold = (
        lax.broadcasted_iota(jnp.int32, (width, width), 0) % code
        == lax.broadcasted_iota(jnp.int32, (width, width), 1) % code
    ).astype(BF)
    latent = dot(jnp.concatenate(split(sums, 3), axis=1), jnp.concatenate([fold] * 3, axis=0))
    scale = lax.rsqrt(jnp.sum(latent * latent, axis=1, keepdims=True) * (1.0 / KS) + 1.0)
    unit_code = latent * scale
    r.mixed[...] = (unit_code + r.chosen_v[...]).astype(BF)
    back = r.bm_v[...] + r.bo_v[...]
    along = jnp.sum(unit_code * back, axis=1, keepdims=True) * (1.0 / KS)
    spread = (back - unit_code * along) * scale
    spread = jnp.where(
        early,
        later_rows(same_before * spread),
        jnp.where(late, earlier(same_after * spread), spread),
    )
    down_t_parts = split(down.T, 2)
    down_t_stack = jnp.concatenate([down_t_parts[0], down_t_parts[1], down_t_parts[0]], axis=0)
    total = jnp.zeros((8, full), F32)
    last_total = jnp.zeros((8, full), F32)
    down_total = jnp.zeros(down.shape, F32)
    for rows, there in tiles:
        own_blocks = spread[rows.start // STRIDE : rows.stop // STRIDE, :]
        wide = jnp.broadcast_to(
            own_blocks[:, None, :], (TILE // STRIDE, STRIDE, width)
        ).reshape(TILE, width) * pattern
        parts = split(wide, 3)
        sums = lax.dot_general(
            r.opened_v[rows, :],
            jnp.concatenate(parts, axis=1),
            (((0,), (0,)), ((), ())),
            preferred_element_type=F32,
        )
        down_total = down_total + (sums[:, :width] + sums[:, width : 2 * width] + sums[:, 2 * width :])
        grad_last = dot(jnp.concatenate([parts[0], parts[0], parts[1]], axis=1), down_t_stack)
        square = r.square_v[rows, :]
        double = r.double_v[rows, :]
        grad = grad_last * (1.0 + double)
        r.grad_v[rows, :] = grad
        copies.start(r.grad_v.at[there], r.grad.at[there])
        rate = grad_last * (running[rows, :] * double - square * inverse)
        last_total = last_total + row_sums(rate)
        total = total + closing_steps(
            r, rows, grad, mid[rows, :], mid_value, (own, oth), r.pm_v[2], r.po_v[2]
        )
        send_closing(r, copies, rows, there, own, oth)
    r.rates[...] = total * (1.0 / mid_value)
    r.last_rates[...] = last_total * inverse
    r.down_sum[:, :width] = down_total[:half, :].astype(BF)
    r.down_sum[:, width:] = down_total[half:, :].astype(BF)
    copies.wait_all()


def closing_steps(r, rows, point, mid, alpha, core_cols, p_mine, p_other):
    own, oth = core_cols
    r.gp_v[rows, :] = point.astype(BF)
    grad = dot_cols(r.gp_v[rows, own], p_mine) + dot_cols(r.gp_v[rows, oth], p_other)
    square, double = snake_slopes(mid, alpha)
    r.gd_v[rows, :] = (grad * (1.0 + double)).astype(BF)
    return row_sums(grad * (mid * double - square * (1.0 / alpha)))


def send_closing(r, copies, rows, there, own, oth):
    frames = r.gp_v.shape[0]
    after = pl.ds(frames + rows.start, TILE)
    copies.start(r.gp_v.at[there, own], r.mine.at[there])
    copies.start(r.gd_v.at[there, own], r.mine.at[after])
    copies.start(r.gp_v.at[there, oth], r.other.at[there])
    copies.start(r.gd_v.at[there, oth], r.other.at[after])


def place_ins(place):
    return {name: (ANY, array) for name, array in zip(("lengths", "alpha_mine", "alpha_other"), place)}


def place_rooms(place, full):
    lengths, alpha, _ = place
    return dict(
        lengths_v=pltpu.SMEM(lengths.shape, jnp.int32),
        alpha_mv=pltpu.VMEM(alpha.shape, F32),
        alpha_ov=pltpu.VMEM(alpha.shape, F32),
        rate_v=pltpu.VMEM((7, 8, full), F32),
    )


def any_ins(**arrays):
    return {name: (ANY, array) for name, array in arrays.items()}


def vmem_ins(**arrays):
    return {name: (VMEM, array) for name, array in arrays.items()}


def run_forward(order, place, frames_in, frames_got, w_mine, w_other, p_mine, p_other, small):
    frames, half = frames_in.shape[2:]
    full = 2 * half
    tiles = frames // TILE
    blocks = frames // STRIDE
    width = small["down_mine"].shape[1]
    wide = (frames, full)
    pair = (ANY, shape((2 * frames, half), BF))
    square = pltpu.VMEM((blocks, width), F32)
    tall = pltpu.VMEM((full, width), F32)
    return call(
        order,
        forward_kernel,
        "forward",
        dict(
            **place_ins(place),
            **any_ins(frames_in=frames_in, frames_got=frames_got, w_mine=w_mine, w_other=w_other,
                      p_mine=p_mine, p_other=p_other, **small),
        ),
        dict(
            running=(ANY, shape((3,) + wide, F32)),
            dilated=(ANY, shape((2,) + wide, F32)),
            seen0=(ANY, shape((2 * full, frames), BF)),
            seen1=(ANY, shape((2 * full, frames), BF)),
            seen2=(ANY, shape((2 * full, frames), BF)),
            grad=(ANY, shape(wide, F32)),
            mixed=(VMEM, shape((blocks, width), BF)),
            down_sum=(VMEM, shape((half, 2 * width), BF)),
            last_rates=(VMEM, shape((8, full), F32)),
            mine=pair,
            other=pair,
            rates=(VMEM, shape((8, full), F32)),
        ),
        dict(
            **place_rooms(place, full),
            mine_v=pltpu.VMEM((frames, half), BF),
            other_v=pltpu.VMEM((frames, half), BF),
            run_v=pltpu.VMEM((2,) + wide, F32),
            mid_v=pltpu.VMEM((2,) + wide, F32),
            seen_v=pltpu.VMEM((2, 2 * full, frames), BF),
            padded=pltpu.VMEM((frames + 2 * HALO, full), F32),
            label=pltpu.VMEM((frames + 2 * HALO, LANES), jnp.int32),
            taps=pltpu.VMEM((2, TILE, K * full), BF),
            w_v=pltpu.VMEM((2, 2) + w_mine.shape[1:], BF),
            pm_v=pltpu.VMEM(p_mine.shape, BF),
            po_v=pltpu.VMEM(p_mine.shape, BF),
            dm_v=tall, do_v=tall, chosen_v=square, bm_v=square, bo_v=square,
            opened_v=pltpu.VMEM(wide, BF),
            square_v=pltpu.VMEM(wide, F32),
            double_v=pltpu.VMEM(wide, F32),
            grad_v=pltpu.VMEM(wide, F32),
            gp_v=pltpu.VMEM(wide, BF),
            gd_v=pltpu.VMEM(wide, BF),
            sem=DMA((3 + 2 + 6 + 2 + 5 + 5 * tiles + 6 + 5 * tiles,)),
        ),
    )


def weight_kernel(unit, pieces, r):
    frames = r.padded.shape[1] - 2 * HALO
    half = r.padded.shape[2]
    full = 2 * half
    core = lax.axis_index(CHAN)
    copies = Copies(r.sem)
    place = copies.start(r.lengths, r.lengths_v)
    grads = []
    for row, source in enumerate((r.grads_mine, r.grads_got)):
        grads.append(copies.start(source.at[pl.ds(frames, frames)], r.gd_v.at[row]))
    opened = []
    for row, source in enumerate((r.seen_mine, r.seen_got)):
        columns = pl.ds(row * frames, frames)
        opened.append(copies.start(source.at[pl.ds(0, full)], r.seen_v.at[pl.ds(0, full), columns]))
    points = []
    for row, (source, seen) in enumerate(((r.grads_mine, r.seen_mine), (r.grads_got, r.seen_got))):
        columns = pl.ds(row * frames, frames)
        points.append(copies.start(source.at[pl.ds(0, frames)], r.gp_v.at[columns]))
        points.append(copies.start(seen.at[pl.ds(full, full)], r.seen_v.at[pl.ds(full, full), columns]))
    if hasattr(r, "value"):
        beside = [copies.start(r.value, r.value_v), copies.start(r.came, r.came_v)]
    for row in range(2):
        put_edges(r.padded.at[row], frames)
    copies.wait(place)
    for row in range(2):
        put_labels(r.label.at[row], ends_of(r.lengths_v, core if row == 0 else 1 - core), frames)
    for row in range(2):
        copies.wait(grads[row])
        r.padded[row, HALO : HALO + frames, :] = r.gd_v[row].astype(F32)
    copies.wait(*opened)
    for index in range(K):
        offset = -DILATIONS[unit] * (index - K // 2)
        taps = r.taps.at[index % 2]
        for row in range(2):
            for start in range(0, frames, TILE):
                taps[row * frames + start : row * frames + start + TILE, :] = tap(
                    r.padded.at[row], r.label.at[row], start, TILE, offset
                )
        r.out_v[index * full : (index + 1) * full, :] = dot(r.seen_v[:full, :], taps[...]).astype(BF)
    if hasattr(r, "value"):
        copies.wait(*beside)
        total = r.value_v[...].astype(F32) + r.came_v[...].astype(F32)
        r.value_v[...] = total.astype(BF)
        copies.start(r.value_v, r.total)
    copies.wait(*points)
    r.out_v[K * full : (K + 1) * full, :] = dot(r.seen_v[full:, :], r.gp_v[...]).astype(BF)
    for piece in pieces:
        side = kept_side(piece.bits)
        there = pl.ds(0, piece.rows)
        for kind, which in (("sent", 1 - side), ("kept", side)):
            here = pl.ds(pl.multiple_of(piece.start + which * piece.rows, 16), piece.rows)
            copies.start(r.out_v.at[here], getattr(r, kind + piece.name).at[there])
    copies.wait_all()


def kept_side(bits):
    bit = jnp.where(lax.axis_index(CHAN) == 0, bits[0], bits[1])
    return lax.shift_right_logical(lax.axis_index(DP), bit) & 1


class Piece:
    def __init__(self, name, start, rows, place, bits):
        self.name, self.start, self.rows, self.place, self.bits = name, start, rows, place, bits


def run_weight(order, unit, place, seen_mine, seen_got, grads_mine, grads_got, pieces, beside=None):
    frames, half = grads_mine.shape[0] // 2, grads_mine.shape[1]
    full = 2 * half
    ins = any_ins(lengths=place[0], seen_mine=seen_mine, seen_got=seen_got,
                  grads_mine=grads_mine, grads_got=grads_got)
    scratch = dict(
        lengths_v=pltpu.SMEM(place[0].shape, jnp.int32),
        seen_v=pltpu.VMEM((2 * full, 2 * frames), BF),
        gd_v=pltpu.VMEM((2, frames, half), BF),
        gp_v=pltpu.VMEM((2 * frames, half), BF),
        padded=pltpu.VMEM((2, frames + 2 * HALO, half), F32),
        label=pltpu.VMEM((2, frames + 2 * HALO, LANES), jnp.int32),
        taps=pltpu.VMEM((2, 2 * frames, half), BF),
        out_v=pltpu.VMEM(((K + 1) * full, half), BF),
        sem=DMA((12 + 2 * len(pieces),)),
    )
    outs = {
        kind + piece.name: (ANY, shape((piece.rows, half), BF))
        for piece in pieces
        for kind in ("sent", "kept")
    }
    if beside is not None:
        value, came = beside
        ins.update(any_ins(value=value, came=came))
        outs["total"] = (ANY, shape(value.shape, BF))
        scratch.update(value_v=pltpu.VMEM(value.shape, BF), came_v=pltpu.VMEM(value.shape, BF))
    return call(
        order, functools.partial(weight_kernel, unit, pieces), "weight_grads", ins, outs, scratch
    )


def opening_kernel(unit, r):
    last = unit == 0
    frames, full = r.running_v.shape
    half = full // 2
    core = lax.axis_index(CHAN)
    own, oth = both_columns(half)
    copies = Copies(r.sem)
    tiles = tiles_of(frames)
    place = [
        copies.start(r.lengths, r.lengths_v),
        copies.start(r.alpha_mine, r.alpha_mv),
        copies.start(r.alpha_other, r.alpha_ov),
    ]
    after = pl.ds(frames, frames)
    grads = [
        copies.start(r.grads_mine.at[after], r.gm_v),
        copies.start(r.grads_other.at[after], r.go_v),
    ]
    weights = [
        copies.start(r.w_mine.at[unit], r.w_v.at[0]),
        copies.start(r.w_other.at[unit], r.w_v.at[1]),
    ]
    if not last:
        points = [
            copies.start(r.p_mine.at[unit - 1], r.pm_v),
            copies.start(r.p_other.at[unit - 1], r.po_v),
        ]
    loads = []
    for _, there in tiles:
        loads.append([
            copies.start(r.running.at[unit, there], r.running_v.at[there]),
            copies.start(r.grad_in.at[there], r.grad_v.at[there]),
        ])
        if not last:
            loads[-1].append(copies.start(r.dilated.at[unit - 1, there], r.mid_v.at[there]))
    for part in range(2):
        put_edges(r.padded.at[part], frames)
    copies.wait(*place)
    put_labels(r.label, ends_of(r.lengths_v, core), frames)
    value = put_row(r.rate_v.at[0], r.alpha_mv, r.alpha_ov, unit, own, oth)
    if not last:
        mid_value = put_row(r.rate_v.at[1], r.alpha_mv, r.alpha_ov, 2 + unit, own, oth)
    for part, values in ((0, r.gm_v), (1, r.go_v)):
        copies.wait(grads[part])
        r.padded[part, HALO : HALO + frames, :] = values[...].astype(F32)
    copies.wait(*weights)
    for part in range(2):
        for index in range(K):
            r.turned_v[(2 * index + part) * half : (2 * index + part + 1) * half, :] = r.w_v[
                part, index * full : (index + 1) * full, :
            ].T
    if not last:
        copies.wait(*points)
    total = jnp.zeros((8, full), F32)
    mid_total = jnp.zeros((8, full), F32)
    for place_of, (rows, there) in enumerate(tiles):
        taps = r.taps.at[place_of % 2]
        for index in range(K):
            offset = -DILATIONS[unit] * (index - K // 2)
            for part in range(2):
                start = (2 * index + part) * half
                taps[:, start : start + half] = tap(
                    r.padded.at[part], r.label, rows.start, TILE, offset
                )
        opened = dot(taps[...], r.turned_v[...])
        copies.wait(*loads[place_of])
        v = r.running_v[rows, :]
        square, double = snake_slopes(v, value)
        grad = r.grad_v[rows, :] + opened * (1.0 + double)
        r.grad_v[rows, :] = grad
        total = total + row_sums(opened * (v * double - square * (1.0 / value)))
        if last:
            copies.start(r.grad_v.at[there, own], r.frames_mine.at[core, 0, there])
            copies.start(r.grad_v.at[there, oth], r.frames_sent.at[there])
        else:
            copies.start(r.grad_v.at[there], r.grad.at[there])
            mid_total = mid_total + closing_steps(
                r, rows, grad, r.mid_v[rows, :], mid_value, (own, oth), r.pm_v[...], r.po_v[...]
            )
            send_closing(r, copies, rows, there, own, oth)
    r.rates[...] = total * (1.0 / value)
    if not last:
        r.mid_rates[...] = mid_total * (1.0 / mid_value)
    copies.wait_all()


def run_opening(order, unit, place, grads_mine, grads_other, running, grad, dilated, w_mine, w_other, p_mine, p_other):
    frames, full = grad.shape
    half = full // 2
    tiles = frames // TILE
    last = unit == 0
    wide = pltpu.VMEM((frames, full), F32)
    narrow = pltpu.VMEM((frames, full), BF)
    part = pltpu.VMEM((frames, half), BF)
    point = pltpu.VMEM(p_mine.shape[1:], BF)
    pair = (ANY, shape((2 * frames, half), BF))
    rates = (VMEM, shape((8, full), F32))
    ins = dict(
        **place_ins(place),
        **any_ins(grads_mine=grads_mine, grads_other=grads_other, running=running, grad_in=grad,
                  w_mine=w_mine, w_other=w_other),
    )
    outs = dict(rates=rates)
    scratch = dict(
        **place_rooms(place, full),
        gm_v=part, go_v=part,
        padded=pltpu.VMEM((2, frames + 2 * HALO, half), F32),
        label=pltpu.VMEM((frames + 2 * HALO, LANES), jnp.int32),
        running_v=wide, grad_v=wide,
        w_v=pltpu.VMEM((2,) + w_mine.shape[1:], BF),
        turned_v=pltpu.VMEM((K * full, full), BF),
        taps=pltpu.VMEM((2, TILE, K * full), BF),
    )
    if last:
        outs["frames_mine"] = (ANY, shape((2, 1, frames, half), F32))
        outs["frames_sent"] = (ANY, shape((frames, half), F32))
    else:
        ins.update(any_ins(dilated=dilated, p_mine=p_mine, p_other=p_other))
        outs.update(grad=(ANY, shape((frames, full), F32)), mine=pair, other=pair, mid_rates=rates)
        scratch.update(mid_v=wide, pm_v=point, po_v=point, gp_v=narrow, gd_v=narrow)
    scratch["sem"] = DMA((3 + 2 + 2 + 2 + 8 * tiles,))
    return call(
        order, functools.partial(opening_kernel, unit), "opening", ins, outs, scratch
    )


def prepare_kernel(r):
    taps, full, out_half = r.w_down.shape
    code, codes = r.codebook.shape
    blocks = r.ids.shape[2]
    width = taps * code
    core = lax.axis_index(CHAN)
    copies = Copies(r.sem)
    first = [copies.start(r.ids.at[core], r.ids_v), copies.start(r.codebook, r.book_v)]
    loads = [copies.start(r.w_down.at[index], r.down_v.at[index]) for index in range(taps)]
    copies.wait(*first)
    mark = r.ids_v[...]
    total = jnp.zeros((3 * code, blocks), F32)
    step = 1024
    for start in range(0, codes, step):
        columns = r.book_v[:, start : start + step]
        unit = columns * lax.rsqrt(jnp.sum(columns * columns, axis=0, keepdims=True) + 1.0)
        parts = jnp.concatenate([part.astype(F32) for part in split(unit, 3)], axis=0).astype(BF)
        number = lax.broadcasted_iota(jnp.int32, (step, blocks), 0) + start
        total = total + dot(parts, jnp.where(number == mark, 1.0, 0.0).astype(BF))
    picked = total[:code] + total[code : 2 * code] + total[2 * code :]
    r.chosen[...] = jnp.concatenate([picked] * taps, axis=0).T
    r.ids_t[...] = jnp.broadcast_to(mark.astype(F32), (blocks, blocks)).T
    expand = jnp.concatenate([r.w_expand[...].astype(F32)] * taps, axis=0).astype(BF)
    r.back_mine[...] = dot_cols(r.out_grad[core, 0], expand)
    r.back_sent[...] = dot_cols(r.out_grad[1 - core, 0], expand)
    fold = (
        lax.broadcasted_iota(jnp.int32, (code, width), 0)
        == lax.broadcasted_iota(jnp.int32, (code, width), 1) % code
    ).astype(BF)
    latent = dot(r.w_latent[...], fold)
    group = lax.broadcasted_iota(jnp.int32, (out_half, width), 1) // code
    product = jnp.zeros((full, width), F32)
    for index in range(taps):
        copies.wait(loads[index])
        product = product + dot(r.down_v[index], jnp.where(group == index, latent, 0.0).astype(BF))
    r.down_mine[...] = product


def run_prepare(order, w_down, w_latent, w_expand, out_grad, ids, codebook):
    taps, full, _ = w_down.shape
    width = taps * codebook.shape[0]
    blocks = ids.shape[2]
    square = (VMEM, shape((blocks, width), F32))
    return call(
        order,
        prepare_kernel,
        "prepare",
        dict(
            **any_ins(w_down=w_down, ids=ids, codebook=codebook),
            **vmem_ins(w_latent=w_latent, w_expand=w_expand, out_grad=out_grad),
        ),
        dict(
            down_mine=(VMEM, shape((full, width), F32)),
            chosen=square, back_mine=square, back_sent=square,
            ids_t=(VMEM, shape((blocks, blocks), F32)),
        ),
        dict(
            down_v=pltpu.VMEM(w_down.shape, BF),
            book_v=pltpu.VMEM(codebook.shape, F32),
            ids_v=pltpu.VMEM(ids.shape[1:], jnp.int32),
            sem=DMA((taps + 2,)),
        ),
    )


def code_grad_kernel(r):
    blocks, width = r.back_mine.shape
    rows, half = r.mine.shape
    code = width // KS
    core = lax.axis_index(CHAN)
    back = (r.back_mine[...] + r.back_other[...]).T[:code, :]
    parts = jnp.concatenate([part.astype(F32) for part in split(back, 3)], axis=0).astype(BF)
    for index in range(rows // code):
        pieces = []
        for lane in range(0, half, blocks):
            number = lax.broadcasted_iota(jnp.int32, (blocks, blocks), 1) + (index * half + lane)
            pieces.append(jnp.where(r.ids_t[...] == number.astype(F32), 1.0, 0.0).astype(BF))
        sums = dot(parts, jnp.concatenate(pieces, axis=1))
        r.stage[index * code : (index + 1) * code, :] = (
            sums[:code] + sums[code : 2 * code] + sums[2 * code :]
        )
    down = r.down_sum[...].astype(F32)
    codes = r.stage[...]
    r.mine[...] = jnp.where(core == 0, down, codes).astype(BF)
    r.other[...] = jnp.where(core == 0, codes, down).astype(BF)


def run_code_grad(order, ids_t, back_mine, back_other, down_sum, codes):
    half = down_sum.shape[1]
    rows = codes // half * (back_mine.shape[1] // KS)
    part = (VMEM, shape((rows, half), BF))
    made = call(
        order,
        code_grad_kernel,
        "code_grads",
        vmem_ins(ids_t=ids_t, back_mine=back_mine, back_other=back_other, down_sum=down_sum),
        dict(mine=part, other=part),
        dict(stage=pltpu.VMEM((rows, half), F32)),
    )
    return made["mine"], made["other"]


def down_kernel(r):
    taps, full, out_half = r.w_down.shape
    width = r.mine.shape[1] // 2
    code = width // taps
    copies = Copies(r.sem)
    loads = [copies.start(r.w_down.at[index], r.down_v.at[index]) for index in range(taps)]
    core = lax.axis_index(CHAN)
    total = jnp.where(core == 0, r.mine[...].astype(F32), r.got[...].astype(F32))
    sums = jnp.concatenate([total[:, :width], total[:, width:]], axis=0)
    rounded = sums.astype(BF)
    fold = (
        lax.broadcasted_iota(jnp.int32, (code, width), 0)
        == lax.broadcasted_iota(jnp.int32, (code, width), 1) % code
    ).astype(BF)
    latent = dot(r.w_latent[...], fold)
    group = lax.broadcasted_iota(jnp.int32, (out_half, width), 1) // code
    across = sums.T
    product = jnp.zeros((code, out_half), F32)
    outs = []
    for index in range(taps):
        slot = index % 4
        if index >= 4:
            copies.wait(outs[index - 4])
        spread = jnp.where(group == index, latent, 0.0).astype(BF)
        r.out_v[slot] = dot_cols(rounded, spread)
        outs.append(copies.start(r.out_v.at[slot], r.grad_down.at[index]))
        copies.wait(loads[index])
        product = product + dot(
            across[index * code : (index + 1) * code, :].astype(BF), r.down_v[index]
        )
    r.grad_latent[...] = product.T
    copies.wait_all()


def run_down(order, mine, got, w_latent, w_down):
    taps, full, out_half = w_down.shape
    made = call(
        order,
        down_kernel,
        "down_grads",
        dict(**vmem_ins(mine=mine, got=got, w_latent=w_latent), **any_ins(w_down=w_down)),
        dict(
            grad_down=(ANY, shape(w_down.shape, F32)),
            grad_latent=(VMEM, shape((out_half, w_latent.shape[1]), F32)),
        ),
        dict(
            down_v=pltpu.VMEM(w_down.shape, BF),
            out_v=pltpu.VMEM((4, full, out_half), F32),
            sem=DMA((2 * taps,)),
        ),
    )
    return made["grad_down"], made["grad_latent"]


def step_kernel(jobs, r):
    copies = Copies(r.sem) if hasattr(r, "sem") else None
    for job in jobs:
        job.load(r, copies)
    for job in jobs:
        job.run(r, copies)
    r.mark_next[...] = jnp.zeros(r.mark_next.shape, F32)
    if copies is not None:
        copies.wait_all()


class Scatter:
    def __init__(self, name, kept, got, bits, large=False, unit=1):
        self.name, self.bits, self.large = name, bits, large
        self.kept, self.got = kept, got
        self.spec = ANY if large else VMEM
        self.used = sum(array.shape[0] for array in kept)
        self.shape = (-(-self.used // unit) * unit, kept[0].shape[1])

    def ins(self):
        arrays = {f"kept{self.name}_{index}": array for index, array in enumerate(self.kept)}
        arrays.update({f"got{self.name}_{index}": array for index, array in enumerate(self.got)})
        return {name: (self.spec, array) for name, array in arrays.items()}

    def outs(self):
        part = (self.spec, shape((self.shape[0] // 2, self.shape[1]), BF))
        return {"sent" + self.name: part, "next" + self.name: part}

    def scratch(self):
        rooms = {"room" + self.name: pltpu.VMEM(self.shape, BF)}
        if self.large:
            rooms["other" + self.name] = pltpu.VMEM(self.shape, BF)
        return rooms

    def copies(self):
        return 2 * len(self.kept) + 2 if self.large else 0

    def spans(self):
        start = 0
        for index, array in enumerate(self.kept):
            yield index, slice(start, start + array.shape[0])
            start += array.shape[0]

    def load(self, r, copies):
        self.loads = []
        if self.large:
            for index, rows in self.spans():
                there = pl.ds(rows.start, rows.stop - rows.start)
                for kind, room in (("kept", "room"), ("got", "other")):
                    source = getattr(r, f"{kind}{self.name}_{index}")
                    self.loads.append(copies.start(source, getattr(r, room + self.name).at[there]))

    def add(self, r, room, copies):
        for index, rows in self.spans():
            if self.large:
                copies.wait(*self.loads[2 * index : 2 * index + 2])
                kept, got = room[rows, :], getattr(r, "other" + self.name)[rows, :]
            else:
                kept = getattr(r, f"kept{self.name}_{index}")[...]
                got = getattr(r, f"got{self.name}_{index}")[...]
            room[rows, :] = (kept.astype(F32) + got.astype(F32)).astype(BF)

    def run(self, r, copies):
        room = getattr(r, "room" + self.name)
        self.add(r, room, copies)
        if room.shape[0] > self.used:
            room[self.used :, :] = jnp.zeros((room.shape[0] - self.used, room.shape[1]), BF)
        rows = room.shape[0] // 2
        side = kept_side(self.bits)
        for kind, which in (("sent", 1 - side), ("next", side)):
            target = getattr(r, kind + self.name)
            here = pl.ds(pl.multiple_of(which * rows, 16), rows)
            if self.large:
                copies.start(room.at[here], target)
            else:
                target[...] = room[here, :]


class Reduce(Scatter):
    def outs(self):
        return {"sent" + self.name: (VMEM, shape(self.shape, BF))}

    def scratch(self):
        return {}

    def run(self, r, copies):
        self.add(r, getattr(r, "sent" + self.name), copies)


class Gather(Scatter):
    def outs(self):
        rows, columns = self.shape
        return {"sent" + self.name: (VMEM, shape((2 * rows, columns), BF))}

    def scratch(self):
        return {}

    def run(self, r, copies):
        out = getattr(r, "sent" + self.name)
        rows = out.shape[0] // 2
        side = kept_side(self.bits)
        for kind, which in (("kept", side), ("got", 1 - side)):
            here = pl.ds(pl.multiple_of(which * rows, 16), rows)
            out[here, :] = getattr(r, f"{kind}{self.name}_0")[...]


def hold_kernel(r):
    pass


def run_hold(order, arrays, mark):
    names = [f"part{index}" for index in range(len(arrays))]
    ins = any_ins(**dict(zip(names, arrays)), mark=mark)
    outs = {"out" + name: (ANY, shape(array.shape, array.dtype)) for name, array in zip(names, arrays)}
    made = call(
        order, hold_kernel, "hold", ins, outs, {},
        aliases={index: index for index in range(len(arrays))}, limit=SMALL_LIMIT,
    )
    return [made["out" + name] for name in names]


class Add:
    def __init__(self, name, value, got):
        self.name, self.value, self.got = name, value, got

    def ins(self):
        return vmem_ins(**{"value" + self.name: self.value, "came" + self.name: self.got})

    def outs(self):
        return {"total" + self.name: (VMEM, shape(self.value.shape, self.value.dtype))}

    def scratch(self):
        return {}

    def copies(self):
        return 0

    def load(self, r, copies):
        pass

    def run(self, r, copies):
        total = getattr(r, "value" + self.name)[...].astype(F32) + getattr(r, "came" + self.name)[...].astype(F32)
        getattr(r, "total" + self.name)[...] = total.astype(self.value.dtype)


def run_step(order, sums, held):
    jobs = [one.job() for one in sums]
    ins, outs, scratch = {}, dict(mark_next=(VMEM, shape((8, LANES), F32))), {}
    for job in jobs:
        ins.update(job.ins())
        outs.update(job.outs())
        scratch.update(job.scratch())
    copies = sum(job.copies() for job in jobs)
    if copies:
        scratch["sem"] = DMA((copies,))
    made = call(
        order,
        functools.partial(step_kernel, jobs),
        "sum_step",
        ins,
        outs,
        scratch,
        limit=VMEM_LIMIT if copies else SMALL_LIMIT,
    )
    if held:
        names = [name for name in made if name.startswith("sent")]
        arrays = run_hold(order, [made[name] for name in names], swap(made["mark_next"]))
        made.update(zip(names, arrays))
    for one in sums:
        one.take(made)


def finish_kernel(pieces, kind, r):
    conv_rows = r.conv.shape[1]
    copies = Copies(r.sem)
    loads, edges = [], []
    for index, (unit, piece) in enumerate(pieces):
        there = pl.ds(piece.place, piece.rows)
        loads.append(copies.start(getattr(r, "part" + piece.name).at[there], getattr(r, f"chunk{index}")))
    for index, (unit, piece) in enumerate(pieces):
        side = kept_side(piece.bits)
        which = side if kind == "part" else 1 - side
        rows = piece.rows
        wide = getattr(r, f"wide{index}")
        copies.wait(loads[index])
        wide[...] = getattr(r, f"chunk{index}")[...].astype(F32)
        if piece.start + 2 * rows <= conv_rows:
            there = pl.ds(pl.multiple_of(piece.start + which * rows, 16), rows)
            copies.start(wide, r.conv.at[unit, there])
            continue
        for choice in range(2):
            start = piece.start + choice * rows
            edge = min(max(conv_rows - start, 0), rows)
            parts = []
            if edge > 0:
                parts.append((wide.at[pl.ds(0, edge)], r.conv.at[unit, pl.ds(start, edge)]))
            if edge < rows:
                target = r.point.at[unit, pl.ds(start + edge - conv_rows, rows - edge)]
                parts.append((wide.at[pl.ds(edge, rows - edge)], target))
            made = [
                pltpu.make_async_copy(source, target, r.edge_sem.at[index, number])
                for number, (source, target) in enumerate(parts)
            ]
            edges.append((which == choice, made))

            @pl.when(which == choice)
            def _():
                for copy in made:
                    copy.start()

    for chosen, made in edges:

        @pl.when(chosen)
        def _():
            for copy in made:
                copy.wait()

    copies.wait_all()


def run_finish(order, pieces, kind, arrays, before, full):
    half = arrays[0].shape[1]
    ins = {}
    if before is not None:
        ins.update(any_ins(conv_in=before["conv"], point_in=before["point"]))
    ins.update(any_ins(**{f"part{index}": array for index, array in enumerate(arrays)}))
    scratch = {}
    for index, (_, piece) in enumerate(pieces):
        scratch[f"chunk{index}"] = pltpu.VMEM((piece.rows, half), BF)
        scratch[f"wide{index}"] = pltpu.VMEM((piece.rows, half), F32)
    scratch["sem"] = DMA((2 * len(pieces),))
    scratch["edge_sem"] = DMA((len(pieces), 2))
    return call(
        order,
        functools.partial(finish_kernel, pieces, kind),
        "finish",
        ins,
        dict(
            conv=(ANY, shape((3, K * full, half), F32)),
            point=(ANY, shape((3, full, half), F32)),
        ),
        scratch,
        aliases=None if before is None else {0: 0, 1: 1},
    )


def collect_kernel(r):
    half = r.mine.shape[1]
    code = r.w_expand.shape[0]
    core = lax.axis_index(CHAN)
    own, oth = both_columns(half)
    r.rate_v[...] = jnp.zeros(r.rate_v.shape, F32)
    for index in range(7):
        rate = getattr(r, f"rate{index}")
        r.rate_v[index : index + 1, :] = jnp.sum(rate[...], axis=0, keepdims=True)
    r.mine[:8, :] = r.rate_v[:, own]
    r.other[:8, :] = r.rate_v[:, oth]
    r.other[8:, :] = jnp.zeros((r.other.shape[0] - 8, half), F32)
    blocks, width = r.mixed_mine.shape
    wide = jnp.concatenate([r.w_expand[...].astype(F32)] * (width // code), axis=0).astype(BF)
    lane = lax.broadcasted_iota(jnp.int32, (blocks, width), 1)
    total = jnp.zeros((code, r.out_grad.shape[3]), F32)
    for row, mixed in ((core, r.mixed_mine), (1 - core, r.mixed_got)):
        value = mixed[...]
        once = jnp.where(lane < code, value.astype(F32), 0.0).astype(BF)
        r.block_out[row, 0] = dot(once, wide).astype(BF)
        sums = lax.dot_general(
            value, r.out_grad[row, 0], (((0,), (0,)), ((), ())), preferred_element_type=F32
        )
        total = total + sums[:code, :]
    for index in range(total.shape[1] // half):
        r.mine[8 * (index + 1) : 8 * (index + 2), :] = total[:, index * half : (index + 1) * half]


def run_collect(order, rates, mixed_mine, mixed_got, out_grad, w_expand, half):
    part = (VMEM, shape((8 + 8 * (w_expand.shape[1] // half), half), F32))
    made = call(
        order,
        collect_kernel,
        "collect",
        vmem_ins(
            **{f"rate{index}": rate for index, rate in enumerate(rates)},
            mixed_mine=mixed_mine, mixed_got=mixed_got, out_grad=out_grad, w_expand=w_expand,
        ),
        dict(block_out=(VMEM, shape(out_grad.shape, BF)), mine=part, other=part),
        dict(rate_v=pltpu.VMEM((8, 2 * half), F32)),
        limit=SMALL_LIMIT,
    )
    return made["block_out"], made["mine"], made["other"]


def place_kernel(r):
    core = lax.axis_index(CHAN)
    copies = Copies(r.sem)
    frames = r.got.shape[0]
    moved = [
        (copies.start(r.got.at[there], r.room.at[there]), there) for _, there in tiles_of(frames)
    ]
    for number, there in moved:
        copies.wait(number)
        copies.start(r.room.at[there], r.out.at[1 - core, 0, there])
    copies.wait_all()


def run_place(order, mine, got):
    return call(
        order,
        place_kernel,
        "place_rows",
        any_ins(mine=mine, got=got),
        dict(out=(ANY, shape(mine.shape, mine.dtype))),
        dict(room=pltpu.VMEM(got.shape, got.dtype), sem=DMA((2 * (got.shape[0] // TILE),))),
        aliases={0: 0},
        limit=SMALL_LIMIT,
    )["out"]


def codebook_kernel(r):
    rows, half = r.mine.shape
    code = r.codebook.shape[0]
    core = lax.axis_index(CHAN)
    sums = jnp.where(core == 0, r.got[...].astype(F32), r.mine[...].astype(F32))
    for index in range(rows // code):
        r.total[:, index * half : (index + 1) * half] = sums[index * code : (index + 1) * code, :]
    columns = r.codebook[...]
    scale = lax.rsqrt(jnp.sum(columns * columns, axis=0, keepdims=True) + 1.0)
    unit = columns * scale
    grad = r.total[...]
    r.out[...] = scale * (grad - unit * jnp.sum(unit * grad, axis=0, keepdims=True))


def run_codebook(order, mine, got, codebook):
    return call(
        order,
        codebook_kernel,
        "codebook_grads",
        vmem_ins(mine=mine, got=got, codebook=codebook),
        dict(out=(VMEM, shape(codebook.shape, F32))),
        dict(total=pltpu.VMEM(codebook.shape, F32)),
        limit=SMALL_LIMIT,
    )["out"]


def chip_axes(count):
    bits = count.bit_length() - 1
    side = bits // 3
    return list(range(side)), list(range(side, 2 * side)), list(range(2 * side, bits))


def two_orders(count):
    x, y, z = chip_axes(count)
    back = z[::-1]
    return ((x + y + z, y + x + back), (z + y + x, back + y + x))


def piece_plan(full, count):
    orders = two_orders(count)
    rows = (K + 1) * full
    cut = 11 * rows // 16
    plan = {2: [], 1: [], 0: []}
    for seq, (share, start) in enumerate(((cut // 2, 0), ((rows - cut) // 2, cut))):
        bits = (orders[seq][0][0], orders[seq][1][0])
        place = 0
        for unit in (2, 1, 0):
            plan[unit].append(Piece(f"{seq}", start, share, place, bits))
            place += share
    return plan


def exchange(values, count, bits):
    pairs = []
    for chip in range(count):
        for core in range(2):
            pairs.append((2 * chip + core, 2 * (chip ^ (1 << bits[core])) + core))
    return lax.ppermute(values, (DP, CHAN), pairs)


def swap(values):
    return lax.ppermute(values, CHAN, [(0, 1), (1, 0)])


class PartSum:
    def __init__(self, name, count, cores):
        self.name = name
        self.count = count
        self.steps = list(zip(*cores))
        self.level = 0
        self.scattering = True
        self.kept = []
        self.got = []

    def begin(self, sent, kept):
        self.kept.append(kept)
        self.got.append(exchange(sent, self.count, self.steps[0]))

    def job(self):
        if not self.scattering:
            return Gather(self.name, [self.sent], self.got, self.steps[self.level])
        if self.level + 1 < len(self.steps):
            large = self.level < 1
            unit = 16 << (len(self.steps) - 1 - self.level)
            return Scatter(self.name, self.kept, self.got, self.steps[self.level + 1], large, unit)
        return Reduce(self.name, self.kept, self.got, None)

    def take(self, made):
        if not self.scattering:
            self.level -= 1
        elif self.level + 1 < len(self.steps):
            self.level += 1
            self.kept = [made["next" + self.name]]
        else:
            self.scattering = False
        self.sent = made["sent" + self.name]
        self.got = [exchange(self.sent, self.count, self.steps[self.level])]

    def ready(self):
        return not self.scattering and self.level == 0


class SmallSum:
    def __init__(self, name, mine, other, count, order):
        self.name, self.count, self.order = name, count, order
        self.value = mine
        self.got = swap(other)
        self.level = 0

    def job(self):
        return Add(self.name, self.value, self.got)

    def take(self, made):
        self.value = made["total" + self.name]
        if self.level < len(self.order):
            bit = self.order[self.level]
            self.got = exchange(self.value, self.count, (bit, bit))
        self.level += 1

    def ready(self):
        return self.level > len(self.order)


def shards(
    frames_in,
    utter_lengths,
    code_ids,
    alpha_first,
    alpha_second,
    alpha_last,
    w_dilated,
    w_point,
    w_down,
    w_latent,
    w_expand,
    codebook,
    out_grad,
):
    count = lax.axis_size(DP)
    half = frames_in.shape[3]
    full = 2 * half
    codes = codebook.shape[1]
    order = Order()

    frames_got = swap(frames_in)
    p_got = swap(w_point)
    w_mine = w_dilated.reshape(3, K * full, half)
    w_got = swap(w_mine)
    alpha_rows = jnp.concatenate([alpha_first, alpha_second, alpha_last[None]], axis=0)
    place = (utter_lengths, alpha_rows, swap(alpha_rows))

    ready = run_prepare(order, w_down, w_latent, w_expand, out_grad, code_ids, codebook)
    back_got = swap(ready["back_sent"])
    made = run_forward(
        order, place, frames_in, frames_got, w_mine, w_got, w_point, p_got,
        dict(
            down_mine=ready["down_mine"], down_other=swap(ready["down_mine"]),
            chosen=ready["chosen"], back_mine=ready["back_mine"], back_other=back_got,
        ),
    )
    seen = [made[f"seen{u}"] for u in range(3)]
    rates = [None] * 5 + [made["rates"], made["last_rates"]]
    grads = [None, None, (made["mine"], swap(made["other"]), made["other"])]
    seen_got = [None, None, swap(seen[2])]
    running, dilated, grad = made["running"], made["dilated"], made["grad"]

    def open_unit(u, grad):
        made = run_opening(
            order, u, place, grads[u][0], grads[u][2], running, grad, dilated, w_mine, w_got, w_point, p_got
        )
        rates[u] = made["rates"]
        if u > 0:
            rates[2 + u] = made["mid_rates"]
            grads[u - 1] = (made["mine"], swap(made["other"]), made["other"])
        return made

    x, y, z = chip_axes(count)
    code_mine, code_sent = run_code_grad(
        order, ready["ids_t"], ready["back_mine"], back_got, made["down_sum"], codes
    )
    codes_sum = SmallSum("", code_mine, code_sent, count, z[::-1] + y + x)
    plan = piece_plan(full, count)
    sums = [PartSum(f"{index}", count, cores) for index, cores in enumerate(two_orders(count))]

    def advance(*more):
        steps = [one for one in sums + list(more) if not one.ready()]
        held = not sums[0].scattering or sums[0].level + 1 == len(sums[0].steps)
        run_step(order, steps, held)

    def weigh(u):
        made = run_weight(
            order, u, place, seen[u], seen_got[u], grads[u][0], grads[u][1], plan[u],
            (codes_sum.value, codes_sum.got) if u > 0 else None,
        )
        if u > 0:
            codes_sum.take(made)
        for index, one in enumerate(sums):
            one.begin(made[f"sent{index}"], made[f"kept{index}"])

    grad = open_unit(2, grad)["grad"]
    seen_got[1] = swap(seen[1])
    order.before += [seen_got[1]]
    weigh(2)
    first = [one.got[0] for one in sums]
    grad = open_unit(1, grad)["grad"]
    seen_got[0] = swap(seen[0])
    mixed_got = swap(made["mixed"])
    order.before += first + [seen_got[0], mixed_got]
    weigh(1)
    weigh(0)
    last = open_unit(0, grad)
    frames_back = swap(last["frames_sent"])
    advance(codes_sum)
    block_out, small_mine, small_other = run_collect(
        order, rates, made["mixed"], mixed_got, out_grad, w_expand, half
    )
    small = SmallSum("small", small_mine, small_other, count, z + y + x)
    grad_frames = run_place(order, last["frames_mine"], frames_back)
    while not (codes_sum.ready() or sums[0].ready()):
        advance(codes_sum, small)
    codes_back = swap(codes_sum.value)
    advance(small)
    grad_codebook = run_codebook(order, codes_sum.value, codes_back, codebook)
    while not sums[0].ready():
        advance(small)
    pieces = [(unit, piece) for unit in (2, 1, 0) for piece in plan[unit]]
    written = run_finish(order, pieces, "part", [one.sent for one in sums], None, full)
    grad_w_down, grad_w_latent = run_down(order, codes_sum.value, codes_back, w_latent, w_down)
    while not small.ready():
        run_step(order, [small], False)
    written = run_finish(order, pieces, "got", [one.got[0] for one in sums], written, full)
    grad_w_dilated, grad_w_point = written["conv"], written["point"]
    small = small.value
    return (
        block_out,
        grad_frames,
        small[0:3],
        small[3:6],
        small[6],
        grad_w_dilated.reshape(3, K, full, half),
        grad_w_point,
        grad_w_down,
        grad_w_latent,
        jnp.concatenate(
            [small[start : start + 8] for start in range(8, small.shape[0], 8)], axis=1
        ),
        grad_codebook,
    )


def solution(mesh):
    placed = (
        P(None, DP, None, CHAN),
        P(None, DP, None),
        P(None, DP, None),
        P(None, CHAN),
        P(None, CHAN),
        P(CHAN),
        P(None, None, None, CHAN),
        P(None, None, CHAN),
        P(None, None, CHAN),
        P(CHAN, None),
        P(None, CHAN),
        P(),
        P(None, DP, None, CHAN),
    )
    return jax.shard_map(
        shards,
        mesh=mesh,
        in_specs=placed,
        out_specs=(
            P(None, DP, None, CHAN),
            P(None, DP, None, CHAN),
            P(None, CHAN),
            P(None, CHAN),
            P(CHAN),
            P(None, None, None, CHAN),
            P(None, None, CHAN),
            P(None, None, CHAN),
            P(CHAN, None),
            P(None, CHAN),
            P(),
        ),
        check_vma=False,
    )
```

```python
import functools
import types
import jax
import jax.numpy as jnp
from jax import lax
from jax.experimental import pallas as pl
from jax.experimental.pallas import tpu as pltpu
from jax.sharding import PartitionSpec as P

DP = "dp"
CHAN = "chan"
K = 7
STRIDE = 8
KS = 16
DILATIONS = (1, 3, 9)
BF = jnp.bfloat16
F32 = jnp.float32
HALO = 32
TILE = 256
LANES = 128
SINE = (3.141592580569316, -5.1677069002071025, 2.550031640919103, -0.5980464504720939, 0.0772222489218058)
COSINE = (0.9999999534666402, -4.934792858671753, 4.058411914096722, -1.3318801607983635, 0.2196967977026182)
VMEM_LIMIT = 60 * 1024 * 1024
SMALL_LIMIT = 16 * 1024 * 1024
COST = dict(prepare=9, forward=36, code_grads=3, weight_grads=10, opening=15)
ANY = pl.BlockSpec(memory_space=pl.ANY)
SMEM = pl.BlockSpec(memory_space=pltpu.SMEM)
VMEM = pl.BlockSpec(memory_space=pltpu.VMEM)
DMA = pltpu.SemaphoreType.DMA


def shape(dims, kind):
    return jax.ShapeDtypeStruct(dims, kind)


class Order:
    def __init__(self):
        self.token = None
        self.before = []


def call(order, kernel, name, ins, outs, scratch, aliases=None, limit=VMEM_LIMIT):
    deps = ([] if order.token is None else [order.token]) + order.before
    order.before = []

    def body(*refs):
        refs = list(refs)
        named = dict(zip(ins, refs))
        refs = refs[len(ins) + len(deps) :]
        named.update(zip(outs, refs))
        refs[len(outs)][0] = jnp.int32(0)
        named.update(zip(scratch, refs[len(outs) + 1 :]))
        kernel(types.SimpleNamespace(**named))

    made = pl.pallas_call(
        body,
        out_shape=[out for _, out in outs.values()] + [shape((1,), jnp.int32)],
        in_specs=[spec for spec, _ in ins.values()] + [ANY] * len(deps),
        out_specs=[spec for spec, _ in outs.values()] + [SMEM],
        scratch_shapes=list(scratch.values()),
        input_output_aliases=aliases or {},
        compiler_params=pltpu.CompilerParams(vmem_limit_bytes=limit),
        cost_estimate=pl.CostEstimate(
            flops=COST.get(name, 0) << 30, bytes_accessed=COST.get(name, 0) * 3500000, transcendentals=0
        ),
        name=name,
    )(*[array for _, array in ins.values()], *deps)
    order.token = made[-1]
    return dict(zip(outs, made))


class Copies:
    def __init__(self, sem):
        self.sem = sem
        self.made = []
        self.done = set()

    def start(self, source, target):
        copy = pltpu.make_async_copy(source, target, self.sem.at[len(self.made)])
        copy.start()
        self.made.append(copy)
        return len(self.made) - 1

    def wait(self, *numbers):
        for number in numbers:
            if number not in self.done:
                self.done.add(number)
                self.made[number].wait()

    def wait_all(self):
        self.wait(*range(len(self.made)))


def dot(left, right):
    return jnp.dot(left, right, preferred_element_type=F32)


def dot_cols(left, right):
    return lax.dot_general(left, right, (((1,), (1,)), ((), ())), preferred_element_type=F32)


def poly(u, terms):
    total = terms[-1]
    for term in terms[-2::-1]:
        total = total * u + term
    return total


def half_turns(v, alpha):
    turns = v * (alpha * 0.3183098861837907)
    return turns - jnp.round(turns)


def snake(v, alpha):
    t = half_turns(v, alpha)
    u = t * t
    p = poly(u, SINE)
    return v + (u * (p * p)) * (1.0 / alpha)


def snake_slopes(v, alpha):
    t = half_turns(v, alpha)
    u = t * t
    sine = t * poly(u, SINE)
    double = 2.0 * sine * poly(u, COSINE)
    return sine * sine, double


def ends_of(lengths, row):
    ends = []
    total = 0
    for utt in range(lengths.shape[2]):
        total = total + lengths[row, 0, utt] * STRIDE
        ends.append(total)
    return ends


def put_labels(label_ref, ends, frames):
    t = lax.broadcasted_iota(jnp.int32, label_ref.shape, 0) - HALO
    label = jnp.zeros(label_ref.shape, jnp.int32)
    for end in ends:
        label = label + (t >= end).astype(jnp.int32)
    label_ref[...] = jnp.where((t < 0) | (t >= frames), -1, label)


def put_edges(padded_ref, frames):
    edge = jnp.zeros((HALO, padded_ref.shape[1]), F32)
    padded_ref[:HALO, :] = edge
    padded_ref[HALO + frames :, :] = edge


def tap(padded_ref, label_ref, row, rows, offset):
    here = HALO + row
    width = padded_ref.shape[1]
    same = label_ref[here + offset : here + offset + rows, :] == label_ref[here : here + rows, :]
    pieces = []
    for lane in range(0, width, LANES):
        piece = padded_ref[here + offset : here + offset + rows, lane : lane + LANES]
        pieces.append(jnp.where(same, piece, 0.0).astype(BF))
    return jnp.concatenate(pieces, axis=1)


def column_half(core, half):
    return pl.ds(pl.multiple_of(core * half, half), half)


def both_columns(half):
    core = lax.axis_index(CHAN)
    return column_half(core, half), column_half(1 - core, half)


def put_row(target, mine, other, index, own, oth):
    half = mine.shape[1]
    target[:, own] = jnp.broadcast_to(mine[index : index + 1, :], (8, half))
    target[:, oth] = jnp.broadcast_to(other[index : index + 1, :], (8, half))
    return target[0:1, :]


def split(values, terms):
    parts = []
    for _ in range(terms):
        part = values.astype(BF)
        parts.append(part)
        values = values - part.astype(F32)
    return parts


def row_sums(values):
    return jnp.sum(values.reshape(values.shape[0] // 8, 8, values.shape[1]), axis=0)


def tiles_of(frames):
    return [(slice(start, start + TILE), pl.ds(start, TILE)) for start in range(0, frames, TILE)]


def forward_kernel(r):
    frames, full = r.run_v.shape[1:]
    half = full // 2
    core = lax.axis_index(CHAN)
    own, oth = both_columns(half)
    copies = Copies(r.sem)
    tiles = tiles_of(frames)
    place = [
        copies.start(r.lengths, r.lengths_v),
        copies.start(r.alpha_mine, r.alpha_mv),
        copies.start(r.alpha_other, r.alpha_ov),
    ]
    loads = [copies.start(r.frames_in.at[core, 0], r.mine_v), copies.start(r.frames_got.at[core, 0], r.other_v)]

    def load_weights(unit):
        return [
            copies.start(r.w_mine.at[unit], r.w_v.at[unit % 2, 0]),
            copies.start(r.w_other.at[unit], r.w_v.at[unit % 2, 1]),
        ]

    weights = [load_weights(0)]
    points = [copies.start(r.p_mine, r.pm_v), copies.start(r.p_other, r.po_v)]
    weights.append(load_weights(1))
    small = [
        copies.start(source, target)
        for source, target in (
            (r.down_mine, r.dm_v), (r.down_other, r.do_v), (r.chosen, r.chosen_v),
            (r.back_mine, r.bm_v), (r.back_other, r.bo_v),
        )
    ]
    put_edges(r.padded, frames)
    copies.wait(*place)
    put_labels(r.label, ends_of(r.lengths_v, core), frames)
    copies.wait(*loads)
    leaving = {(kind, slot): [] for kind in ("run", "mid", "seen") for slot in range(2)}

    def settle(kind, slot):
        copies.wait(*leaving[kind, slot])
        leaving[kind, slot] = []

    for unit in range(3):
        now, later = r.run_v.at[unit % 2], r.run_v.at[(unit + 1) % 2]
        mid = r.mid_v.at[unit % 2]
        seen = r.seen_v.at[unit % 2]
        rate_in = put_row(r.rate_v.at[unit], r.alpha_mv, r.alpha_ov, unit, own, oth)
        rate_mid = put_row(r.rate_v.at[3 + unit], r.alpha_mv, r.alpha_ov, 3 + unit, own, oth)
        settle("seen", unit % 2)
        for rows, there in tiles:
            if unit == 0:
                now[rows, own] = r.mine_v[rows, :].astype(F32)
                now[rows, oth] = r.other_v[rows, :].astype(F32)
                leaving["run", 0].append(copies.start(now.at[there], r.running.at[unit, there]))
            opened = snake(now[rows, :], rate_in)
            r.padded[HALO + rows.start : HALO + rows.stop, :] = opened
            seen[:full, rows] = opened.T.astype(BF)
        seen_out = getattr(r, f"seen{unit}")
        leaving["seen", unit % 2].append(
            copies.start(seen.at[pl.ds(0, full)], seen_out.at[pl.ds(0, full)])
        )
        copies.wait(*weights[unit])
        if unit == 0:
            copies.wait(*points)
        settle("mid", unit % 2)
        settle("run", (unit + 1) % 2)
        for place_of, (rows, there) in enumerate(tiles):
            taps = r.taps.at[place_of % 2]
            for index in range(K):
                offset = DILATIONS[unit] * (index - K // 2)
                taps[:, index * full : (index + 1) * full] = tap(
                    r.padded, r.label, rows.start, TILE, offset
                )
            mid[rows, own] = dot(taps[...], r.w_v[unit % 2, 0])
            mid[rows, oth] = dot(taps[...], r.w_v[unit % 2, 1])
            if unit < 2:
                leaving["mid", unit % 2].append(copies.start(mid.at[there], r.dilated.at[unit, there]))
            closed = snake(mid[rows, :], rate_mid)
            seen[full:, rows] = closed.T.astype(BF)
            closed = closed.astype(BF)
            later[rows, own] = now[rows, own] + dot(closed, r.pm_v[unit])
            later[rows, oth] = now[rows, oth] + dot(closed, r.po_v[unit])
            if unit < 2:
                leaving["run", (unit + 1) % 2].append(
                    copies.start(later.at[there], r.running.at[unit + 1, there])
                )
        leaving["seen", unit % 2].append(
            copies.start(seen.at[pl.ds(full, full)], seen_out.at[pl.ds(full, full)])
        )
        if unit == 0:
            weights.append(load_weights(2))

    running, mid = r.run_v.at[1], r.mid_v.at[0]
    blocks = frames // STRIDE
    value = put_row(r.rate_v.at[6], r.alpha_mv, r.alpha_ov, 6, own, oth)
    mid_value = r.rate_v[5, 0:1, :]
    inverse = 1.0 / value
    copies.wait(*small)
    width = r.dm_v.shape[1]
    code = width // KS
    lane = lax.broadcasted_iota(jnp.int32, (TILE, width), 1) // code
    step = lax.broadcasted_iota(jnp.int32, (TILE, width), 0) % STRIDE
    pattern = (lane % STRIDE == (step + STRIDE // 2) % STRIDE).astype(F32)
    down = r.dm_v[...] + r.do_v[...]
    down_parts = jnp.concatenate(split(down, 3), axis=1)
    sums = []
    for rows, _ in tiles:
        v = running[rows, :]
        square, double = snake_slopes(v, value)
        r.square_v[rows, :] = square
        r.double_v[rows, :] = double
        opened = (v + square * inverse).astype(BF)
        r.opened_v[rows, :] = opened
        products = dot(opened, down_parts)
        products = products[:, :width] + products[:, width : 2 * width] + products[:, 2 * width :]
        products = (products * pattern).reshape(TILE // STRIDE, STRIDE, width)
        sums.append(jnp.sum(products, axis=1))
    sums = jnp.concatenate(sums, axis=0)
    block = lax.broadcasted_iota(jnp.int32, (blocks, width), 0)
    block_lane = lax.broadcasted_iota(jnp.int32, (blocks, width), 1)
    label = jnp.zeros((blocks, width), jnp.int32)
    for end in ends_of(r.lengths_v, core):
        label = label + (block * STRIDE >= end).astype(jnp.int32)

    def earlier(values):
        return pltpu.roll(values, 1, 0)

    def later_rows(values):
        return pltpu.roll(values, blocks - 1, 0)

    same_before = jnp.where((block > 0) & (earlier(label) == label), 1.0, 0.0)
    same_after = jnp.where((block < blocks - 1) & (later_rows(label) == label), 1.0, 0.0)
    early = block_lane < 4 * code
    late = block_lane >= 12 * code
    sums = jnp.where(
        early, same_before * earlier(sums), jnp.where(late, same_after * later_rows(sums), sums)
    )
    fold = (
        lax.broadcasted_iota(jnp.int32, (width, width), 0) % code
        == lax.broadcasted_iota(jnp.int32, (width, width), 1) % code
    ).astype(BF)
    latent = dot(jnp.concatenate(split(sums, 3), axis=1), jnp.concatenate([fold] * 3, axis=0))
    scale = lax.rsqrt(jnp.sum(latent * latent, axis=1, keepdims=True) * (1.0 / KS) + 1.0)
    unit_code = latent * scale
    r.mixed[...] = (unit_code + r.chosen_v[...]).astype(BF)
    back = r.bm_v[...] + r.bo_v[...]
    along = jnp.sum(unit_code * back, axis=1, keepdims=True) * (1.0 / KS)
    spread = (back - unit_code * along) * scale
    spread = jnp.where(
        early,
        later_rows(same_before * spread),
        jnp.where(late, earlier(same_after * spread), spread),
    )
    down_t_parts = split(down.T, 2)
    down_t_stack = jnp.concatenate([down_t_parts[0], down_t_parts[1], down_t_parts[0]], axis=0)
    total = jnp.zeros((8, full), F32)
    last_total = jnp.zeros((8, full), F32)
    down_total = jnp.zeros(down.shape, F32)
    for rows, there in tiles:
        own_blocks = spread[rows.start // STRIDE : rows.stop // STRIDE, :]
        wide = jnp.broadcast_to(
            own_blocks[:, None, :], (TILE // STRIDE, STRIDE, width)
        ).reshape(TILE, width) * pattern
        parts = split(wide, 3)
        sums = lax.dot_general(
            r.opened_v[rows, :],
            jnp.concatenate(parts, axis=1),
            (((0,), (0,)), ((), ())),
            preferred_element_type=F32,
        )
        down_total = down_total + (sums[:, :width] + sums[:, width : 2 * width] + sums[:, 2 * width :])
        grad_last = dot(jnp.concatenate([parts[0], parts[0], parts[1]], axis=1), down_t_stack)
        square = r.square_v[rows, :]
        double = r.double_v[rows, :]
        grad = grad_last * (1.0 + double)
        r.grad_v[rows, :] = grad
        copies.start(r.grad_v.at[there], r.grad.at[there])
        rate = grad_last * (running[rows, :] * double - square * inverse)
        last_total = last_total + row_sums(rate)
        total = total + closing_steps(
            r, rows, grad, mid[rows, :], mid_value, (own, oth), r.pm_v[2], r.po_v[2]
        )
        send_closing(r, copies, rows, there, own, oth)
    r.rates[...] = total * (1.0 / mid_value)
    r.last_rates[...] = last_total * inverse
    r.down_sum[:, :width] = down_total[:half, :].astype(BF)
    r.down_sum[:, width:] = down_total[half:, :].astype(BF)
    copies.wait_all()


def closing_steps(r, rows, point, mid, alpha, core_cols, p_mine, p_other):
    own, oth = core_cols
    r.gp_v[rows, :] = point.astype(BF)
    grad = dot_cols(r.gp_v[rows, own], p_mine) + dot_cols(r.gp_v[rows, oth], p_other)
    square, double = snake_slopes(mid, alpha)
    r.gd_v[rows, :] = (grad * (1.0 + double)).astype(BF)
    return row_sums(grad * (mid * double - square * (1.0 / alpha)))


def send_closing(r, copies, rows, there, own, oth):
    frames = r.gp_v.shape[0]
    after = pl.ds(frames + rows.start, TILE)
    copies.start(r.gp_v.at[there, own], r.mine.at[there])
    copies.start(r.gd_v.at[there, own], r.mine.at[after])
    copies.start(r.gp_v.at[there, oth], r.other.at[there])
    copies.start(r.gd_v.at[there, oth], r.other.at[after])


def place_ins(place):
    return {name: (ANY, array) for name, array in zip(("lengths", "alpha_mine", "alpha_other"), place)}


def place_rooms(place, full):
    lengths, alpha, _ = place
    return dict(
        lengths_v=pltpu.SMEM(lengths.shape, jnp.int32),
        alpha_mv=pltpu.VMEM(alpha.shape, F32),
        alpha_ov=pltpu.VMEM(alpha.shape, F32),
        rate_v=pltpu.VMEM((7, 8, full), F32),
    )


def any_ins(**arrays):
    return {name: (ANY, array) for name, array in arrays.items()}


def vmem_ins(**arrays):
    return {name: (VMEM, array) for name, array in arrays.items()}


def run_forward(order, place, frames_in, frames_got, w_mine, w_other, p_mine, p_other, small):
    frames, half = frames_in.shape[2:]
    full = 2 * half
    tiles = frames // TILE
    blocks = frames // STRIDE
    width = small["down_mine"].shape[1]
    wide = (frames, full)
    pair = (ANY, shape((2 * frames, half), BF))
    square = pltpu.VMEM((blocks, width), F32)
    tall = pltpu.VMEM((full, width), F32)
    return call(
        order,
        forward_kernel,
        "forward",
        dict(
            **place_ins(place),
            **any_ins(frames_in=frames_in, frames_got=frames_got, w_mine=w_mine, w_other=w_other,
                      p_mine=p_mine, p_other=p_other, **small),
        ),
        dict(
            running=(ANY, shape((3,) + wide, F32)),
            dilated=(ANY, shape((2,) + wide, F32)),
            seen0=(ANY, shape((2 * full, frames), BF)),
            seen1=(ANY, shape((2 * full, frames), BF)),
            seen2=(ANY, shape((2 * full, frames), BF)),
            grad=(ANY, shape(wide, F32)),
            mixed=(VMEM, shape((blocks, width), BF)),
            down_sum=(VMEM, shape((half, 2 * width), BF)),
            last_rates=(VMEM, shape((8, full), F32)),
            mine=pair,
            other=pair,
            rates=(VMEM, shape((8, full), F32)),
        ),
        dict(
            **place_rooms(place, full),
            mine_v=pltpu.VMEM((frames, half), BF),
            other_v=pltpu.VMEM((frames, half), BF),
            run_v=pltpu.VMEM((2,) + wide, F32),
            mid_v=pltpu.VMEM((2,) + wide, F32),
            seen_v=pltpu.VMEM((2, 2 * full, frames), BF),
            padded=pltpu.VMEM((frames + 2 * HALO, full), F32),
            label=pltpu.VMEM((frames + 2 * HALO, LANES), jnp.int32),
            taps=pltpu.VMEM((2, TILE, K * full), BF),
            w_v=pltpu.VMEM((2, 2) + w_mine.shape[1:], BF),
            pm_v=pltpu.VMEM(p_mine.shape, BF),
            po_v=pltpu.VMEM(p_mine.shape, BF),
            dm_v=tall, do_v=tall, chosen_v=square, bm_v=square, bo_v=square,
            opened_v=pltpu.VMEM(wide, BF),
            square_v=pltpu.VMEM(wide, F32),
            double_v=pltpu.VMEM(wide, F32),
            grad_v=pltpu.VMEM(wide, F32),
            gp_v=pltpu.VMEM(wide, BF),
            gd_v=pltpu.VMEM(wide, BF),
            sem=DMA((3 + 2 + 6 + 2 + 5 + 5 * tiles + 6 + 5 * tiles,)),
        ),
    )


def weight_kernel(unit, pieces, r):
    frames = r.padded.shape[1] - 2 * HALO
    half = r.padded.shape[2]
    full = 2 * half
    core = lax.axis_index(CHAN)
    copies = Copies(r.sem)
    place = copies.start(r.lengths, r.lengths_v)
    grads = []
    for row, source in enumerate((r.grads_mine, r.grads_got)):
        grads.append(copies.start(source.at[pl.ds(frames, frames)], r.gd_v.at[row]))
    opened = []
    for row, source in enumerate((r.seen_mine, r.seen_got)):
        columns = pl.ds(row * frames, frames)
        opened.append(copies.start(source.at[pl.ds(0, full)], r.seen_v.at[pl.ds(0, full), columns]))
    points = []
    for row, (source, seen) in enumerate(((r.grads_mine, r.seen_mine), (r.grads_got, r.seen_got))):
        columns = pl.ds(row * frames, frames)
        points.append(copies.start(source.at[pl.ds(0, frames)], r.gp_v.at[columns]))
        points.append(copies.start(seen.at[pl.ds(full, full)], r.seen_v.at[pl.ds(full, full), columns]))
    if hasattr(r, "value"):
        beside = [copies.start(r.value, r.value_v), copies.start(r.came, r.came_v)]
    for row in range(2):
        put_edges(r.padded.at[row], frames)
    copies.wait(place)
    for row in range(2):
        put_labels(r.label.at[row], ends_of(r.lengths_v, core if row == 0 else 1 - core), frames)
    for row in range(2):
        copies.wait(grads[row])
        r.padded[row, HALO : HALO + frames, :] = r.gd_v[row].astype(F32)
    copies.wait(*opened)
    for index in range(K):
        offset = -DILATIONS[unit] * (index - K // 2)
        taps = r.taps.at[index % 2]
        for row in range(2):
            for start in range(0, frames, TILE):
                taps[row * frames + start : row * frames + start + TILE, :] = tap(
                    r.padded.at[row], r.label.at[row], start, TILE, offset
                )
        r.out_v[index * full : (index + 1) * full, :] = dot(r.seen_v[:full, :], taps[...]).astype(BF)
    if hasattr(r, "value"):
        copies.wait(*beside)
        total = r.value_v[...].astype(F32) + r.came_v[...].astype(F32)
        r.value_v[...] = total.astype(BF)
        copies.start(r.value_v, r.total)
    copies.wait(*points)
    r.out_v[K * full : (K + 1) * full, :] = dot(r.seen_v[full:, :], r.gp_v[...]).astype(BF)
    for piece in pieces:
        side = kept_side(piece.bits)
        there = pl.ds(0, piece.rows)
        for kind, which in (("sent", 1 - side), ("kept", side)):
            here = pl.ds(pl.multiple_of(piece.start + which * piece.rows, 16), piece.rows)
            copies.start(r.out_v.at[here], getattr(r, kind + piece.name).at[there])
    copies.wait_all()


def kept_side(bits):
    bit = jnp.where(lax.axis_index(CHAN) == 0, bits[0], bits[1])
    return lax.shift_right_logical(lax.axis_index(DP), bit) & 1


class Piece:
    def __init__(self, name, start, rows, place, bits, span):
        self.name, self.start, self.rows, self.place, self.bits, self.span = name, start, rows, place, bits, span


def run_weight(order, unit, place, seen_mine, seen_got, grads_mine, grads_got, pieces, beside=None):
    frames, half = grads_mine.shape[0] // 2, grads_mine.shape[1]
    full = 2 * half
    ins = any_ins(lengths=place[0], seen_mine=seen_mine, seen_got=seen_got,
                  grads_mine=grads_mine, grads_got=grads_got)
    scratch = dict(
        lengths_v=pltpu.SMEM(place[0].shape, jnp.int32),
        seen_v=pltpu.VMEM((2 * full, 2 * frames), BF),
        gd_v=pltpu.VMEM((2, frames, half), BF),
        gp_v=pltpu.VMEM((2 * frames, half), BF),
        padded=pltpu.VMEM((2, frames + 2 * HALO, half), F32),
        label=pltpu.VMEM((2, frames + 2 * HALO, LANES), jnp.int32),
        taps=pltpu.VMEM((2, 2 * frames, half), BF),
        out_v=pltpu.VMEM(((K + 1) * full, half), BF),
        sem=DMA((12 + 2 * len(pieces),)),
    )
    outs = {
        kind + piece.name: (ANY, shape((piece.rows, half), BF))
        for piece in pieces
        for kind in ("sent", "kept")
    }
    if beside is not None:
        value, came = beside
        ins.update(any_ins(value=value, came=came))
        outs["total"] = (ANY, shape(value.shape, BF))
        scratch.update(value_v=pltpu.VMEM(value.shape, BF), came_v=pltpu.VMEM(value.shape, BF))
    return call(
        order, functools.partial(weight_kernel, unit, pieces), "weight_grads", ins, outs, scratch
    )


def opening_kernel(unit, r):
    last = unit == 0
    frames, full = r.running_v.shape
    half = full // 2
    core = lax.axis_index(CHAN)
    own, oth = both_columns(half)
    copies = Copies(r.sem)
    tiles = tiles_of(frames)
    place = [
        copies.start(r.lengths, r.lengths_v),
        copies.start(r.alpha_mine, r.alpha_mv),
        copies.start(r.alpha_other, r.alpha_ov),
    ]
    after = pl.ds(frames, frames)
    grads = [
        copies.start(r.grads_mine.at[after], r.gm_v),
        copies.start(r.grads_other.at[after], r.go_v),
    ]
    weights = [
        copies.start(r.w_mine.at[unit], r.w_v.at[0]),
        copies.start(r.w_other.at[unit], r.w_v.at[1]),
    ]
    if not last:
        points = [
            copies.start(r.p_mine.at[unit - 1], r.pm_v),
            copies.start(r.p_other.at[unit - 1], r.po_v),
        ]
    loads = []
    for _, there in tiles:
        loads.append([
            copies.start(r.running.at[unit, there], r.running_v.at[there]),
            copies.start(r.grad_in.at[there], r.grad_v.at[there]),
        ])
        if not last:
            loads[-1].append(copies.start(r.dilated.at[unit - 1, there], r.mid_v.at[there]))
    for part in range(2):
        put_edges(r.padded.at[part], frames)
    copies.wait(*place)
    put_labels(r.label, ends_of(r.lengths_v, core), frames)
    value = put_row(r.rate_v.at[0], r.alpha_mv, r.alpha_ov, unit, own, oth)
    if not last:
        mid_value = put_row(r.rate_v.at[1], r.alpha_mv, r.alpha_ov, 2 + unit, own, oth)
    for part, values in ((0, r.gm_v), (1, r.go_v)):
        copies.wait(grads[part])
        r.padded[part, HALO : HALO + frames, :] = values[...].astype(F32)
    copies.wait(*weights)
    for part in range(2):
        for index in range(K):
            r.turned_v[(2 * index + part) * half : (2 * index + part + 1) * half, :] = r.w_v[
                part, index * full : (index + 1) * full, :
            ].T
    if not last:
        copies.wait(*points)
    total = jnp.zeros((8, full), F32)
    mid_total = jnp.zeros((8, full), F32)
    for place_of, (rows, there) in enumerate(tiles):
        taps = r.taps.at[place_of % 2]
        for index in range(K):
            offset = -DILATIONS[unit] * (index - K // 2)
            for part in range(2):
                start = (2 * index + part) * half
                taps[:, start : start + half] = tap(
                    r.padded.at[part], r.label, rows.start, TILE, offset
                )
        opened = dot(taps[...], r.turned_v[...])
        copies.wait(*loads[place_of])
        v = r.running_v[rows, :]
        square, double = snake_slopes(v, value)
        grad = r.grad_v[rows, :] + opened * (1.0 + double)
        r.grad_v[rows, :] = grad
        total = total + row_sums(opened * (v * double - square * (1.0 / value)))
        if last:
            copies.start(r.grad_v.at[there, own], r.frames_mine.at[core, 0, there])
            copies.start(r.grad_v.at[there, oth], r.frames_sent.at[there])
        else:
            copies.start(r.grad_v.at[there], r.grad.at[there])
            mid_total = mid_total + closing_steps(
                r, rows, grad, r.mid_v[rows, :], mid_value, (own, oth), r.pm_v[...], r.po_v[...]
            )
            send_closing(r, copies, rows, there, own, oth)
    r.rates[...] = total * (1.0 / value)
    if not last:
        r.mid_rates[...] = mid_total * (1.0 / mid_value)
    copies.wait_all()


def run_opening(order, unit, place, grads_mine, grads_other, running, grad, dilated, w_mine, w_other, p_mine, p_other):
    frames, full = grad.shape
    half = full // 2
    tiles = frames // TILE
    last = unit == 0
    wide = pltpu.VMEM((frames, full), F32)
    narrow = pltpu.VMEM((frames, full), BF)
    part = pltpu.VMEM((frames, half), BF)
    point = pltpu.VMEM(p_mine.shape[1:], BF)
    pair = (ANY, shape((2 * frames, half), BF))
    rates = (VMEM, shape((8, full), F32))
    ins = dict(
        **place_ins(place),
        **any_ins(grads_mine=grads_mine, grads_other=grads_other, running=running, grad_in=grad,
                  w_mine=w_mine, w_other=w_other),
    )
    outs = dict(rates=rates)
    scratch = dict(
        **place_rooms(place, full),
        gm_v=part, go_v=part,
        padded=pltpu.VMEM((2, frames + 2 * HALO, half), F32),
        label=pltpu.VMEM((frames + 2 * HALO, LANES), jnp.int32),
        running_v=wide, grad_v=wide,
        w_v=pltpu.VMEM((2,) + w_mine.shape[1:], BF),
        turned_v=pltpu.VMEM((K * full, full), BF),
        taps=pltpu.VMEM((2, TILE, K * full), BF),
    )
    if last:
        outs["frames_mine"] = (ANY, shape((2, 1, frames, half), F32))
        outs["frames_sent"] = (ANY, shape((frames, half), F32))
    else:
        ins.update(any_ins(dilated=dilated, p_mine=p_mine, p_other=p_other))
        outs.update(grad=(ANY, shape((frames, full), F32)), mine=pair, other=pair, mid_rates=rates)
        scratch.update(mid_v=wide, pm_v=point, po_v=point, gp_v=narrow, gd_v=narrow)
    scratch["sem"] = DMA((3 + 2 + 2 + 2 + 8 * tiles,))
    return call(
        order, functools.partial(opening_kernel, unit), "opening", ins, outs, scratch
    )


def prepare_kernel(r):
    taps, full, out_half = r.w_down.shape
    code, codes = r.codebook.shape
    blocks = r.ids.shape[2]
    width = taps * code
    core = lax.axis_index(CHAN)
    copies = Copies(r.sem)
    first = [copies.start(r.ids.at[core], r.ids_v), copies.start(r.codebook, r.book_v)]
    loads = [copies.start(r.w_down.at[index], r.down_v.at[index]) for index in range(taps)]
    copies.wait(*first)
    mark = r.ids_v[...]
    total = jnp.zeros((3 * code, blocks), F32)
    step = 1024
    for start in range(0, codes, step):
        columns = r.book_v[:, start : start + step]
        unit = columns * lax.rsqrt(jnp.sum(columns * columns, axis=0, keepdims=True) + 1.0)
        parts = jnp.concatenate([part.astype(F32) for part in split(unit, 3)], axis=0).astype(BF)
        number = lax.broadcasted_iota(jnp.int32, (step, blocks), 0) + start
        total = total + dot(parts, jnp.where(number == mark, 1.0, 0.0).astype(BF))
    picked = total[:code] + total[code : 2 * code] + total[2 * code :]
    r.chosen[...] = jnp.concatenate([picked] * taps, axis=0).T
    r.ids_t[...] = jnp.broadcast_to(mark.astype(F32), (blocks, blocks)).T
    expand = jnp.concatenate([r.w_expand[...].astype(F32)] * taps, axis=0).astype(BF)
    r.back_mine[...] = dot_cols(r.out_grad[core, 0], expand)
    r.back_sent[...] = dot_cols(r.out_grad[1 - core, 0], expand)
    fold = (
        lax.broadcasted_iota(jnp.int32, (code, width), 0)
        == lax.broadcasted_iota(jnp.int32, (code, width), 1) % code
    ).astype(BF)
    latent = dot(r.w_latent[...], fold)
    group = lax.broadcasted_iota(jnp.int32, (out_half, width), 1) // code
    product = jnp.zeros((full, width), F32)
    for index in range(taps):
        copies.wait(loads[index])
        product = product + dot(r.down_v[index], jnp.where(group == index, latent, 0.0).astype(BF))
    r.down_mine[...] = product


def run_prepare(order, w_down, w_latent, w_expand, out_grad, ids, codebook):
    taps, full, _ = w_down.shape
    width = taps * codebook.shape[0]
    blocks = ids.shape[2]
    square = (VMEM, shape((blocks, width), F32))
    return call(
        order,
        prepare_kernel,
        "prepare",
        dict(
            **any_ins(w_down=w_down, ids=ids, codebook=codebook),
            **vmem_ins(w_latent=w_latent, w_expand=w_expand, out_grad=out_grad),
        ),
        dict(
            down_mine=(VMEM, shape((full, width), F32)),
            chosen=square, back_mine=square, back_sent=square,
            ids_t=(VMEM, shape((blocks, blocks), F32)),
        ),
        dict(
            down_v=pltpu.VMEM(w_down.shape, BF),
            book_v=pltpu.VMEM(codebook.shape, F32),
            ids_v=pltpu.VMEM(ids.shape[1:], jnp.int32),
            sem=DMA((taps + 2,)),
        ),
    )


def code_grad_kernel(r):
    blocks, width = r.back_mine.shape
    rows, half = r.mine.shape
    code = width // KS
    core = lax.axis_index(CHAN)
    back = (r.back_mine[...] + r.back_other[...]).T[:code, :]
    parts = jnp.concatenate([part.astype(F32) for part in split(back, 3)], axis=0).astype(BF)
    for index in range(rows // code):
        pieces = []
        for lane in range(0, half, blocks):
            number = lax.broadcasted_iota(jnp.int32, (blocks, blocks), 1) + (index * half + lane)
            pieces.append(jnp.where(r.ids_t[...] == number.astype(F32), 1.0, 0.0).astype(BF))
        sums = dot(parts, jnp.concatenate(pieces, axis=1))
        r.stage[index * code : (index + 1) * code, :] = (
            sums[:code] + sums[code : 2 * code] + sums[2 * code :]
        )
    down = r.down_sum[...].astype(F32)
    codes = r.stage[...]
    r.mine[...] = jnp.where(core == 0, down, codes).astype(BF)
    r.other[...] = jnp.where(core == 0, codes, down).astype(BF)


def run_code_grad(order, ids_t, back_mine, back_other, down_sum, codes):
    half = down_sum.shape[1]
    rows = codes // half * (back_mine.shape[1] // KS)
    part = (VMEM, shape((rows, half), BF))
    made = call(
        order,
        code_grad_kernel,
        "code_grads",
        vmem_ins(ids_t=ids_t, back_mine=back_mine, back_other=back_other, down_sum=down_sum),
        dict(mine=part, other=part),
        dict(stage=pltpu.VMEM((rows, half), F32)),
    )
    return made["mine"], made["other"]


def down_kernel(r):
    taps, full, out_half = r.w_down.shape
    width = r.mine.shape[1] // 2
    code = width // taps
    copies = Copies(r.sem)
    loads = [copies.start(r.w_down.at[index], r.down_v.at[index]) for index in range(taps)]
    core = lax.axis_index(CHAN)
    total = jnp.where(core == 0, r.mine[...].astype(F32), r.got[...].astype(F32))
    sums = jnp.concatenate([total[:, :width], total[:, width:]], axis=0)
    rounded = sums.astype(BF)
    fold = (
        lax.broadcasted_iota(jnp.int32, (code, width), 0)
        == lax.broadcasted_iota(jnp.int32, (code, width), 1) % code
    ).astype(BF)
    latent = dot(r.w_latent[...], fold)
    group = lax.broadcasted_iota(jnp.int32, (out_half, width), 1) // code
    across = sums.T
    product = jnp.zeros((code, out_half), F32)
    outs = []
    for index in range(taps):
        slot = index % 4
        if index >= 4:
            copies.wait(outs[index - 4])
        spread = jnp.where(group == index, latent, 0.0).astype(BF)
        r.out_v[slot] = dot_cols(rounded, spread)
        outs.append(copies.start(r.out_v.at[slot], r.grad_down.at[index]))
        copies.wait(loads[index])
        product = product + dot(
            across[index * code : (index + 1) * code, :].astype(BF), r.down_v[index]
        )
    r.grad_latent[...] = product.T
    copies.wait_all()


def run_down(order, mine, got, w_latent, w_down):
    taps, full, out_half = w_down.shape
    made = call(
        order,
        down_kernel,
        "down_grads",
        dict(**vmem_ins(mine=mine, got=got, w_latent=w_latent), **any_ins(w_down=w_down)),
        dict(
            grad_down=(ANY, shape(w_down.shape, F32)),
            grad_latent=(VMEM, shape((out_half, w_latent.shape[1]), F32)),
        ),
        dict(
            down_v=pltpu.VMEM(w_down.shape, BF),
            out_v=pltpu.VMEM((4, full, out_half), F32),
            sem=DMA((2 * taps,)),
        ),
    )
    return made["grad_down"], made["grad_latent"]


def step_kernel(jobs, r):
    copies = Copies(r.sem) if hasattr(r, "sem") else None
    for job in jobs:
        job.load(r, copies)
    for job in jobs:
        job.run(r, copies)
    if copies is not None:
        copies.wait_all()


class Scatter:
    def __init__(self, name, kept, got, bits, large=False, unit=1, ways=1):
        self.name, self.bits, self.large, self.ways = name, bits, large, ways
        self.kept, self.got = kept, got
        self.spec = ANY if large else VMEM
        self.used = sum(array.shape[0] for array in kept)
        self.shape = (-(-self.used // unit) * unit, kept[0].shape[1])

    def ins(self):
        arrays = {f"kept{self.name}_{index}": array for index, array in enumerate(self.kept)}
        arrays.update({f"got{self.name}_{index}": array for index, array in enumerate(self.got)})
        return {name: (self.spec, array) for name, array in arrays.items()}

    def outs(self):
        part = (self.spec, shape((self.shape[0] // (2 * self.ways), self.shape[1]), BF))
        return {kind + self.name + "w" * way: part for way in range(self.ways) for kind in ("sent", "next")}

    def scratch(self):
        rooms = {"room" + self.name: pltpu.VMEM(self.shape, BF)}
        if self.large:
            rooms["other" + self.name] = pltpu.VMEM(self.shape, BF)
        return rooms

    def copies(self):
        return 2 * len(self.kept) + 2 * self.ways if self.large else 0

    def spans(self):
        start = 0
        for index, array in enumerate(self.kept):
            yield index, slice(start, start + array.shape[0])
            start += array.shape[0]

    def load(self, r, copies):
        self.loads = []
        if self.large:
            for index, rows in self.spans():
                there = pl.ds(rows.start, rows.stop - rows.start)
                for kind, room in (("kept", "room"), ("got", "other")):
                    source = getattr(r, f"{kind}{self.name}_{index}")
                    self.loads.append(copies.start(source, getattr(r, room + self.name).at[there]))

    def add(self, r, room, copies):
        for index, rows in self.spans():
            if self.large:
                copies.wait(*self.loads[2 * index : 2 * index + 2])
                kept, got = room[rows, :], getattr(r, "other" + self.name)[rows, :]
            else:
                kept = getattr(r, f"kept{self.name}_{index}")[...]
                got = getattr(r, f"got{self.name}_{index}")[...]
            room[rows, :] = (kept.astype(F32) + got.astype(F32)).astype(BF)

    def run(self, r, copies):
        room = getattr(r, "room" + self.name)
        self.add(r, room, copies)
        if room.shape[0] > self.used:
            room[self.used :, :] = jnp.zeros((room.shape[0] - self.used, room.shape[1]), BF)
        rows = room.shape[0] // (2 * self.ways)
        side = kept_side(self.bits)
        for way in range(self.ways):
            for kind, which in (("sent", 1 - side), ("next", side)):
                target = getattr(r, kind + self.name + "w" * way)
                here = pl.ds(pl.multiple_of((2 * way + which) * rows, 16), rows)
                if self.large:
                    copies.start(room.at[here], target)
                else:
                    target[...] = room[here, :]


class Reduce(Scatter):
    def outs(self):
        return {"sent" + self.name: (VMEM, shape(self.shape, BF))}

    def scratch(self):
        return {}

    def run(self, r, copies):
        self.add(r, getattr(r, "sent" + self.name), copies)


class Gather(Scatter):
    def outs(self):
        rows, columns = self.shape
        return {"sent" + self.name: (VMEM, shape((2 * rows, columns), BF))}

    def scratch(self):
        return {}

    def run(self, r, copies):
        out = getattr(r, "sent" + self.name)
        rows = out.shape[0] // 2
        side = kept_side(self.bits)
        for kind, which in (("kept", side), ("got", 1 - side)):
            here = pl.ds(pl.multiple_of(which * rows, 16), rows)
            out[here, :] = getattr(r, f"{kind}{self.name}_0")[...]


def hold_kernel(r):
    pass


def run_hold(order, arrays):
    names = [f"part{index}" for index in range(len(arrays))]
    outs = {"out" + name: (ANY, shape(array.shape, array.dtype)) for name, array in zip(names, arrays)}
    made = call(
        order, hold_kernel, "hold", any_ins(**dict(zip(names, arrays))), outs, {},
        aliases={index: index for index in range(len(arrays))}, limit=SMALL_LIMIT,
    )
    return [made["out" + name] for name in names]


class Add:
    def __init__(self, name, value, got):
        self.name, self.value, self.got = name, value, got

    def ins(self):
        return vmem_ins(**{"value" + self.name: self.value, "came" + self.name: self.got})

    def outs(self):
        return {"total" + self.name: (VMEM, shape(self.value.shape, self.value.dtype))}

    def scratch(self):
        return {}

    def copies(self):
        return 0

    def load(self, r, copies):
        pass

    def run(self, r, copies):
        total = getattr(r, "value" + self.name)[...].astype(F32) + getattr(r, "came" + self.name)[...].astype(F32)
        getattr(r, "total" + self.name)[...] = total.astype(self.value.dtype)


def run_step(order, sums):
    jobs = [one.job() for one in sums]
    ins, outs, scratch = {}, {}, {}
    for job in jobs:
        ins.update(job.ins())
        outs.update(job.outs())
        scratch.update(job.scratch())
    copies = sum(job.copies() for job in jobs)
    if copies:
        scratch["sem"] = DMA((copies,))
    made = call(
        order,
        functools.partial(step_kernel, jobs),
        "sum_step",
        ins,
        outs,
        scratch,
        limit=VMEM_LIMIT if copies else SMALL_LIMIT,
    )
    for one in sums:
        one.take(made)


def finish_kernel(pieces, kind, r):
    conv_rows = r.conv.shape[1]
    copies = Copies(r.sem)
    loads, edges = [], []
    for index, (unit, piece) in enumerate(pieces):
        there = pl.ds(piece.place, piece.rows)
        loads.append(copies.start(getattr(r, "part" + piece.name).at[there], getattr(r, f"chunk{index}")))
    for index, (unit, piece) in enumerate(pieces):
        side = kept_side(piece.bits)
        which = side if kind == "part" else 1 - side
        rows = piece.rows
        wide = getattr(r, f"wide{index}")
        copies.wait(loads[index])
        wide[...] = getattr(r, f"chunk{index}")[...].astype(F32)
        if piece.start + piece.span + rows <= conv_rows:
            there = pl.ds(pl.multiple_of(piece.start + which * piece.span, 16), rows)
            copies.start(wide, r.conv.at[unit, there])
            continue
        for choice in range(2):
            start = piece.start + choice * piece.span
            edge = min(max(conv_rows - start, 0), rows)
            parts = []
            if edge > 0:
                parts.append((wide.at[pl.ds(0, edge)], r.conv.at[unit, pl.ds(start, edge)]))
            if edge < rows:
                target = r.point.at[unit, pl.ds(start + edge - conv_rows, rows - edge)]
                parts.append((wide.at[pl.ds(edge, rows - edge)], target))
            made = [
                pltpu.make_async_copy(source, target, r.edge_sem.at[index, number])
                for number, (source, target) in enumerate(parts)
            ]
            edges.append((which == choice, made))

            @pl.when(which == choice)
            def _():
                for copy in made:
                    copy.start()

    for chosen, made in edges:

        @pl.when(chosen)
        def _():
            for copy in made:
                copy.wait()

    copies.wait_all()


def run_finish(order, pieces, kind, arrays, before, full):
    half = arrays[0].shape[1]
    ins = {}
    if before is not None:
        ins.update(any_ins(conv_in=before["conv"], point_in=before["point"]))
    ins.update(any_ins(**{f"part{index}": array for index, array in enumerate(arrays)}))
    scratch = {}
    for index, (_, piece) in enumerate(pieces):
        scratch[f"chunk{index}"] = pltpu.VMEM((piece.rows, half), BF)
        scratch[f"wide{index}"] = pltpu.VMEM((piece.rows, half), F32)
    scratch["sem"] = DMA((2 * len(pieces),))
    scratch["edge_sem"] = DMA((len(pieces), 2))
    return call(
        order,
        functools.partial(finish_kernel, pieces, kind),
        "finish",
        ins,
        dict(
            conv=(ANY, shape((3, K * full, half), F32)),
            point=(ANY, shape((3, full, half), F32)),
        ),
        scratch,
        aliases=None if before is None else {0: 0, 1: 1},
    )


def collect_kernel(r):
    half = r.mine.shape[1]
    code = r.w_expand.shape[0]
    core = lax.axis_index(CHAN)
    own, oth = both_columns(half)
    r.rate_v[...] = jnp.zeros(r.rate_v.shape, F32)
    for index in range(7):
        rate = getattr(r, f"rate{index}")
        r.rate_v[index : index + 1, :] = jnp.sum(rate[...], axis=0, keepdims=True)
    r.mine[:8, :] = r.rate_v[:, own]
    r.other[:8, :] = r.rate_v[:, oth]
    r.other[8:, :] = jnp.zeros((r.other.shape[0] - 8, half), F32)
    blocks, width = r.mixed_mine.shape
    wide = jnp.concatenate([r.w_expand[...].astype(F32)] * (width // code), axis=0).astype(BF)
    lane = lax.broadcasted_iota(jnp.int32, (blocks, width), 1)
    total = jnp.zeros((code, r.out_grad.shape[3]), F32)
    for row, mixed in ((core, r.mixed_mine), (1 - core, r.mixed_got)):
        value = mixed[...]
        once = jnp.where(lane < code, value.astype(F32), 0.0).astype(BF)
        r.block_out[row, 0] = dot(once, wide).astype(BF)
        sums = lax.dot_general(
            value, r.out_grad[row, 0], (((0,), (0,)), ((), ())), preferred_element_type=F32
        )
        total = total + sums[:code, :]
    for index in range(total.shape[1] // half):
        r.mine[8 * (index + 1) : 8 * (index + 2), :] = total[:, index * half : (index + 1) * half]


def run_collect(order, rates, mixed_mine, mixed_got, out_grad, w_expand, half):
    part = (VMEM, shape((8 + 8 * (w_expand.shape[1] // half), half), F32))
    made = call(
        order,
        collect_kernel,
        "collect",
        vmem_ins(
            **{f"rate{index}": rate for index, rate in enumerate(rates)},
            mixed_mine=mixed_mine, mixed_got=mixed_got, out_grad=out_grad, w_expand=w_expand,
        ),
        dict(block_out=(VMEM, shape(out_grad.shape, BF)), mine=part, other=part),
        dict(rate_v=pltpu.VMEM((8, 2 * half), F32)),
        limit=SMALL_LIMIT,
    )
    return made["block_out"], made["mine"], made["other"]


def place_kernel(r):
    core = lax.axis_index(CHAN)
    copies = Copies(r.sem)
    frames = r.got.shape[0]
    moved = [
        (copies.start(r.got.at[there], r.room.at[there]), there) for _, there in tiles_of(frames)
    ]
    for number, there in moved:
        copies.wait(number)
        copies.start(r.room.at[there], r.out.at[1 - core, 0, there])
    copies.wait_all()


def run_place(order, mine, got):
    return call(
        order,
        place_kernel,
        "place_rows",
        any_ins(mine=mine, got=got),
        dict(out=(ANY, shape(mine.shape, mine.dtype))),
        dict(room=pltpu.VMEM(got.shape, got.dtype), sem=DMA((2 * (got.shape[0] // TILE),))),
        aliases={0: 0},
        limit=SMALL_LIMIT,
    )["out"]


def codebook_kernel(r):
    rows, half = r.mine.shape
    code = r.codebook.shape[0]
    core = lax.axis_index(CHAN)
    sums = jnp.where(core == 0, r.got[...].astype(F32), r.mine[...].astype(F32))
    for index in range(rows // code):
        r.total[:, index * half : (index + 1) * half] = sums[index * code : (index + 1) * code, :]
    columns = r.codebook[...]
    scale = lax.rsqrt(jnp.sum(columns * columns, axis=0, keepdims=True) + 1.0)
    unit = columns * scale
    grad = r.total[...]
    r.out[...] = scale * (grad - unit * jnp.sum(unit * grad, axis=0, keepdims=True))


def run_codebook(order, mine, got, codebook):
    return call(
        order,
        codebook_kernel,
        "codebook_grads",
        vmem_ins(mine=mine, got=got, codebook=codebook),
        dict(out=(VMEM, shape(codebook.shape, F32))),
        dict(total=pltpu.VMEM(codebook.shape, F32)),
        limit=SMALL_LIMIT,
    )["out"]


def chip_axes(count):
    bits = count.bit_length() - 1
    side = bits // 3
    return list(range(side)), list(range(side, 2 * side)), list(range(2 * side, bits))


def two_orders(count):
    x, y, z = chip_axes(count)
    back = z[::-1]
    return ((x + y + z, y + x + back), (z + y + x, back + y + x))


def first_unit(count, ways):
    return ways * 8 * count


def piece_plan(full, count):
    orders = two_orders(count)
    rows = (K + 1) * full
    cut = 11 * rows // 16
    first = {2: [], 1: [], 0: []}
    later = []
    for seq, (share, start) in enumerate(((cut // 2, 0), ((rows - cut) // 2, cut))):
        bits = (orders[seq][0][0], orders[seq][1][0])
        place = 0
        for unit in (2, 1, 0):
            first[unit].append(Piece(f"{seq}", start, share, place, bits, share))
            place += share
        ways = 2 - seq
        unit_rows = first_unit(count, ways)
        place = -(-place // unit_rows) * unit_rows
        for unit in (2, 1, 0):
            lo = (2 - unit) * share
            for way in range(ways):
                at = max(lo, way * place // ways)
                stop = min(lo + share, (way + 1) * place // ways)
                if stop > at:
                    name = f"{2 * seq + way}"
                    later.append(
                        (unit, Piece(name, start + at - lo, stop - at, at - way * place // ways, bits, share))
                    )
    return first, later


def exchange(values, count, bits):
    pairs = []
    for chip in range(count):
        for core in range(2):
            pairs.append((2 * chip + core, 2 * (chip ^ (1 << bits[core])) + core))
    return lax.ppermute(values, (DP, CHAN), pairs)


def swap(values):
    return lax.ppermute(values, CHAN, [(0, 1), (1, 0)])


class FirstStep:
    def __init__(self, name, count, cores, ways):
        self.name, self.count, self.ways = name, count, ways
        self.steps = list(zip(*cores))
        self.kept = []
        self.got = []

    def begin(self, sent, kept):
        self.kept.append(kept)
        self.got.append(exchange(sent, self.count, self.steps[0]))

    def job(self):
        unit = first_unit(self.count, self.ways)
        return Scatter("f" + self.name, self.kept, self.got, self.steps[1], True, unit, self.ways)

    def take(self, made):
        self.made = [
            (f"{2 * int(self.name) + way}", made["sentf" + self.name + "w" * way], made["nextf" + self.name + "w" * way])
            for way in range(self.ways)
        ]

    def go_on(self, name, sent, kept):
        return PartSum(name, self.count, self.steps, sent, kept)


class PartSum:
    def __init__(self, name, count, steps, sent, kept):
        self.name, self.count, self.steps = name, count, steps
        self.level = 1
        self.scattering = True
        self.kept = [kept]
        self.send(sent)

    def send(self, sent):
        self.sent = sent
        self.got = [exchange(sent, self.count, self.steps[self.level])]

    def job(self):
        if not self.scattering:
            return Gather(self.name, [self.sent], self.got, self.steps[self.level])
        if self.level + 1 < len(self.steps):
            unit = 16 << (len(self.steps) - 1 - self.level)
            return Scatter(self.name, self.kept, self.got, self.steps[self.level + 1], False, unit)
        return Reduce(self.name, self.kept, self.got, None)

    def take(self, made):
        if not self.scattering:
            self.level -= 1
        elif self.level + 1 < len(self.steps):
            self.level += 1
            self.kept = [made["next" + self.name]]
        else:
            self.scattering = False
        self.send(made["sent" + self.name])

    def ready(self):
        return not self.scattering and self.level == 0


class SmallSum:
    def __init__(self, name, mine, other, count, order):
        self.name, self.count, self.order = name, count, order
        self.value = mine
        self.got = swap(other)
        self.level = 0

    def job(self):
        return Add(self.name, self.value, self.got)

    def take(self, made):
        self.value = made["total" + self.name]
        if self.level < len(self.order):
            bit = self.order[self.level]
            self.got = exchange(self.value, self.count, (bit, bit))
        self.level += 1

    def ready(self):
        return self.level > len(self.order)


def shards(
    frames_in,
    utter_lengths,
    code_ids,
    alpha_first,
    alpha_second,
    alpha_last,
    w_dilated,
    w_point,
    w_down,
    w_latent,
    w_expand,
    codebook,
    out_grad,
):
    count = lax.axis_size(DP)
    half = frames_in.shape[3]
    full = 2 * half
    codes = codebook.shape[1]
    order = Order()

    frames_got = swap(frames_in)
    p_got = swap(w_point)
    w_mine = w_dilated.reshape(3, K * full, half)
    w_got = swap(w_mine)
    alpha_rows = jnp.concatenate([alpha_first, alpha_second, alpha_last[None]], axis=0)
    place = (utter_lengths, alpha_rows, swap(alpha_rows))

    ready = run_prepare(order, w_down, w_latent, w_expand, out_grad, code_ids, codebook)
    back_got = swap(ready["back_sent"])
    made = run_forward(
        order, place, frames_in, frames_got, w_mine, w_got, w_point, p_got,
        dict(
            down_mine=ready["down_mine"], down_other=swap(ready["down_mine"]),
            chosen=ready["chosen"], back_mine=ready["back_mine"], back_other=back_got,
        ),
    )
    seen = [made[f"seen{u}"] for u in range(3)]
    rates = [None] * 5 + [made["rates"], made["last_rates"]]
    grads = [None, None, (made["mine"], swap(made["other"]), made["other"])]
    seen_got = [None, None, swap(seen[2])]
    running, dilated, grad = made["running"], made["dilated"], made["grad"]

    def open_unit(u, grad):
        made = run_opening(
            order, u, place, grads[u][0], grads[u][2], running, grad, dilated, w_mine, w_got, w_point, p_got
        )
        rates[u] = made["rates"]
        if u > 0:
            rates[2 + u] = made["mid_rates"]
            grads[u - 1] = (made["mine"], swap(made["other"]), made["other"])
        return made

    x, y, z = chip_axes(count)
    code_mine, code_sent = run_code_grad(
        order, ready["ids_t"], ready["back_mine"], back_got, made["down_sum"], codes
    )
    codes_sum = SmallSum("", code_mine, code_sent, count, z[::-1] + y + x)
    plan, later = piece_plan(full, count)
    firsts = [
        FirstStep(f"{index}", count, cores, 2 - index) for index, cores in enumerate(two_orders(count))
    ]

    def weigh(u):
        made = run_weight(
            order, u, place, seen[u], seen_got[u], grads[u][0], grads[u][1], plan[u],
            (codes_sum.value, codes_sum.got) if u > 0 else None,
        )
        if u > 0:
            codes_sum.take(made)
        for index, one in enumerate(firsts):
            one.begin(made[f"sent{index}"], made[f"kept{index}"])

    grad = open_unit(2, grad)["grad"]
    seen_got[1] = swap(seen[1])
    order.before += [seen_got[1]]
    weigh(2)
    first = [one.got[0] for one in firsts]
    grad = open_unit(1, grad)["grad"]
    seen_got[0] = swap(seen[0])
    mixed_got = swap(made["mixed"])
    order.before += first + [seen_got[0], mixed_got]
    weigh(1)
    weigh(0)
    order.before += [one.got[1] for one in firsts] + [codes_sum.got]
    last = open_unit(0, grad)
    run_step(order, firsts + [codes_sum])
    (name0, sent0, kept0), (name1, sent1, kept1) = firsts[0].made
    [(name2, sent2, kept2)] = firsts[1].made
    sums = [firsts[0].go_on(name0, sent0, kept0)]
    sent1, sent2, frames_sent = run_hold(order, [sent1, sent2, last["frames_sent"]])
    sums += [firsts[0].go_on(name1, sent1, kept1), firsts[1].go_on(name2, sent2, kept2)]

    def advance(*more):
        if not sums[0].scattering:
            order.before.append(swap(sums[0].got[0][:16]))
        run_step(order, sums[:1])
        run_step(order, sums[1:] + [one for one in more if not one.ready()])

    block_out, small_mine, small_other = run_collect(
        order, rates, made["mixed"], mixed_got, out_grad, w_expand, half
    )
    small = SmallSum("small", small_mine, small_other, count, z + y + x)
    grad_frames = run_place(order, last["frames_mine"], swap(frames_sent))
    while not (codes_sum.ready() or sums[0].ready()):
        advance(codes_sum, small)
    codes_back = swap(codes_sum.value)
    advance(small)
    grad_codebook = run_codebook(order, codes_sum.value, codes_back, codebook)
    while not sums[0].ready():
        advance(small)
    parts, gots = [one.sent for one in sums], [one.got[0] for one in sums]
    written = run_finish(order, later, "part", parts, None, full)
    soon = [(unit, piece) for unit, piece in later if piece.name == "0"]
    written = run_finish(order, soon, "got", gots[:1], written, full)
    grad_w_down, grad_w_latent = run_down(order, codes_sum.value, codes_back, w_latent, w_down)
    while not small.ready():
        run_step(order, [small])
    rest = [(unit, piece) for unit, piece in later if piece.name != "0"]
    written = run_finish(order, rest, "got", gots, written, full)
    grad_w_dilated, grad_w_point = written["conv"], written["point"]
    small = small.value
    return (
        block_out,
        grad_frames,
        small[0:3],
        small[3:6],
        small[6],
        grad_w_dilated.reshape(3, K, full, half),
        grad_w_point,
        grad_w_down,
        grad_w_latent,
        jnp.concatenate(
            [small[start : start + 8] for start in range(8, small.shape[0], 8)], axis=1
        ),
        grad_codebook,
    )


def solution(mesh):
    placed = (
        P(None, DP, None, CHAN),
        P(None, DP, None),
        P(None, DP, None),
        P(None, CHAN),
        P(None, CHAN),
        P(CHAN),
        P(None, None, None, CHAN),
        P(None, None, CHAN),
        P(None, None, CHAN),
        P(CHAN, None),
        P(None, CHAN),
        P(),
        P(None, DP, None, CHAN),
    )
    return jax.shard_map(
        shards,
        mesh=mesh,
        in_specs=placed,
        out_specs=(
            P(None, DP, None, CHAN),
            P(None, DP, None, CHAN),
            P(None, CHAN),
            P(None, CHAN),
            P(CHAN),
            P(None, None, None, CHAN),
            P(None, None, CHAN),
            P(None, None, CHAN),
            P(CHAN, None),
            P(None, CHAN),
            P(),
        ),
        check_vma=False,
    )
```

```python
import functools
import types
import jax
import jax.numpy as jnp
from jax import lax
from jax.experimental import pallas as pl
from jax.experimental.pallas import tpu as pltpu
from jax.sharding import PartitionSpec as P

DP = "dp"
CHAN = "chan"
K = 7
STRIDE = 8
KS = 16
DILATIONS = (1, 3, 9)
BF = jnp.bfloat16
F32 = jnp.float32
HALO = 32
TILE = 512
LANES = 128
SINE = (3.141592580569316, -5.1677069002071025, 2.550031640919103, -0.5980464504720939, 0.0772222489218058)
COSINE = (0.9999999534666402, -4.934792858671753, 4.058411914096722, -1.3318801607983635, 0.2196967977026182)
VMEM_LIMIT = 63 * 1024 * 1024
SMALL_LIMIT = 16 * 1024 * 1024
COST = dict(prepare=9, forward=36, code_grads=3, weight_grads=10, opening=15)
ANY = pl.BlockSpec(memory_space=pl.ANY)
SMEM = pl.BlockSpec(memory_space=pltpu.SMEM)
VMEM = pl.BlockSpec(memory_space=pltpu.VMEM)
DMA = pltpu.SemaphoreType.DMA


def shape(dims, kind):
    return jax.ShapeDtypeStruct(dims, kind)


class Order:
    def __init__(self):
        self.token = None
        self.before = []


def call(order, kernel, name, ins, outs, scratch, aliases=None, limit=VMEM_LIMIT):
    deps = ([] if order.token is None else [order.token]) + order.before
    order.before = []

    def body(*refs):
        refs = list(refs)
        named = dict(zip(ins, refs))
        refs = refs[len(ins) + len(deps) :]
        named.update(zip(outs, refs))
        refs[len(outs)][0] = jnp.int32(0)
        named.update(zip(scratch, refs[len(outs) + 1 :]))
        kernel(types.SimpleNamespace(**named))

    made = pl.pallas_call(
        body,
        out_shape=[out for _, out in outs.values()] + [shape((1,), jnp.int32)],
        in_specs=[spec for spec, _ in ins.values()] + [ANY] * len(deps),
        out_specs=[spec for spec, _ in outs.values()] + [SMEM],
        scratch_shapes=list(scratch.values()),
        input_output_aliases=aliases or {},
        compiler_params=pltpu.CompilerParams(vmem_limit_bytes=limit),
        cost_estimate=pl.CostEstimate(
            flops=COST.get(name, 0) << 30, bytes_accessed=COST.get(name, 0) * 3500000, transcendentals=0
        ),
        name=name,
    )(*[array for _, array in ins.values()], *deps)
    order.token = made[-1]
    return dict(zip(outs, made))


class Copies:
    def __init__(self, sem):
        self.sem = sem
        self.made = []
        self.done = set()

    def start(self, source, target):
        copy = pltpu.make_async_copy(source, target, self.sem.at[len(self.made)])
        copy.start()
        self.made.append(copy)
        return len(self.made) - 1

    def wait(self, *numbers):
        for number in numbers:
            if number not in self.done:
                self.done.add(number)
                self.made[number].wait()

    def wait_all(self):
        self.wait(*range(len(self.made)))


def dot(left, right):
    return jnp.dot(left, right, preferred_element_type=F32)


def dot_cols(left, right):
    return lax.dot_general(left, right, (((1,), (1,)), ((), ())), preferred_element_type=F32)


def dot_rows(left, right):
    return lax.dot_general(left, right, (((0,), (0,)), ((), ())), preferred_element_type=F32)


def poly(u, terms):
    total = terms[-1]
    for term in terms[-2::-1]:
        total = total * u + term
    return total


def half_turns(v, alpha):
    turns = v * (alpha * 0.3183098861837907)
    return turns - jnp.round(turns)


def snake(v, alpha):
    t = half_turns(v, alpha)
    u = t * t
    p = poly(u, SINE)
    return v + (u * (p * p)) * (1.0 / alpha)


def snake_slopes(v, alpha):
    t = half_turns(v, alpha)
    u = t * t
    sine = t * poly(u, SINE)
    double = 2.0 * sine * poly(u, COSINE)
    return sine * sine, double


def ends_of(lengths, row):
    ends = []
    total = 0
    for utt in range(lengths.shape[2]):
        total = total + lengths[row, 0, utt] * STRIDE
        ends.append(total)
    return ends


def put_labels(label_ref, ends, frames):
    t = lax.broadcasted_iota(jnp.int32, label_ref.shape, 0) - HALO
    label = jnp.zeros(label_ref.shape, jnp.int32)
    for end in ends:
        label = label + (t >= end).astype(jnp.int32)
    label_ref[...] = jnp.where((t < 0) | (t >= frames), -1, label)


def put_edges(padded_ref, frames):
    edge = jnp.zeros((HALO, padded_ref.shape[1]), F32)
    padded_ref[:HALO, :] = edge
    padded_ref[HALO + frames :, :] = edge


def tap(padded_ref, label_ref, row, rows, offset):
    here = HALO + row
    width = padded_ref.shape[1]
    same = label_ref[here + offset : here + offset + rows, :] == label_ref[here : here + rows, :]
    pieces = []
    for lane in range(0, width, LANES):
        piece = padded_ref[here + offset : here + offset + rows, lane : lane + LANES]
        pieces.append(jnp.where(same, piece, 0.0).astype(BF))
    return jnp.concatenate(pieces, axis=1)


def column_half(core, half):
    return pl.ds(pl.multiple_of(core * half, half), half)


def both_columns(half):
    core = lax.axis_index(CHAN)
    return column_half(core, half), column_half(1 - core, half)


def put_row(target, mine, other, index, own, oth):
    half = mine.shape[1]
    target[:, own] = jnp.broadcast_to(mine[index : index + 1, :], (8, half))
    target[:, oth] = jnp.broadcast_to(other[index : index + 1, :], (8, half))
    return target[0:1, :]


def split(values, terms):
    parts = []
    for _ in range(terms):
        part = values.astype(BF)
        parts.append(part)
        values = values - part.astype(F32)
    return parts


def row_sums(values):
    return jnp.sum(values.reshape(values.shape[0] // 8, 8, values.shape[1]), axis=0)


def tiles_of(frames):
    return [(slice(start, start + TILE), pl.ds(start, TILE)) for start in range(0, frames, TILE)]


def forward_kernel(r):
    frames, full = r.run_v.shape[1:]
    half = full // 2
    core = lax.axis_index(CHAN)
    own, oth = both_columns(half)
    copies = Copies(r.sem)
    tiles = tiles_of(frames)
    place = [
        copies.start(r.lengths, r.lengths_v),
        copies.start(r.alpha_mine, r.alpha_mv),
        copies.start(r.alpha_other, r.alpha_ov),
    ]
    loads = [copies.start(r.frames_in.at[core, 0], r.mine_v), copies.start(r.frames_got.at[core, 0], r.other_v)]

    def load_weights(unit):
        return [
            copies.start(r.w_mine.at[unit], r.w_v.at[unit % 2, 0]),
            copies.start(r.w_other.at[unit], r.w_v.at[unit % 2, 1]),
        ]

    weights = [load_weights(0)]
    points = [copies.start(r.p_mine, r.pm_v), copies.start(r.p_other, r.po_v)]
    weights.append(load_weights(1))
    small = [
        copies.start(source, target)
        for source, target in (
            (r.sent.at[pl.ds(0, full)], r.dm_v), (r.came.at[pl.ds(0, full)], r.do_v),
            (r.chosen, r.chosen_v), (r.back_mine, r.bm_v),
            (r.came.at[pl.ds(full, r.bo_v.shape[0])], r.bo_v),
        )
    ]
    put_edges(r.padded, frames)
    copies.wait(*place)
    put_labels(r.label, ends_of(r.lengths_v, core), frames)
    copies.wait(*loads)
    leaving = {(kind, slot): [] for kind in ("run", "mid", "seen") for slot in range(2)}

    def settle(kind, slot):
        copies.wait(*leaving[kind, slot])
        leaving[kind, slot] = []

    for unit in range(3):
        now, later = r.run_v.at[unit % 2], r.run_v.at[(unit + 1) % 2]
        mid = r.mid_v.at[unit % 2]
        seen = r.seen_v.at[unit % 2]
        rate_in = put_row(r.rate_v.at[unit], r.alpha_mv, r.alpha_ov, unit, own, oth)
        rate_mid = put_row(r.rate_v.at[3 + unit], r.alpha_mv, r.alpha_ov, 3 + unit, own, oth)
        settle("seen", unit % 2)
        for rows, there in tiles:
            if unit == 0:
                now[rows, own] = r.mine_v[rows, :].astype(F32)
                now[rows, oth] = r.other_v[rows, :].astype(F32)
                leaving["run", 0].append(copies.start(now.at[there], r.running.at[unit, there]))
            opened = snake(now[rows, :], rate_in)
            r.padded[HALO + rows.start : HALO + rows.stop, :] = opened
            seen[:full, rows] = opened.T.astype(BF)
        seen_out = getattr(r, f"seen{unit}")
        leaving["seen", unit % 2].append(
            copies.start(seen.at[pl.ds(0, full)], seen_out.at[pl.ds(0, full)])
        )
        copies.wait(*weights[unit])
        if unit == 0:
            copies.wait(*points)
        settle("mid", unit % 2)
        settle("run", (unit + 1) % 2)
        for place_of, (rows, there) in enumerate(tiles):
            taps = r.taps.at[place_of % 2]
            for index in range(K):
                offset = DILATIONS[unit] * (index - K // 2)
                taps[:, index * full : (index + 1) * full] = tap(
                    r.padded, r.label, rows.start, TILE, offset
                )
            mid[rows, own] = dot(taps[...], r.w_v[unit % 2, 0])
            mid[rows, oth] = dot(taps[...], r.w_v[unit % 2, 1])
            if unit < 2:
                leaving["mid", unit % 2].append(copies.start(mid.at[there], r.dilated.at[unit, there]))
            closed = snake(mid[rows, :], rate_mid)
            seen[full:, rows] = closed.T.astype(BF)
            closed = closed.astype(BF)
            later[rows, own] = now[rows, own] + dot(closed, r.pm_v[unit])
            later[rows, oth] = now[rows, oth] + dot(closed, r.po_v[unit])
            if unit < 2:
                leaving["run", (unit + 1) % 2].append(
                    copies.start(later.at[there], r.running.at[unit + 1, there])
                )
        leaving["seen", unit % 2].append(
            copies.start(seen.at[pl.ds(full, full)], seen_out.at[pl.ds(full, full)])
        )
        if unit == 0:
            weights.append(load_weights(2))

    running, mid = r.run_v.at[1], r.mid_v.at[0]
    blocks = frames // STRIDE
    value = put_row(r.rate_v.at[6], r.alpha_mv, r.alpha_ov, 6, own, oth)
    mid_value = r.rate_v[5, 0:1, :]
    inverse = 1.0 / value
    copies.wait(*small)
    width = r.dm_v.shape[1]
    code = width // KS
    lane = lax.broadcasted_iota(jnp.int32, (TILE, width), 1) // code
    step = lax.broadcasted_iota(jnp.int32, (TILE, width), 0) % STRIDE
    pattern = (lane % STRIDE == (step + STRIDE // 2) % STRIDE).astype(F32)
    down = r.dm_v[...] + r.do_v[...]
    down_parts = jnp.concatenate(split(down, 2), axis=1)
    sums = []
    for rows, _ in tiles:
        v = running[rows, :]
        square, double = snake_slopes(v, value)
        r.square_v[rows, :] = square
        r.double_v[rows, :] = double
        opened = (v + square * inverse).astype(BF)
        r.opened_v[rows, :] = opened
        products = dot(opened, down_parts)
        products = products[:, :width] + products[:, width:]
        products = (products * pattern).reshape(TILE // STRIDE, STRIDE, width)
        sums.append(jnp.sum(products, axis=1))
    sums = jnp.concatenate(sums, axis=0)
    block = lax.broadcasted_iota(jnp.int32, (blocks, width), 0)
    block_lane = lax.broadcasted_iota(jnp.int32, (blocks, width), 1)
    label = jnp.zeros((blocks, width), jnp.int32)
    for end in ends_of(r.lengths_v, core):
        label = label + (block * STRIDE >= end).astype(jnp.int32)

    def earlier(values):
        return pltpu.roll(values, 1, 0)

    def later_rows(values):
        return pltpu.roll(values, blocks - 1, 0)

    same_before = jnp.where((block > 0) & (earlier(label) == label), 1.0, 0.0)
    same_after = jnp.where((block < blocks - 1) & (later_rows(label) == label), 1.0, 0.0)
    early = block_lane < 4 * code
    late = block_lane >= 12 * code
    sums = jnp.where(
        early, same_before * earlier(sums), jnp.where(late, same_after * later_rows(sums), sums)
    )
    fold = (
        lax.broadcasted_iota(jnp.int32, (width, width), 0) % code
        == lax.broadcasted_iota(jnp.int32, (width, width), 1) % code
    ).astype(BF)
    latent = dot(jnp.concatenate(split(sums, 3), axis=1), jnp.concatenate([fold] * 3, axis=0))
    scale = lax.rsqrt(jnp.sum(latent * latent, axis=1, keepdims=True) * (1.0 / KS) + 1.0)
    unit_code = latent * scale
    r.mixed[...] = (unit_code + r.chosen_v[...]).astype(BF)
    back = r.bm_v[...] + r.bo_v[...]
    along = jnp.sum(unit_code * back, axis=1, keepdims=True) * (1.0 / KS)
    spread = (back - unit_code * along) * scale
    spread = jnp.where(
        early,
        later_rows(same_before * spread),
        jnp.where(late, earlier(same_after * spread), spread),
    )
    down_t_parts = split(down.T, 2)
    down_t_stack = jnp.concatenate([down_t_parts[0], down_t_parts[1], down_t_parts[0]], axis=0)
    total = jnp.zeros((8, full), F32)
    last_total = jnp.zeros((8, full), F32)
    down_total = jnp.zeros(down.shape, F32)
    for rows, there in tiles:
        own_blocks = spread[rows.start // STRIDE : rows.stop // STRIDE, :]
        wide = jnp.broadcast_to(
            own_blocks[:, None, :], (TILE // STRIDE, STRIDE, width)
        ).reshape(TILE, width) * pattern
        parts = split(wide, 2)
        sums = lax.dot_general(
            r.opened_v[rows, :],
            jnp.concatenate(parts, axis=1),
            (((0,), (0,)), ((), ())),
            preferred_element_type=F32,
        )
        down_total = down_total + (sums[:, :width] + sums[:, width:])
        grad_last = dot(jnp.concatenate([parts[0], parts[0], parts[1]], axis=1), down_t_stack)
        square = r.square_v[rows, :]
        double = r.double_v[rows, :]
        grad = grad_last * (1.0 + double)
        r.grad_v[rows, :] = grad
        copies.start(r.grad_v.at[there], r.grad.at[there])
        rate = grad_last * (running[rows, :] * double - square * inverse)
        last_total = last_total + row_sums(rate)
        total = total + closing_steps(
            r, rows, grad, mid[rows, :], mid_value, (own, oth), r.pm_v[2], r.po_v[2]
        )
        send_closing(r, copies, rows, there, own, oth)
    r.rates[...] = total * (1.0 / mid_value)
    r.last_rates[...] = last_total * inverse
    r.down_sum[:, :width] = down_total[:half, :].astype(BF)
    r.down_sum[:, width:] = down_total[half:, :].astype(BF)
    copies.wait_all()


def closing_steps(r, rows, point, mid, alpha, core_cols, p_mine, p_other):
    own, oth = core_cols
    r.gp_v[rows, :] = point.astype(BF)
    grad = dot_cols(r.gp_v[rows, own], p_mine) + dot_cols(r.gp_v[rows, oth], p_other)
    square, double = snake_slopes(mid, alpha)
    r.gd_v[rows, :] = (grad * (1.0 + double)).astype(BF)
    return row_sums(grad * (mid * double - square * (1.0 / alpha)))


def send_closing(r, copies, rows, there, own, oth):
    frames = r.gp_v.shape[0]
    after = pl.ds(frames + rows.start, TILE)
    copies.start(r.gp_v.at[there, own], r.mine.at[there])
    copies.start(r.gd_v.at[there, own], r.mine.at[after])
    copies.start(r.gp_v.at[there, oth], r.other.at[there])
    copies.start(r.gd_v.at[there, oth], r.other.at[after])


def place_ins(place):
    return {name: (ANY, array) for name, array in zip(("lengths", "alpha_mine", "alpha_other"), place)}


def place_rooms(place, full):
    lengths, alpha, _ = place
    return dict(
        lengths_v=pltpu.SMEM(lengths.shape, jnp.int32),
        alpha_mv=pltpu.VMEM(alpha.shape, F32),
        alpha_ov=pltpu.VMEM(alpha.shape, F32),
        rate_v=pltpu.VMEM((7, 8, full), F32),
    )


def any_ins(**arrays):
    return {name: (ANY, array) for name, array in arrays.items()}


def vmem_ins(**arrays):
    return {name: (VMEM, array) for name, array in arrays.items()}


def run_forward(order, place, frames_in, frames_got, w_mine, w_other, p_mine, p_other, small):
    frames, half = frames_in.shape[2:]
    full = 2 * half
    tiles = frames // TILE
    blocks = frames // STRIDE
    width = small["chosen"].shape[1]
    wide = (frames, full)
    pair = (ANY, shape((2 * frames, half), BF))
    square = pltpu.VMEM((blocks, width), F32)
    tall = pltpu.VMEM((full, width), F32)
    return call(
        order,
        forward_kernel,
        "forward",
        dict(
            **place_ins(place),
            **any_ins(frames_in=frames_in, frames_got=frames_got, w_mine=w_mine, w_other=w_other,
                      p_mine=p_mine, p_other=p_other, **small),
        ),
        dict(
            running=(ANY, shape((3,) + wide, F32)),
            dilated=(ANY, shape((2,) + wide, F32)),
            seen0=(ANY, shape((2 * full, frames), BF)),
            seen1=(ANY, shape((2 * full, frames), BF)),
            seen2=(ANY, shape((2 * full, frames), BF)),
            grad=(ANY, shape(wide, F32)),
            mixed=(VMEM, shape((blocks, width), BF)),
            down_sum=(VMEM, shape((half, 2 * width), BF)),
            last_rates=(VMEM, shape((8, full), F32)),
            mine=pair,
            other=pair,
            rates=(VMEM, shape((8, full), F32)),
        ),
        dict(
            **place_rooms(place, full),
            mine_v=pltpu.VMEM((frames, half), BF),
            other_v=pltpu.VMEM((frames, half), BF),
            run_v=pltpu.VMEM((2,) + wide, F32),
            mid_v=pltpu.VMEM((2,) + wide, F32),
            seen_v=pltpu.VMEM((2, 2 * full, frames), BF),
            padded=pltpu.VMEM((frames + 2 * HALO, full), F32),
            label=pltpu.VMEM((frames + 2 * HALO, LANES), jnp.int32),
            taps=pltpu.VMEM((2, TILE, K * full), BF),
            w_v=pltpu.VMEM((2, 2) + w_mine.shape[1:], BF),
            pm_v=pltpu.VMEM(p_mine.shape, BF),
            po_v=pltpu.VMEM(p_mine.shape, BF),
            dm_v=tall, do_v=tall, chosen_v=square, bm_v=square, bo_v=square,
            opened_v=pltpu.VMEM(wide, BF),
            square_v=pltpu.VMEM(wide, F32),
            double_v=pltpu.VMEM(wide, F32),
            grad_v=pltpu.VMEM(wide, F32),
            gp_v=pltpu.VMEM(wide, BF),
            gd_v=pltpu.VMEM(wide, BF),
            sem=DMA((3 + 2 + 6 + 2 + 5 + 5 * tiles + 6 + 5 * tiles,)),
        ),
    )


def weight_kernel(unit, pieces, r):
    frames = r.padded.shape[1] - 2 * HALO
    half = r.padded.shape[2]
    full = 2 * half
    core = lax.axis_index(CHAN)
    copies = Copies(r.sem)
    place = copies.start(r.lengths, r.lengths_v)
    grads = []
    for row, source in enumerate((r.grads_mine, r.grads_got)):
        grads.append(copies.start(source.at[pl.ds(frames, frames)], r.gd_v.at[row]))
    opened = []
    for row, source in enumerate((r.seen_mine, r.seen_got)):
        columns = pl.ds(row * frames, frames)
        opened.append(copies.start(source.at[pl.ds(0, full)], r.seen_v.at[pl.ds(0, full), columns]))
    points = []
    for row, (source, seen) in enumerate(((r.grads_mine, r.seen_mine), (r.grads_got, r.seen_got))):
        columns = pl.ds(row * frames, frames)
        points.append(copies.start(source.at[pl.ds(0, frames)], r.gp_v.at[columns]))
        points.append(copies.start(seen.at[pl.ds(full, full)], r.seen_v.at[pl.ds(full, full), columns]))
    if hasattr(r, "value"):
        beside = [copies.start(r.value, r.value_v), copies.start(r.came, r.came_v)]
    for row in range(2):
        put_edges(r.padded.at[row], frames)
    copies.wait(place)
    for row in range(2):
        put_labels(r.label.at[row], ends_of(r.lengths_v, core if row == 0 else 1 - core), frames)
    for row in range(2):
        copies.wait(grads[row])
        r.padded[row, HALO : HALO + frames, :] = r.gd_v[row].astype(F32)
    copies.wait(*opened)
    waiting = list(pieces)

    def send_pieces(rows):
        for piece in [piece for piece in waiting if piece.start + 2 * piece.rows <= rows]:
            waiting.remove(piece)
            side = kept_side(piece.bits)
            for kind, which in (("sent", 1 - side), ("kept", side)):
                here = pl.ds(pl.multiple_of(piece.start + which * piece.rows, 16), piece.rows)
                copies.start(r.out_v.at[here], getattr(r, kind + piece.name))

    for index in range(K):
        offset = -DILATIONS[unit] * (index - K // 2)
        taps = r.taps.at[index % 2]
        for row in range(2):
            for start in range(0, frames, TILE):
                taps[row * frames + start : row * frames + start + TILE, :] = tap(
                    r.padded.at[row], r.label.at[row], start, TILE, offset
                )
        r.out_v[index * full : (index + 1) * full, :] = dot(r.seen_v[:full, :], taps[...]).astype(BF)
        send_pieces((index + 1) * full)
    if hasattr(r, "value"):
        copies.wait(*beside)
        total = r.value_v[...].astype(F32) + r.came_v[...].astype(F32)
        r.value_v[...] = total.astype(BF)
        copies.start(r.value_v, r.total)
    copies.wait(*points)
    r.out_v[K * full : (K + 1) * full, :] = dot(r.seen_v[full:, :], r.gp_v[...]).astype(BF)
    send_pieces((K + 1) * full)
    copies.wait_all()


def kept_side(bits):
    bit = jnp.where(lax.axis_index(CHAN) == 0, bits[0], bits[1])
    return lax.shift_right_logical(lax.axis_index(DP), bit) & 1


class Piece:
    def __init__(self, name, start, rows, place, bits, span):
        self.name, self.start, self.rows, self.place, self.bits, self.span = name, start, rows, place, bits, span


def run_weight(order, unit, place, seen_mine, seen_got, grads_mine, grads_got, pieces, beside=None):
    frames, half = grads_mine.shape[0] // 2, grads_mine.shape[1]
    full = 2 * half
    ins = any_ins(lengths=place[0], seen_mine=seen_mine, seen_got=seen_got,
                  grads_mine=grads_mine, grads_got=grads_got)
    scratch = dict(
        lengths_v=pltpu.SMEM(place[0].shape, jnp.int32),
        seen_v=pltpu.VMEM((2 * full, 2 * frames), BF),
        gd_v=pltpu.VMEM((2, frames, half), BF),
        gp_v=pltpu.VMEM((2 * frames, half), BF),
        padded=pltpu.VMEM((2, frames + 2 * HALO, half), F32),
        label=pltpu.VMEM((2, frames + 2 * HALO, LANES), jnp.int32),
        taps=pltpu.VMEM((2, 2 * frames, half), BF),
        out_v=pltpu.VMEM(((K + 1) * full, half), BF),
        sem=DMA((12 + 2 * len(pieces),)),
    )
    outs = {
        kind + piece.name: (ANY, shape((piece.rows, half), BF))
        for piece in pieces
        for kind in ("sent", "kept")
    }
    if beside is not None:
        value, came = beside
        ins.update(any_ins(value=value, came=came))
        outs["total"] = (ANY, shape(value.shape, BF))
        scratch.update(value_v=pltpu.VMEM(value.shape, BF), came_v=pltpu.VMEM(value.shape, BF))
    return call(
        order, functools.partial(weight_kernel, unit, pieces), "weight_grads", ins, outs, scratch
    )


def opening_kernel(unit, r):
    last = unit == 0
    frames, full = r.running_v.shape
    half = full // 2
    core = lax.axis_index(CHAN)
    own, oth = both_columns(half)
    copies = Copies(r.sem)
    tiles = tiles_of(frames)
    place = [
        copies.start(r.lengths, r.lengths_v),
        copies.start(r.alpha_mine, r.alpha_mv),
        copies.start(r.alpha_other, r.alpha_ov),
    ]
    after = pl.ds(frames, frames)
    grads = [
        copies.start(r.grads_mine.at[after], r.gm_v),
        copies.start(r.grads_other.at[after], r.go_v),
    ]
    weights = [
        copies.start(r.w_mine.at[unit], r.w_v.at[0]),
        copies.start(r.w_other.at[unit], r.w_v.at[1]),
    ]
    if not last:
        points = [
            copies.start(r.p_mine.at[unit - 1], r.pm_v),
            copies.start(r.p_other.at[unit - 1], r.po_v),
        ]
    loads = []
    for _, there in tiles:
        loads.append([
            copies.start(r.running.at[unit, there], r.running_v.at[there]),
            copies.start(r.grad_in.at[there], r.grad_v.at[there]),
        ])
        if not last:
            loads[-1].append(copies.start(r.dilated.at[unit - 1, there], r.mid_v.at[there]))
    for part in range(2):
        put_edges(r.padded.at[part], frames)
    copies.wait(*place)
    put_labels(r.label, ends_of(r.lengths_v, core), frames)
    value = put_row(r.rate_v.at[0], r.alpha_mv, r.alpha_ov, unit, own, oth)
    if not last:
        mid_value = put_row(r.rate_v.at[1], r.alpha_mv, r.alpha_ov, 2 + unit, own, oth)
    for part, values in ((0, r.gm_v), (1, r.go_v)):
        copies.wait(grads[part])
        r.padded[part, HALO : HALO + frames, :] = values[...].astype(F32)
    copies.wait(*weights)
    for part in range(2):
        for index in range(K):
            r.turned_v[(2 * index + part) * half : (2 * index + part + 1) * half, :] = r.w_v[
                part, index * full : (index + 1) * full, :
            ].T
    if not last:
        copies.wait(*points)
    total = jnp.zeros((8, full), F32)
    mid_total = jnp.zeros((8, full), F32)
    for place_of, (rows, there) in enumerate(tiles):
        taps = r.taps.at[place_of % 2]
        for index in range(K):
            offset = -DILATIONS[unit] * (index - K // 2)
            for part in range(2):
                start = (2 * index + part) * half
                taps[:, start : start + half] = tap(
                    r.padded.at[part], r.label, rows.start, TILE, offset
                )
        opened = dot(taps[...], r.turned_v[...])
        copies.wait(*loads[place_of])
        v = r.running_v[rows, :]
        square, double = snake_slopes(v, value)
        grad = r.grad_v[rows, :] + opened * (1.0 + double)
        r.grad_v[rows, :] = grad
        total = total + row_sums(opened * (v * double - square * (1.0 / value)))
        if last:
            copies.start(r.grad_v.at[there, own], r.frames_mine.at[core, 0, there])
            copies.start(r.grad_v.at[there, oth], r.frames_sent.at[there])
        else:
            copies.start(r.grad_v.at[there], r.grad.at[there])
            mid_total = mid_total + closing_steps(
                r, rows, grad, r.mid_v[rows, :], mid_value, (own, oth), r.pm_v[...], r.po_v[...]
            )
            send_closing(r, copies, rows, there, own, oth)
    r.rates[...] = total * (1.0 / value)
    if not last:
        r.mid_rates[...] = mid_total * (1.0 / mid_value)
    copies.wait_all()


def run_opening(order, unit, place, grads_mine, grads_other, running, grad, dilated, w_mine, w_other, p_mine, p_other):
    frames, full = grad.shape
    half = full // 2
    tiles = frames // TILE
    last = unit == 0
    wide = pltpu.VMEM((frames, full), F32)
    narrow = pltpu.VMEM((frames, full), BF)
    part = pltpu.VMEM((frames, half), BF)
    point = pltpu.VMEM(p_mine.shape[1:], BF)
    pair = (ANY, shape((2 * frames, half), BF))
    rates = (VMEM, shape((8, full), F32))
    ins = dict(
        **place_ins(place),
        **any_ins(grads_mine=grads_mine, grads_other=grads_other, running=running, grad_in=grad,
                  w_mine=w_mine, w_other=w_other),
    )
    outs = dict(rates=rates)
    scratch = dict(
        **place_rooms(place, full),
        gm_v=part, go_v=part,
        padded=pltpu.VMEM((2, frames + 2 * HALO, half), F32),
        label=pltpu.VMEM((frames + 2 * HALO, LANES), jnp.int32),
        running_v=wide, grad_v=wide,
        w_v=pltpu.VMEM((2,) + w_mine.shape[1:], BF),
        turned_v=pltpu.VMEM((K * full, full), BF),
        taps=pltpu.VMEM((2, TILE, K * full), BF),
    )
    if last:
        outs["frames_mine"] = (ANY, shape((2, 1, frames, half), F32))
        outs["frames_sent"] = (ANY, shape((frames, half), F32))
    else:
        ins.update(any_ins(dilated=dilated, p_mine=p_mine, p_other=p_other))
        outs.update(grad=(ANY, shape((frames, full), F32)), mine=pair, other=pair, mid_rates=rates)
        scratch.update(mid_v=wide, pm_v=point, po_v=point, gp_v=narrow, gd_v=narrow)
    scratch["sem"] = DMA((3 + 2 + 2 + 2 + 8 * tiles,))
    return call(
        order, functools.partial(opening_kernel, unit), "opening", ins, outs, scratch
    )


def prepare_kernel(r):
    taps, full, out_half = r.w_down.shape
    code, codes = r.codebook.shape
    blocks = r.ids.shape[2]
    width = taps * code
    core = lax.axis_index(CHAN)
    copies = Copies(r.sem)
    first = [copies.start(r.ids.at[core], r.ids_v), copies.start(r.codebook, r.book_v)]
    loads = [copies.start(r.w_down.at[index], r.down_v.at[index]) for index in range(taps)]
    copies.wait(*first)
    mark = r.ids_v[...]
    total = jnp.zeros((3 * code, blocks), F32)
    step = 1024
    for start in range(0, codes, step):
        columns = r.book_v[:, start : start + step]
        unit = columns * lax.rsqrt(jnp.sum(columns * columns, axis=0, keepdims=True) + 1.0)
        parts = jnp.concatenate([part.astype(F32) for part in split(unit, 3)], axis=0).astype(BF)
        number = lax.broadcasted_iota(jnp.int32, (step, blocks), 0) + start
        total = total + dot(parts, jnp.where(number == mark, 1.0, 0.0).astype(BF))
    picked = total[:code] + total[code : 2 * code] + total[2 * code :]
    r.chosen[...] = jnp.concatenate([picked] * taps, axis=0).T
    r.ids_t[...] = jnp.broadcast_to(mark.astype(F32), (blocks, blocks)).T
    expand = jnp.concatenate([r.w_expand[...].astype(F32)] * taps, axis=0).astype(BF)
    r.back_mine[...] = dot_cols(r.out_grad[core, 0], expand)
    r.sent[full:, :] = dot_cols(r.out_grad[1 - core, 0], expand)
    fold = (
        lax.broadcasted_iota(jnp.int32, (code, width), 0)
        == lax.broadcasted_iota(jnp.int32, (code, width), 1) % code
    ).astype(BF)
    latent = dot_rows(r.w_latent[...], fold)
    group = lax.broadcasted_iota(jnp.int32, (out_half, width), 1) // code
    product = jnp.zeros((full, width), F32)
    for index in range(taps):
        copies.wait(loads[index])
        product = product + dot(r.down_v[index], jnp.where(group == index, latent, 0.0).astype(BF))
    r.sent[:full, :] = product


def run_prepare(order, w_down, w_latent, w_expand, out_grad, ids, codebook):
    taps, full, _ = w_down.shape
    width = taps * codebook.shape[0]
    blocks = ids.shape[2]
    square = (VMEM, shape((blocks, width), F32))
    return call(
        order,
        prepare_kernel,
        "prepare",
        dict(
            **any_ins(w_down=w_down, ids=ids, codebook=codebook),
            **vmem_ins(w_latent=w_latent, w_expand=w_expand, out_grad=out_grad),
        ),
        dict(
            sent=(VMEM, shape((full + blocks, width), F32)),
            chosen=square, back_mine=square,
            ids_t=(VMEM, shape((blocks, blocks), F32)),
        ),
        dict(
            down_v=pltpu.VMEM(w_down.shape, BF),
            book_v=pltpu.VMEM(codebook.shape, F32),
            ids_v=pltpu.VMEM(ids.shape[1:], jnp.int32),
            sem=DMA((taps + 2,)),
        ),
    )


def code_grad_kernel(r):
    blocks, width = r.back_mine.shape
    rows, half = r.mine.shape
    code = width // KS
    core = lax.axis_index(CHAN)
    came = r.came.shape[0] - blocks
    back = (r.back_mine[...] + r.came[came:, :]).T[:code, :]
    parts = jnp.concatenate([part.astype(F32) for part in split(back, 3)], axis=0).astype(BF)
    for index in range(rows // code):
        pieces = []
        for lane in range(0, half, blocks):
            number = lax.broadcasted_iota(jnp.int32, (blocks, blocks), 1) + (index * half + lane)
            pieces.append(jnp.where(r.ids_t[...] == number.astype(F32), 1.0, 0.0).astype(BF))
        sums = dot(parts, jnp.concatenate(pieces, axis=1))
        r.stage[index * code : (index + 1) * code, :] = (
            sums[:code] + sums[code : 2 * code] + sums[2 * code :]
        )
    down = r.down_sum[...].astype(F32)
    codes = r.stage[...]
    r.mine[...] = jnp.where(core == 0, down, codes).astype(BF)
    r.other[...] = jnp.where(core == 0, codes, down).astype(BF)


def run_code_grad(order, ids_t, back_mine, came, down_sum, codes):
    half = down_sum.shape[1]
    rows = codes // half * (back_mine.shape[1] // KS)
    part = (VMEM, shape((rows, half), BF))
    made = call(
        order,
        code_grad_kernel,
        "code_grads",
        vmem_ins(ids_t=ids_t, back_mine=back_mine, came=came, down_sum=down_sum),
        dict(mine=part, other=part),
        dict(stage=pltpu.VMEM((rows, half), F32)),
    )
    return made["mine"], made["other"]


def down_kernel(r):
    taps, full, out_half = r.w_down.shape
    width = r.mine.shape[1] // 2
    code = width // taps
    copies = Copies(r.sem)
    loads = [copies.start(r.w_down.at[index], r.down_v.at[index]) for index in range(taps)]
    core = lax.axis_index(CHAN)
    total = jnp.where(core == 0, r.mine[...].astype(F32), r.got[...].astype(F32))
    sums = jnp.concatenate([total[:, :width], total[:, width:]], axis=0)
    rounded = sums.astype(BF)
    fold = (
        lax.broadcasted_iota(jnp.int32, (code, width), 0)
        == lax.broadcasted_iota(jnp.int32, (code, width), 1) % code
    ).astype(BF)
    latent = dot_rows(r.w_latent[...], fold)
    group = lax.broadcasted_iota(jnp.int32, (out_half, width), 1) // code
    across = sums.T
    product = jnp.zeros((code, out_half), F32)
    outs = []
    for index in range(taps):
        slot = index % 4
        if index >= 4:
            copies.wait(outs[index - 4])
        spread = jnp.where(group == index, latent, 0.0).astype(BF)
        r.out_v[slot] = dot_cols(rounded, spread)
        outs.append(copies.start(r.out_v.at[slot], r.grad_down.at[index]))
        copies.wait(loads[index])
        product = product + dot(
            across[index * code : (index + 1) * code, :].astype(BF), r.down_v[index]
        )
    r.grad_latent[...] = product
    copies.wait_all()


def run_down(order, mine, got, w_latent, w_down):
    taps, full, out_half = w_down.shape
    made = call(
        order,
        down_kernel,
        "down_grads",
        dict(**vmem_ins(mine=mine, got=got, w_latent=w_latent), **any_ins(w_down=w_down)),
        dict(
            grad_down=(ANY, shape(w_down.shape, F32)),
            grad_latent=(VMEM, shape(w_latent.shape, F32)),
        ),
        dict(
            down_v=pltpu.VMEM(w_down.shape, BF),
            out_v=pltpu.VMEM((4, full, out_half), F32),
            sem=DMA((2 * taps,)),
        ),
    )
    return made["grad_down"], made["grad_latent"]


def step_kernel(jobs, r):
    copies = Copies(r.sem) if hasattr(r, "sem") else None
    for job in jobs:
        job.load(r, copies)
    for job in jobs:
        job.run(r, copies)
    if copies is not None:
        copies.wait_all()


class Scatter:
    def __init__(self, name, kept, got, bits, large=False, unit=1, ways=1):
        self.name, self.bits, self.large, self.ways = name, bits, large, ways
        self.kept, self.got = kept, got
        self.spec = ANY if large else VMEM
        self.used = sum(array.shape[0] for array in kept)
        self.shape = (-(-self.used // unit) * unit, kept[0].shape[1])

    def ins(self):
        arrays = {f"kept{self.name}_{index}": array for index, array in enumerate(self.kept)}
        arrays.update({f"got{self.name}_{index}": array for index, array in enumerate(self.got)})
        return {name: (self.spec, array) for name, array in arrays.items()}

    def outs(self):
        part = (self.spec, shape((self.shape[0] // (2 * self.ways), self.shape[1]), BF))
        return {kind + self.name + "w" * way: part for way in range(self.ways) for kind in ("sent", "next")}

    def scratch(self):
        rooms = {"room" + self.name: pltpu.VMEM(self.shape, BF)}
        if self.large:
            rooms["other" + self.name] = pltpu.VMEM(self.shape, BF)
        return rooms

    def copies(self):
        return 2 * len(self.kept) + 2 * self.ways if self.large else 0

    def spans(self):
        start = 0
        for index, array in enumerate(self.kept):
            yield index, slice(start, start + array.shape[0])
            start += array.shape[0]

    def load(self, r, copies):
        self.loads = []
        if self.large:
            for index, rows in self.spans():
                there = pl.ds(rows.start, rows.stop - rows.start)
                for kind, room in (("kept", "room"), ("got", "other")):
                    source = getattr(r, f"{kind}{self.name}_{index}")
                    self.loads.append(copies.start(source, getattr(r, room + self.name).at[there]))

    def add(self, r, room, copies):
        for index, rows in self.spans():
            if self.large:
                copies.wait(*self.loads[2 * index : 2 * index + 2])
                kept, got = room[rows, :], getattr(r, "other" + self.name)[rows, :]
            else:
                kept = getattr(r, f"kept{self.name}_{index}")[...]
                got = getattr(r, f"got{self.name}_{index}")[...]
            room[rows, :] = (kept.astype(F32) + got.astype(F32)).astype(BF)

    def run(self, r, copies):
        room = getattr(r, "room" + self.name)
        self.add(r, room, copies)
        if room.shape[0] > self.used:
            room[self.used :, :] = jnp.zeros((room.shape[0] - self.used, room.shape[1]), BF)
        rows = room.shape[0] // (2 * self.ways)
        side = kept_side(self.bits)
        for way in range(self.ways):
            for kind, which in (("sent", 1 - side), ("next", side)):
                target = getattr(r, kind + self.name + "w" * way)
                here = pl.ds(pl.multiple_of((2 * way + which) * rows, 16), rows)
                if self.large:
                    copies.start(room.at[here], target)
                else:
                    target[...] = room[here, :]


class Reduce(Scatter):
    def outs(self):
        return {"sent" + self.name: (VMEM, shape(self.shape, BF))}

    def scratch(self):
        return {}

    def run(self, r, copies):
        self.add(r, getattr(r, "sent" + self.name), copies)


class Gather(Scatter):
    def outs(self):
        rows, columns = self.shape
        return {"sent" + self.name: (VMEM, shape((2 * rows, columns), BF))}

    def scratch(self):
        return {}

    def run(self, r, copies):
        out = getattr(r, "sent" + self.name)
        rows = out.shape[0] // 2
        side = kept_side(self.bits)
        for kind, which in (("kept", side), ("got", 1 - side)):
            here = pl.ds(pl.multiple_of(which * rows, 16), rows)
            out[here, :] = getattr(r, f"{kind}{self.name}_0")[...]


def hold_kernel(r):
    pass


def run_hold(order, arrays):
    names = [f"part{index}" for index in range(len(arrays))]
    outs = {"out" + name: (ANY, shape(array.shape, array.dtype)) for name, array in zip(names, arrays)}
    made = call(
        order, hold_kernel, "hold", any_ins(**dict(zip(names, arrays))), outs, {},
        aliases={index: index for index in range(len(arrays))},
    )
    return [made["out" + name] for name in names]


class Add:
    def __init__(self, name, value, got):
        self.name, self.value, self.got = name, value, got

    def ins(self):
        return vmem_ins(**{"value" + self.name: self.value, "came" + self.name: self.got})

    def outs(self):
        return {"total" + self.name: (VMEM, shape(self.value.shape, self.value.dtype))}

    def scratch(self):
        return {}

    def copies(self):
        return 0

    def load(self, r, copies):
        pass

    def run(self, r, copies):
        total = getattr(r, "value" + self.name)[...].astype(F32) + getattr(r, "came" + self.name)[...].astype(F32)
        getattr(r, "total" + self.name)[...] = total.astype(self.value.dtype)


def run_step(order, sums):
    jobs = [one.job() for one in sums]
    ins, outs, scratch = {}, {}, {}
    for job in jobs:
        ins.update(job.ins())
        outs.update(job.outs())
        scratch.update(job.scratch())
    copies = sum(job.copies() for job in jobs)
    if copies:
        scratch["sem"] = DMA((copies,))
    made = call(
        order,
        functools.partial(step_kernel, jobs),
        "sum_step",
        ins,
        outs,
        scratch,
        limit=VMEM_LIMIT if copies else SMALL_LIMIT,
    )
    for one in sums:
        one.take(made)


def finish_kernel(pieces, kind, r):
    conv_rows = r.conv.shape[1]
    copies = Copies(r.sem)
    loads, edges = [], []
    for index, (unit, piece) in enumerate(pieces):
        there = pl.ds(piece.place, piece.rows)
        loads.append(copies.start(getattr(r, "part" + piece.name).at[there], getattr(r, f"chunk{index}")))
    for index, (unit, piece) in enumerate(pieces):
        side = kept_side(piece.bits)
        which = side if kind == "part" else 1 - side
        rows = piece.rows
        wide = getattr(r, f"wide{index}")
        copies.wait(loads[index])
        wide[...] = getattr(r, f"chunk{index}")[...].astype(F32)
        if piece.start + piece.span + rows <= conv_rows:
            there = pl.ds(pl.multiple_of(piece.start + which * piece.span, 16), rows)
            copies.start(wide, r.conv.at[unit, there])
            continue
        for choice in range(2):
            start = piece.start + choice * piece.span
            edge = min(max(conv_rows - start, 0), rows)
            parts = []
            if edge > 0:
                parts.append((wide.at[pl.ds(0, edge)], r.conv.at[unit, pl.ds(start, edge)]))
            if edge < rows:
                target = r.point.at[unit, pl.ds(start + edge - conv_rows, rows - edge)]
                parts.append((wide.at[pl.ds(edge, rows - edge)], target))
            made = [
                pltpu.make_async_copy(source, target, r.edge_sem.at[index, number])
                for number, (source, target) in enumerate(parts)
            ]
            edges.append((which == choice, made))

            @pl.when(which == choice)
            def _():
                for copy in made:
                    copy.start()

    for chosen, made in edges:

        @pl.when(chosen)
        def _():
            for copy in made:
                copy.wait()

    copies.wait_all()


def run_finish(order, pieces, kind, arrays, before, full):
    half = arrays[0].shape[1]
    ins = {}
    if before is not None:
        ins.update(any_ins(conv_in=before["conv"], point_in=before["point"]))
    ins.update(any_ins(**{f"part{index}": array for index, array in enumerate(arrays)}))
    scratch = {}
    for index, (_, piece) in enumerate(pieces):
        scratch[f"chunk{index}"] = pltpu.VMEM((piece.rows, half), BF)
        scratch[f"wide{index}"] = pltpu.VMEM((piece.rows, half), F32)
    scratch["sem"] = DMA((2 * len(pieces),))
    scratch["edge_sem"] = DMA((len(pieces), 2))
    return call(
        order,
        functools.partial(finish_kernel, pieces, kind),
        "finish",
        ins,
        dict(
            conv=(ANY, shape((3, K * full, half), F32)),
            point=(ANY, shape((3, full, half), F32)),
        ),
        scratch,
        aliases=None if before is None else {0: 0, 1: 1},
    )


def collect_kernel(r):
    half = r.mine.shape[1]
    code = r.w_expand.shape[0]
    core = lax.axis_index(CHAN)
    own, oth = both_columns(half)
    r.rate_v[...] = jnp.zeros(r.rate_v.shape, F32)
    for index in range(7):
        rate = getattr(r, f"rate{index}")
        r.rate_v[index : index + 1, :] = jnp.sum(rate[...], axis=0, keepdims=True)
    r.mine[:8, :] = r.rate_v[:, own]
    r.other[:8, :] = r.rate_v[:, oth]
    r.other[8:, :] = jnp.zeros((r.other.shape[0] - 8, half), F32)
    blocks, width = r.mixed_mine.shape
    wide = jnp.concatenate([r.w_expand[...].astype(F32)] * (width // code), axis=0).astype(BF)
    lane = lax.broadcasted_iota(jnp.int32, (blocks, width), 1)
    total = jnp.zeros((code, r.out_grad.shape[3]), F32)
    for row, mixed in ((core, r.mixed_mine), (1 - core, r.mixed_got)):
        value = mixed[...]
        once = jnp.where(lane < code, value.astype(F32), 0.0).astype(BF)
        r.block_out[row, 0] = dot(once, wide).astype(BF)
        sums = lax.dot_general(
            value, r.out_grad[row, 0], (((0,), (0,)), ((), ())), preferred_element_type=F32
        )
        total = total + sums[:code, :]
    for index in range(total.shape[1] // half):
        r.mine[8 * (index + 1) : 8 * (index + 2), :] = total[:, index * half : (index + 1) * half]


def run_collect(order, rates, mixed_mine, mixed_got, out_grad, w_expand, half):
    part = (VMEM, shape((8 + 8 * (w_expand.shape[1] // half), half), F32))
    made = call(
        order,
        collect_kernel,
        "collect",
        vmem_ins(
            **{f"rate{index}": rate for index, rate in enumerate(rates)},
            mixed_mine=mixed_mine, mixed_got=mixed_got, out_grad=out_grad, w_expand=w_expand,
        ),
        dict(block_out=(VMEM, shape(out_grad.shape, BF)), mine=part, other=part),
        dict(rate_v=pltpu.VMEM((8, 2 * half), F32)),
        limit=SMALL_LIMIT,
    )
    return made["block_out"], made["mine"], made["other"]


def place_kernel(r):
    core = lax.axis_index(CHAN)
    copies = Copies(r.sem)
    frames = r.got.shape[0]
    moved = [
        (copies.start(r.got.at[there], r.room.at[there]), there) for _, there in tiles_of(frames)
    ]
    for number, there in moved:
        copies.wait(number)
        copies.start(r.room.at[there], r.out.at[1 - core, 0, there])
    copies.wait_all()


def run_place(order, mine, got):
    return call(
        order,
        place_kernel,
        "place_rows",
        any_ins(mine=mine, got=got),
        dict(out=(ANY, shape(mine.shape, mine.dtype))),
        dict(room=pltpu.VMEM(got.shape, got.dtype), sem=DMA((2 * (got.shape[0] // TILE),))),
        aliases={0: 0},
        limit=SMALL_LIMIT,
    )["out"]


def codebook_kernel(r):
    rows, half = r.mine.shape
    code = r.codebook.shape[0]
    core = lax.axis_index(CHAN)
    sums = jnp.where(core == 0, r.got[...].astype(F32), r.mine[...].astype(F32))
    for index in range(rows // code):
        r.total[:, index * half : (index + 1) * half] = sums[index * code : (index + 1) * code, :]
    columns = r.codebook[...]
    scale = lax.rsqrt(jnp.sum(columns * columns, axis=0, keepdims=True) + 1.0)
    unit = columns * scale
    grad = r.total[...]
    r.out[...] = scale * (grad - unit * jnp.sum(unit * grad, axis=0, keepdims=True))


def run_codebook(order, mine, got, codebook):
    return call(
        order,
        codebook_kernel,
        "codebook_grads",
        vmem_ins(mine=mine, got=got, codebook=codebook),
        dict(out=(VMEM, shape(codebook.shape, F32))),
        dict(total=pltpu.VMEM(codebook.shape, F32)),
        limit=SMALL_LIMIT,
    )["out"]


def chip_axes(count):
    bits = count.bit_length() - 1
    side = bits // 3
    return list(range(side)), list(range(side, 2 * side)), list(range(2 * side, bits))


def two_orders(count):
    x, y, z = chip_axes(count)
    back = z[::-1]
    return ((x + y + z, y + x + back), (z + y + x, back + y + x))


def first_unit(count, ways):
    return ways * 8 * count


def piece_plan(full, count):
    orders = two_orders(count)
    rows = (K + 1) * full
    cut = 3 * rows // 4
    first = {2: [], 1: [], 0: []}
    later = []
    for seq, (share, start) in enumerate(((cut // 2, 0), ((rows - cut) // 2, cut))):
        bits = (orders[seq][0][0], orders[seq][1][0])
        place = 0
        for unit in (2, 1, 0):
            first[unit].append(Piece(f"{seq}", start, share, place, bits, share))
            place += share
        ways = 2 - seq
        unit_rows = first_unit(count, ways)
        place = -(-place // unit_rows) * unit_rows
        for unit in (2, 1, 0):
            lo = (2 - unit) * share
            for way in range(ways):
                at = max(lo, way * place // ways)
                stop = min(lo + share, (way + 1) * place // ways)
                if stop > at:
                    name = f"{2 * seq + way}"
                    later.append(
                        (unit, Piece(name, start + at - lo, stop - at, at - way * place // ways, bits, share))
                    )
    return first, later


def exchange(values, count, bits):
    pairs = []
    for chip in range(count):
        for core in range(2):
            pairs.append((2 * chip + core, 2 * (chip ^ (1 << bits[core])) + core))
    return lax.ppermute(values, (DP, CHAN), pairs)


def swap(values):
    return lax.ppermute(values, CHAN, [(0, 1), (1, 0)])


class FirstStep:
    def __init__(self, name, count, cores, ways):
        self.name, self.count, self.ways = name, count, ways
        self.steps = list(zip(*cores))
        self.kept = []
        self.got = []

    def begin(self, sent, kept):
        self.kept.append(kept)
        self.got.append(exchange(sent, self.count, self.steps[0]))

    def job(self):
        unit = first_unit(self.count, self.ways)
        return Scatter("f" + self.name, self.kept, self.got, self.steps[1], True, unit, self.ways)

    def take(self, made):
        self.made = [
            (f"{2 * int(self.name) + way}", made["sentf" + self.name + "w" * way], made["nextf" + self.name + "w" * way])
            for way in range(self.ways)
        ]

    def go_on(self, name, sent, kept):
        return PartSum(name, self.count, self.steps, sent, kept)


class PartSum:
    def __init__(self, name, count, steps, sent, kept):
        self.name, self.count, self.steps = name, count, steps
        self.level = 1
        self.scattering = True
        self.kept = [kept]
        self.send(sent)

    def send(self, sent):
        self.sent = sent
        self.got = [exchange(sent, self.count, self.steps[self.level])]

    def job(self):
        if not self.scattering:
            return Gather(self.name, [self.sent], self.got, self.steps[self.level])
        if self.level + 1 < len(self.steps):
            unit = 16 << (len(self.steps) - 1 - self.level)
            return Scatter(self.name, self.kept, self.got, self.steps[self.level + 1], False, unit)
        return Reduce(self.name, self.kept, self.got, None)

    def take(self, made):
        if not self.scattering:
            self.level -= 1
        elif self.level + 1 < len(self.steps):
            self.level += 1
            self.kept = [made["next" + self.name]]
        else:
            self.scattering = False
        self.send(made["sent" + self.name])

    def ready(self):
        return not self.scattering and self.level == 0


class SmallSum:
    def __init__(self, name, mine, other, count, order):
        self.name, self.count, self.order = name, count, order
        self.value = mine
        self.got = swap(other)
        self.level = 0

    def job(self):
        return Add(self.name, self.value, self.got)

    def take(self, made):
        self.value = made["total" + self.name]
        if self.level < len(self.order):
            bit = self.order[self.level]
            self.got = exchange(self.value, self.count, (bit, bit))
        self.level += 1

    def ready(self):
        return self.level > len(self.order)


def shards(
    frames_in,
    utter_lengths,
    code_ids,
    alpha_first,
    alpha_second,
    alpha_last,
    w_dilated,
    w_point,
    w_down,
    w_latent,
    w_expand,
    codebook,
    out_grad,
):
    count = lax.axis_size(DP)
    half = frames_in.shape[3]
    full = 2 * half
    codes = codebook.shape[1]
    order = Order()

    frames_got = swap(frames_in)
    p_got = swap(w_point)
    w_mine = w_dilated.reshape(3, K * full, half)
    w_got = swap(w_mine)
    alpha_rows = jnp.concatenate([alpha_first, alpha_second, alpha_last[None]], axis=0)
    place = (utter_lengths, alpha_rows, swap(alpha_rows))

    ready = run_prepare(order, w_down, w_latent.T, w_expand, out_grad, code_ids, codebook)
    came = swap(ready["sent"])
    made = run_forward(
        order, place, frames_in, frames_got, w_mine, w_got, w_point, p_got,
        dict(
            sent=ready["sent"], came=came,
            chosen=ready["chosen"], back_mine=ready["back_mine"],
        ),
    )
    seen = [made[f"seen{u}"] for u in range(3)]
    rates = [None] * 5 + [made["rates"], made["last_rates"]]
    grads = [None, None, (made["mine"], swap(made["other"]), made["other"])]
    seen_got = [None, None, swap(seen[2])]
    running, dilated, grad = made["running"], made["dilated"], made["grad"]

    def open_unit(u, grad):
        made = run_opening(
            order, u, place, grads[u][0], grads[u][2], running, grad, dilated, w_mine, w_got, w_point, p_got
        )
        rates[u] = made["rates"]
        if u > 0:
            rates[2 + u] = made["mid_rates"]
            grads[u - 1] = (made["mine"], swap(made["other"]), made["other"])
        return made

    x, y, z = chip_axes(count)
    code_mine, code_sent = run_code_grad(
        order, ready["ids_t"], ready["back_mine"], came, made["down_sum"], codes
    )
    codes_sum = SmallSum("", code_mine, code_sent, count, z[::-1] + y + x)
    plan, later = piece_plan(full, count)
    firsts = [
        FirstStep(f"{index}", count, cores, 2 - index) for index, cores in enumerate(two_orders(count))
    ]

    def weigh(u):
        made = run_weight(
            order, u, place, seen[u], seen_got[u], grads[u][0], grads[u][1], plan[u],
            (codes_sum.value, codes_sum.got) if u > 0 else None,
        )
        if u > 0:
            codes_sum.take(made)
        for index, one in enumerate(firsts):
            one.begin(made[f"sent{index}"], made[f"kept{index}"])

    grad = open_unit(2, grad)["grad"]
    seen_got[1] = swap(seen[1])
    order.before += [seen_got[1]]
    weigh(2)
    first = [one.got[0] for one in firsts]
    grad = open_unit(1, grad)["grad"]
    seen_got[0] = swap(seen[0])
    mixed_got = swap(made["mixed"])
    order.before += first + [seen_got[0], mixed_got]
    weigh(1)
    weigh(0)
    order.before += [one.got[1] for one in firsts] + [codes_sum.got]
    last = open_unit(0, grad)
    run_step(order, firsts + [codes_sum])
    (name0, sent0, kept0), (name1, sent1, kept1) = firsts[0].made
    [(name2, sent2, kept2)] = firsts[1].made
    sums = [firsts[0].go_on(name0, sent0, kept0)]
    sent1, sent2, frames_sent = run_hold(order, [sent1, sent2, last["frames_sent"]])
    sums += [firsts[0].go_on(name1, sent1, kept1), firsts[1].go_on(name2, sent2, kept2)]

    def advance(*more):
        if not sums[0].scattering:
            order.before.append(swap(sums[0].got[0][:16]))
        run_step(order, sums[:1])
        run_step(order, sums[1:] + [one for one in more if not one.ready()])

    block_out, small_mine, small_other = run_collect(
        order, rates, made["mixed"], mixed_got, out_grad, w_expand, half
    )
    small = SmallSum("small", small_mine, small_other, count, z + y + x)
    grad_frames = run_place(order, last["frames_mine"], swap(frames_sent))
    while not (codes_sum.ready() or sums[0].ready()):
        advance(codes_sum, small)
    codes_back = swap(codes_sum.value)
    advance(small)
    grad_codebook = run_codebook(order, codes_sum.value, codes_back, codebook)
    while not sums[0].ready():
        advance(small)
    parts, gots = [one.sent for one in sums], [one.got[0] for one in sums]
    written = run_finish(order, later, "part", parts, None, full)
    soon = [(unit, piece) for unit, piece in later if piece.name == "0"]
    written = run_finish(order, soon, "got", gots[:1], written, full)
    grad_w_down, grad_w_latent = run_down(order, codes_sum.value, codes_back, w_latent.T, w_down)
    while not small.ready():
        run_step(order, [small])
    rest = [(unit, piece) for unit, piece in later if piece.name != "0"]
    written = run_finish(order, rest, "got", gots, written, full)
    grad_w_dilated, grad_w_point = written["conv"], written["point"]
    small = small.value
    return (
        block_out,
        grad_frames,
        small[0:3],
        small[3:6],
        small[6],
        grad_w_dilated.reshape(3, K, full, half),
        grad_w_point,
        grad_w_down,
        grad_w_latent.T,
        jnp.concatenate(
            [small[start : start + 8] for start in range(8, small.shape[0], 8)], axis=1
        ),
        grad_codebook,
    )


def solution(mesh):
    placed = (
        P(None, DP, None, CHAN),
        P(None, DP, None),
        P(None, DP, None),
        P(None, CHAN),
        P(None, CHAN),
        P(CHAN),
        P(None, None, None, CHAN),
        P(None, None, CHAN),
        P(None, None, CHAN),
        P(CHAN, None),
        P(None, CHAN),
        P(),
        P(None, DP, None, CHAN),
    )
    return jax.shard_map(
        shards,
        mesh=mesh,
        in_specs=placed,
        out_specs=(
            P(None, DP, None, CHAN),
            P(None, DP, None, CHAN),
            P(None, CHAN),
            P(None, CHAN),
            P(CHAN),
            P(None, None, None, CHAN),
            P(None, None, CHAN),
            P(None, None, CHAN),
            P(CHAN, None),
            P(None, CHAN),
            P(),
        ),
        check_vma=False,
    )
```

```python
import functools
import types
import jax
import jax.numpy as jnp
from jax import lax
from jax.experimental import pallas as pl
from jax.experimental.pallas import tpu as pltpu
from jax.sharding import PartitionSpec as P

DP = "dp"
CHAN = "chan"
K = 7
STRIDE = 8
KS = 16
DILATIONS = (1, 3, 9)
BF = jnp.bfloat16
F32 = jnp.float32
HALO = 32
TILE = 512
LANES = 128
SINE = (3.141592580569316, -5.1677069002071025, 2.550031640919103, -0.5980464504720939, 0.0772222489218058)
COSINE = (0.9999999534666402, -4.934792858671753, 4.058411914096722, -1.3318801607983635, 0.2196967977026182)
VMEM_LIMIT = 63 * 1024 * 1024
SMALL_LIMIT = 16 * 1024 * 1024
COST = dict(prepare=9, forward=36, code_grads=3, weight_grads=10, opening=15)
ANY = pl.BlockSpec(memory_space=pl.ANY)
SMEM = pl.BlockSpec(memory_space=pltpu.SMEM)
VMEM = pl.BlockSpec(memory_space=pltpu.VMEM)
DMA = pltpu.SemaphoreType.DMA


def shape(dims, kind):
    return jax.ShapeDtypeStruct(dims, kind)


class Order:
    def __init__(self):
        self.token = None
        self.before = []


def call(order, kernel, name, ins, outs, scratch, aliases=None, limit=VMEM_LIMIT):
    deps = ([] if order.token is None else [order.token]) + order.before
    order.before = []

    def body(*refs):
        refs = list(refs)
        named = dict(zip(ins, refs))
        refs = refs[len(ins) + len(deps) :]
        named.update(zip(outs, refs))
        refs[len(outs)][...] = jnp.zeros((8, LANES), F32)
        named.update(zip(scratch, refs[len(outs) + 1 :]))
        kernel(types.SimpleNamespace(**named))

    token = shape((8, LANES), F32)
    made = pl.pallas_call(
        body,
        out_shape=[out for _, out in outs.values()] + [token],
        in_specs=[spec for spec, _ in ins.values()] + [ANY] * len(deps),
        out_specs=[spec for spec, _ in outs.values()] + [VMEM],
        scratch_shapes=list(scratch.values()),
        input_output_aliases=aliases or {},
        compiler_params=pltpu.CompilerParams(vmem_limit_bytes=limit),
        cost_estimate=pl.CostEstimate(
            flops=COST.get(name, 0) << 30, bytes_accessed=COST.get(name, 0) * 3500000, transcendentals=0
        ),
        name=name,
    )(*[array for _, array in ins.values()], *deps)
    order.token = made[-1]
    return dict(zip(outs, made))


class Copies:
    def __init__(self, sem):
        self.sem = sem
        self.made = []
        self.done = set()

    def start(self, source, target):
        copy = pltpu.make_async_copy(source, target, self.sem.at[len(self.made)])
        copy.start()
        self.made.append(copy)
        return len(self.made) - 1

    def wait(self, *numbers):
        for number in numbers:
            if number not in self.done:
                self.done.add(number)
                self.made[number].wait()

    def wait_all(self):
        self.wait(*range(len(self.made)))


def dot(left, right):
    return jnp.dot(left, right, preferred_element_type=F32)


def dot_cols(left, right):
    return lax.dot_general(left, right, (((1,), (1,)), ((), ())), preferred_element_type=F32)


def dot_rows(left, right):
    return lax.dot_general(left, right, (((0,), (0,)), ((), ())), preferred_element_type=F32)


def poly(u, terms):
    total = terms[-1]
    for term in terms[-2::-1]:
        total = total * u + term
    return total


def half_turns(v, alpha):
    turns = v * (alpha * 0.3183098861837907)
    return turns - jnp.round(turns)


def snake(v, alpha):
    t = half_turns(v, alpha)
    u = t * t
    p = poly(u, SINE)
    return v + (u * (p * p)) * (1.0 / alpha)


def snake_slopes(v, alpha):
    t = half_turns(v, alpha)
    u = t * t
    sine = t * poly(u, SINE)
    double = 2.0 * sine * poly(u, COSINE)
    return sine * sine, double


def ends_of(lengths, row):
    ends = []
    total = 0
    for utt in range(lengths.shape[2]):
        total = total + lengths[row, 0, utt] * STRIDE
        ends.append(total)
    return ends


def put_labels(label_ref, ends, frames):
    t = lax.broadcasted_iota(jnp.int32, label_ref.shape, 0) - HALO
    label = jnp.zeros(label_ref.shape, jnp.int32)
    for end in ends:
        label = label + (t >= end).astype(jnp.int32)
    label_ref[...] = jnp.where((t < 0) | (t >= frames), -1, label)


def put_edges(padded_ref, frames):
    edge = jnp.zeros((HALO, padded_ref.shape[1]), F32)
    padded_ref[:HALO, :] = edge
    padded_ref[HALO + frames :, :] = edge


def tap(padded_ref, label_ref, row, rows, offset):
    here = HALO + row
    width = padded_ref.shape[1]
    same = label_ref[here + offset : here + offset + rows, :] == label_ref[here : here + rows, :]
    pieces = []
    for lane in range(0, width, LANES):
        piece = padded_ref[here + offset : here + offset + rows, lane : lane + LANES]
        pieces.append(jnp.where(same, piece, 0.0).astype(BF))
    return jnp.concatenate(pieces, axis=1)


def column_half(core, half):
    return pl.ds(pl.multiple_of(core * half, half), half)


def both_columns(half):
    core = lax.axis_index(CHAN)
    return column_half(core, half), column_half(1 - core, half)


def put_row(target, mine, other, index, own, oth):
    half = mine.shape[1]
    target[:, own] = jnp.broadcast_to(mine[index : index + 1, :], (8, half))
    target[:, oth] = jnp.broadcast_to(other[index : index + 1, :], (8, half))
    return target[0:1, :]


def split(values, terms):
    parts = []
    for _ in range(terms):
        part = values.astype(BF)
        parts.append(part)
        values = values - part.astype(F32)
    return parts


def row_sums(values):
    return jnp.sum(values.reshape(values.shape[0] // 8, 8, values.shape[1]), axis=0)


def tiles_of(frames):
    return [(slice(start, start + TILE), pl.ds(start, TILE)) for start in range(0, frames, TILE)]


def forward_kernel(r):
    frames, full = r.run_v.shape[1:]
    half = full // 2
    core = lax.axis_index(CHAN)
    own, oth = both_columns(half)
    copies = Copies(r.sem)
    tiles = tiles_of(frames)
    place = [
        copies.start(r.lengths, r.lengths_v),
        copies.start(r.alpha_mine, r.alpha_mv),
        copies.start(r.alpha_other, r.alpha_ov),
    ]
    loads = [copies.start(r.frames_in.at[core, 0], r.mine_v), copies.start(r.frames_got.at[core, 0], r.other_v)]

    def load_weights(unit):
        return [
            copies.start(r.w_mine.at[unit], r.w_v.at[unit % 2, 0]),
            copies.start(r.w_other.at[unit], r.w_v.at[unit % 2, 1]),
        ]

    weights = [load_weights(0)]
    points = [copies.start(r.p_mine, r.pm_v), copies.start(r.p_other, r.po_v)]
    weights.append(load_weights(1))
    small = [
        copies.start(source, target)
        for source, target in (
            (r.sent.at[pl.ds(0, full)], r.dm_v), (r.came.at[pl.ds(0, full)], r.do_v),
            (r.chosen, r.chosen_v), (r.back_mine, r.bm_v),
            (r.came.at[pl.ds(full, r.bo_v.shape[0])], r.bo_v),
        )
    ]
    put_edges(r.padded, frames)
    copies.wait(*place)
    put_labels(r.label, ends_of(r.lengths_v, core), frames)
    copies.wait(*loads)
    leaving = {(kind, slot): [] for kind in ("run", "mid", "seen") for slot in range(2)}

    def settle(kind, slot):
        copies.wait(*leaving[kind, slot])
        leaving[kind, slot] = []

    for unit in range(3):
        now, later = r.run_v.at[unit % 2], r.run_v.at[(unit + 1) % 2]
        mid = r.mid_v.at[unit % 2]
        seen = r.seen_v.at[unit % 2]
        rate_in = put_row(r.rate_v.at[unit], r.alpha_mv, r.alpha_ov, unit, own, oth)
        rate_mid = put_row(r.rate_v.at[3 + unit], r.alpha_mv, r.alpha_ov, 3 + unit, own, oth)
        settle("seen", unit % 2)
        for rows, there in tiles:
            if unit == 0:
                now[rows, own] = r.mine_v[rows, :].astype(F32)
                now[rows, oth] = r.other_v[rows, :].astype(F32)
                leaving["run", 0].append(copies.start(now.at[there], r.running.at[unit, there]))
            opened = snake(now[rows, :], rate_in)
            r.padded[HALO + rows.start : HALO + rows.stop, :] = opened
            seen[:full, rows] = opened.T.astype(BF)
        seen_out = getattr(r, f"seen{unit}")
        leaving["seen", unit % 2].append(
            copies.start(seen.at[pl.ds(0, full)], seen_out.at[pl.ds(0, full)])
        )
        copies.wait(*weights[unit])
        if unit == 0:
            copies.wait(*points)
        settle("mid", unit % 2)
        settle("run", (unit + 1) % 2)
        for place_of, (rows, there) in enumerate(tiles):
            taps = r.taps.at[place_of % 2]
            for index in range(K):
                offset = DILATIONS[unit] * (index - K // 2)
                taps[:, index * full : (index + 1) * full] = tap(
                    r.padded, r.label, rows.start, TILE, offset
                )
            mid[rows, own] = dot(taps[...], r.w_v[unit % 2, 0])
            mid[rows, oth] = dot(taps[...], r.w_v[unit % 2, 1])
            if unit < 2:
                leaving["mid", unit % 2].append(copies.start(mid.at[there], r.dilated.at[unit, there]))
            closed = snake(mid[rows, :], rate_mid)
            seen[full:, rows] = closed.T.astype(BF)
            closed = closed.astype(BF)
            later[rows, own] = now[rows, own] + dot(closed, r.pm_v[unit])
            later[rows, oth] = now[rows, oth] + dot(closed, r.po_v[unit])
            if unit < 2:
                leaving["run", (unit + 1) % 2].append(
                    copies.start(later.at[there], r.running.at[unit + 1, there])
                )
        leaving["seen", unit % 2].append(
            copies.start(seen.at[pl.ds(full, full)], seen_out.at[pl.ds(full, full)])
        )
        if unit == 0:
            weights.append(load_weights(2))

    running, mid = r.run_v.at[1], r.mid_v.at[0]
    blocks = frames // STRIDE
    value = put_row(r.rate_v.at[6], r.alpha_mv, r.alpha_ov, 6, own, oth)
    mid_value = r.rate_v[5, 0:1, :]
    inverse = 1.0 / value
    copies.wait(*small)
    width = r.dm_v.shape[1]
    code = width // KS
    lane = lax.broadcasted_iota(jnp.int32, (TILE, width), 1) // code
    step = lax.broadcasted_iota(jnp.int32, (TILE, width), 0) % STRIDE
    pattern = (lane % STRIDE == (step + STRIDE // 2) % STRIDE).astype(F32)
    down = r.dm_v[...] + r.do_v[...]
    down_parts = jnp.concatenate(split(down, 2), axis=1)
    sums = []
    for rows, _ in tiles:
        v = running[rows, :]
        square, double = snake_slopes(v, value)
        r.square_v[rows, :] = square
        r.double_v[rows, :] = double
        opened = (v + square * inverse).astype(BF)
        r.opened_v[rows, :] = opened
        products = dot(opened, down_parts)
        products = products[:, :width] + products[:, width:]
        products = (products * pattern).reshape(TILE // STRIDE, STRIDE, width)
        sums.append(jnp.sum(products, axis=1))
    sums = jnp.concatenate(sums, axis=0)
    block = lax.broadcasted_iota(jnp.int32, (blocks, width), 0)
    block_lane = lax.broadcasted_iota(jnp.int32, (blocks, width), 1)
    label = jnp.zeros((blocks, width), jnp.int32)
    for end in ends_of(r.lengths_v, core):
        label = label + (block * STRIDE >= end).astype(jnp.int32)

    def earlier(values):
        return pltpu.roll(values, 1, 0)

    def later_rows(values):
        return pltpu.roll(values, blocks - 1, 0)

    same_before = jnp.where((block > 0) & (earlier(label) == label), 1.0, 0.0)
    same_after = jnp.where((block < blocks - 1) & (later_rows(label) == label), 1.0, 0.0)
    early = block_lane < 4 * code
    late = block_lane >= 12 * code
    sums = jnp.where(
        early, same_before * earlier(sums), jnp.where(late, same_after * later_rows(sums), sums)
    )
    fold = (
        lax.broadcasted_iota(jnp.int32, (width, width), 0) % code
        == lax.broadcasted_iota(jnp.int32, (width, width), 1) % code
    ).astype(BF)
    latent = dot(jnp.concatenate(split(sums, 3), axis=1), jnp.concatenate([fold] * 3, axis=0))
    scale = lax.rsqrt(jnp.sum(latent * latent, axis=1, keepdims=True) * (1.0 / KS) + 1.0)
    unit_code = latent * scale
    r.mixed[...] = (unit_code + r.chosen_v[...]).astype(BF)
    back = r.bm_v[...] + r.bo_v[...]
    along = jnp.sum(unit_code * back, axis=1, keepdims=True) * (1.0 / KS)
    spread = (back - unit_code * along) * scale
    spread = jnp.where(
        early,
        later_rows(same_before * spread),
        jnp.where(late, earlier(same_after * spread), spread),
    )
    down_t_parts = split(down.T, 2)
    down_t_stack = jnp.concatenate([down_t_parts[0], down_t_parts[1], down_t_parts[0]], axis=0)
    total = jnp.zeros((8, full), F32)
    last_total = jnp.zeros((8, full), F32)
    down_total = jnp.zeros(down.shape, F32)
    for rows, there in tiles:
        own_blocks = spread[rows.start // STRIDE : rows.stop // STRIDE, :]
        wide = jnp.broadcast_to(
            own_blocks[:, None, :], (TILE // STRIDE, STRIDE, width)
        ).reshape(TILE, width) * pattern
        parts = split(wide, 2)
        sums = lax.dot_general(
            r.opened_v[rows, :],
            jnp.concatenate(parts, axis=1),
            (((0,), (0,)), ((), ())),
            preferred_element_type=F32,
        )
        down_total = down_total + (sums[:, :width] + sums[:, width:])
        grad_last = dot(jnp.concatenate([parts[0], parts[0], parts[1]], axis=1), down_t_stack)
        square = r.square_v[rows, :]
        double = r.double_v[rows, :]
        grad = grad_last * (1.0 + double)
        r.grad_v[rows, :] = grad
        copies.start(r.grad_v.at[there], r.grad.at[there])
        rate = grad_last * (running[rows, :] * double - square * inverse)
        last_total = last_total + row_sums(rate)
        total = total + closing_steps(
            r, rows, grad, mid[rows, :], mid_value, (own, oth), r.pm_v[2], r.po_v[2]
        )
        send_closing(r, copies, rows, there, own, oth)
    r.rates[...] = total * (1.0 / mid_value)
    r.last_rates[...] = last_total * inverse
    r.down_sum[:, :width] = down_total[:half, :].astype(BF)
    r.down_sum[:, width:] = down_total[half:, :].astype(BF)
    copies.wait_all()


def closing_steps(r, rows, point, mid, alpha, core_cols, p_mine, p_other):
    own, oth = core_cols
    r.gp_v[rows, :] = point.astype(BF)
    grad = dot_cols(r.gp_v[rows, own], p_mine) + dot_cols(r.gp_v[rows, oth], p_other)
    square, double = snake_slopes(mid, alpha)
    r.gd_v[rows, :] = (grad * (1.0 + double)).astype(BF)
    return row_sums(grad * (mid * double - square * (1.0 / alpha)))


def send_closing(r, copies, rows, there, own, oth):
    frames = r.gp_v.shape[0]
    after = pl.ds(frames + rows.start, TILE)
    copies.start(r.gp_v.at[there, own], r.mine.at[there])
    copies.start(r.gd_v.at[there, own], r.mine.at[after])
    copies.start(r.gp_v.at[there, oth], r.other.at[there])
    copies.start(r.gd_v.at[there, oth], r.other.at[after])


def place_ins(place):
    return {name: (ANY, array) for name, array in zip(("lengths", "alpha_mine", "alpha_other"), place)}


def place_rooms(place, full):
    lengths, alpha, _ = place
    return dict(
        lengths_v=pltpu.SMEM(lengths.shape, jnp.int32),
        alpha_mv=pltpu.VMEM(alpha.shape, F32),
        alpha_ov=pltpu.VMEM(alpha.shape, F32),
        rate_v=pltpu.VMEM((7, 8, full), F32),
    )


def any_ins(**arrays):
    return {name: (ANY, array) for name, array in arrays.items()}


def vmem_ins(**arrays):
    return {name: (VMEM, array) for name, array in arrays.items()}


def run_forward(order, place, frames_in, frames_got, w_mine, w_other, p_mine, p_other, small):
    frames, half = frames_in.shape[2:]
    full = 2 * half
    tiles = frames // TILE
    blocks = frames // STRIDE
    width = small["chosen"].shape[1]
    wide = (frames, full)
    pair = (ANY, shape((2 * frames, half), BF))
    square = pltpu.VMEM((blocks, width), F32)
    tall = pltpu.VMEM((full, width), F32)
    return call(
        order,
        forward_kernel,
        "forward",
        dict(
            **place_ins(place),
            **any_ins(frames_in=frames_in, frames_got=frames_got, w_mine=w_mine, w_other=w_other,
                      p_mine=p_mine, p_other=p_other, **small),
        ),
        dict(
            running=(ANY, shape((3,) + wide, F32)),
            dilated=(ANY, shape((2,) + wide, F32)),
            seen0=(ANY, shape((2 * full, frames), BF)),
            seen1=(ANY, shape((2 * full, frames), BF)),
            seen2=(ANY, shape((2 * full, frames), BF)),
            grad=(ANY, shape(wide, F32)),
            mixed=(VMEM, shape((blocks, width), BF)),
            down_sum=(VMEM, shape((half, 2 * width), BF)),
            last_rates=(VMEM, shape((8, full), F32)),
            mine=pair,
            other=pair,
            rates=(VMEM, shape((8, full), F32)),
        ),
        dict(
            **place_rooms(place, full),
            mine_v=pltpu.VMEM((frames, half), BF),
            other_v=pltpu.VMEM((frames, half), BF),
            run_v=pltpu.VMEM((2,) + wide, F32),
            mid_v=pltpu.VMEM((2,) + wide, F32),
            seen_v=pltpu.VMEM((2, 2 * full, frames), BF),
            padded=pltpu.VMEM((frames + 2 * HALO, full), F32),
            label=pltpu.VMEM((frames + 2 * HALO, LANES), jnp.int32),
            taps=pltpu.VMEM((2, TILE, K * full), BF),
            w_v=pltpu.VMEM((2, 2) + w_mine.shape[1:], BF),
            pm_v=pltpu.VMEM(p_mine.shape, BF),
            po_v=pltpu.VMEM(p_mine.shape, BF),
            dm_v=tall, do_v=tall, chosen_v=square, bm_v=square, bo_v=square,
            opened_v=pltpu.VMEM(wide, BF),
            square_v=pltpu.VMEM(wide, F32),
            double_v=pltpu.VMEM(wide, F32),
            grad_v=pltpu.VMEM(wide, F32),
            gp_v=pltpu.VMEM(wide, BF),
            gd_v=pltpu.VMEM(wide, BF),
            sem=DMA((3 + 2 + 6 + 2 + 5 + 5 * tiles + 6 + 5 * tiles,)),
        ),
    )


def weight_kernel(unit, pieces, r):
    frames = r.padded.shape[1] - 2 * HALO
    half = r.padded.shape[2]
    full = 2 * half
    core = lax.axis_index(CHAN)
    copies = Copies(r.sem)
    place = copies.start(r.lengths, r.lengths_v)
    grads = []
    for row, source in enumerate((r.grads_mine, r.grads_got)):
        grads.append(copies.start(source.at[pl.ds(frames, frames)], r.gd_v.at[row]))
    opened = []
    for row, source in enumerate((r.seen_mine, r.seen_got)):
        columns = pl.ds(row * frames, frames)
        opened.append(copies.start(source.at[pl.ds(0, full)], r.seen_v.at[pl.ds(0, full), columns]))
    points = []
    for row, (source, seen) in enumerate(((r.grads_mine, r.seen_mine), (r.grads_got, r.seen_got))):
        columns = pl.ds(row * frames, frames)
        points.append(copies.start(source.at[pl.ds(0, frames)], r.gp_v.at[columns]))
        points.append(copies.start(seen.at[pl.ds(full, full)], r.seen_v.at[pl.ds(full, full), columns]))
    if hasattr(r, "value"):
        beside = [copies.start(r.value, r.value_v), copies.start(r.came, r.came_v)]
    for row in range(2):
        put_edges(r.padded.at[row], frames)
    copies.wait(place)
    for row in range(2):
        put_labels(r.label.at[row], ends_of(r.lengths_v, core if row == 0 else 1 - core), frames)
    for row in range(2):
        copies.wait(grads[row])
        r.padded[row, HALO : HALO + frames, :] = r.gd_v[row].astype(F32)
    copies.wait(*opened)
    waiting = list(pieces)

    def send_pieces(rows):
        for piece in [piece for piece in waiting if piece.start + 2 * piece.rows <= rows]:
            waiting.remove(piece)
            side = kept_side(piece.bits)
            for kind, which in (("sent", 1 - side), ("kept", side)):
                here = pl.ds(pl.multiple_of(piece.start + which * piece.rows, 16), piece.rows)
                copies.start(r.out_v.at[here], getattr(r, kind + piece.name))

    for index in range(K):
        offset = -DILATIONS[unit] * (index - K // 2)
        taps = r.taps.at[index % 2]
        for row in range(2):
            for start in range(0, frames, TILE):
                taps[row * frames + start : row * frames + start + TILE, :] = tap(
                    r.padded.at[row], r.label.at[row], start, TILE, offset
                )
        r.out_v[index * full : (index + 1) * full, :] = dot(r.seen_v[:full, :], taps[...]).astype(BF)
        send_pieces((index + 1) * full)
    if hasattr(r, "value"):
        copies.wait(*beside)
        total = r.value_v[...].astype(F32) + r.came_v[...].astype(F32)
        r.value_v[...] = total.astype(BF)
        copies.start(r.value_v, r.total)
    copies.wait(*points)
    r.out_v[K * full : (K + 1) * full, :] = dot(r.seen_v[full:, :], r.gp_v[...]).astype(BF)
    send_pieces((K + 1) * full)
    copies.wait_all()


def kept_side(bits):
    bit = jnp.where(lax.axis_index(CHAN) == 0, bits[0], bits[1])
    return lax.shift_right_logical(lax.axis_index(DP), bit) & 1


class Piece:
    def __init__(self, name, start, rows, place, bits, span):
        self.name, self.start, self.rows, self.place, self.bits, self.span = name, start, rows, place, bits, span


def run_weight(order, unit, place, seen_mine, seen_got, grads_mine, grads_got, pieces, beside=None):
    frames, half = grads_mine.shape[0] // 2, grads_mine.shape[1]
    full = 2 * half
    ins = any_ins(lengths=place[0], seen_mine=seen_mine, seen_got=seen_got,
                  grads_mine=grads_mine, grads_got=grads_got)
    scratch = dict(
        lengths_v=pltpu.SMEM(place[0].shape, jnp.int32),
        seen_v=pltpu.VMEM((2 * full, 2 * frames), BF),
        gd_v=pltpu.VMEM((2, frames, half), BF),
        gp_v=pltpu.VMEM((2 * frames, half), BF),
        padded=pltpu.VMEM((2, frames + 2 * HALO, half), F32),
        label=pltpu.VMEM((2, frames + 2 * HALO, LANES), jnp.int32),
        taps=pltpu.VMEM((2, 2 * frames, half), BF),
        out_v=pltpu.VMEM(((K + 1) * full, half), BF),
        sem=DMA((12 + 2 * len(pieces),)),
    )
    outs = {
        kind + piece.name: (ANY, shape((piece.rows, half), BF))
        for piece in pieces
        for kind in ("sent", "kept")
    }
    if beside is not None:
        value, came = beside
        ins.update(any_ins(value=value, came=came))
        outs["total"] = (ANY, shape(value.shape, BF))
        scratch.update(value_v=pltpu.VMEM(value.shape, BF), came_v=pltpu.VMEM(value.shape, BF))
    return call(
        order, functools.partial(weight_kernel, unit, pieces), "weight_grads", ins, outs, scratch
    )


def opening_kernel(unit, r):
    last = unit == 0
    frames, full = r.running_v.shape
    half = full // 2
    core = lax.axis_index(CHAN)
    own, oth = both_columns(half)
    copies = Copies(r.sem)
    tiles = tiles_of(frames)
    place = [
        copies.start(r.lengths, r.lengths_v),
        copies.start(r.alpha_mine, r.alpha_mv),
        copies.start(r.alpha_other, r.alpha_ov),
    ]
    after = pl.ds(frames, frames)
    grads = [
        copies.start(r.grads_mine.at[after], r.gm_v),
        copies.start(r.grads_other.at[after], r.go_v),
    ]
    weights = [
        copies.start(r.w_mine.at[unit], r.w_v.at[0]),
        copies.start(r.w_other.at[unit], r.w_v.at[1]),
    ]
    if not last:
        points = [
            copies.start(r.p_mine.at[unit - 1], r.pm_v),
            copies.start(r.p_other.at[unit - 1], r.po_v),
        ]
    loads = []
    for _, there in tiles:
        loads.append([
            copies.start(r.running.at[unit, there], r.running_v.at[there]),
            copies.start(r.grad_in.at[there], r.grad_v.at[there]),
        ])
        if not last:
            loads[-1].append(copies.start(r.dilated.at[unit - 1, there], r.mid_v.at[there]))
    for part in range(2):
        put_edges(r.padded.at[part], frames)
    copies.wait(*place)
    put_labels(r.label, ends_of(r.lengths_v, core), frames)
    value = put_row(r.rate_v.at[0], r.alpha_mv, r.alpha_ov, unit, own, oth)
    if not last:
        mid_value = put_row(r.rate_v.at[1], r.alpha_mv, r.alpha_ov, 2 + unit, own, oth)
    for part, values in ((0, r.gm_v), (1, r.go_v)):
        copies.wait(grads[part])
        r.padded[part, HALO : HALO + frames, :] = values[...].astype(F32)
    for part in range(2):
        copies.wait(weights[part])
        for index in range(K):
            r.turned_v[(2 * index + part) * half : (2 * index + part + 1) * half, :] = r.w_v[
                part, index * full : (index + 1) * full, :
            ].T
    if not last:
        copies.wait(*points)
    total = jnp.zeros((8, full), F32)
    mid_total = jnp.zeros((8, full), F32)
    for place_of, (rows, there) in enumerate(tiles):
        taps = r.taps.at[place_of % 2]
        for index in range(K):
            offset = -DILATIONS[unit] * (index - K // 2)
            for part in range(2):
                start = (2 * index + part) * half
                taps[:, start : start + half] = tap(
                    r.padded.at[part], r.label, rows.start, TILE, offset
                )
        opened = dot(taps[...], r.turned_v[...])
        copies.wait(*loads[place_of])
        v = r.running_v[rows, :]
        square, double = snake_slopes(v, value)
        grad = r.grad_v[rows, :] + opened * (1.0 + double)
        r.grad_v[rows, :] = grad
        total = total + row_sums(opened * (v * double - square * (1.0 / value)))
        if last:
            copies.start(r.grad_v.at[there, own], r.frames_mine.at[core, 0, there])
            copies.start(r.grad_v.at[there, oth], r.frames_sent.at[there])
        else:
            copies.start(r.grad_v.at[there], r.grad.at[there])
            mid_total = mid_total + closing_steps(
                r, rows, grad, r.mid_v[rows, :], mid_value, (own, oth), r.pm_v[...], r.po_v[...]
            )
            send_closing(r, copies, rows, there, own, oth)
    r.rates[...] = total * (1.0 / value)
    if not last:
        r.mid_rates[...] = mid_total * (1.0 / mid_value)
    copies.wait_all()


def run_opening(order, unit, place, grads_mine, grads_other, running, grad, dilated, w_mine, w_other, p_mine, p_other):
    frames, full = grad.shape
    half = full // 2
    tiles = frames // TILE
    last = unit == 0
    wide = pltpu.VMEM((frames, full), F32)
    narrow = pltpu.VMEM((frames, full), BF)
    part = pltpu.VMEM((frames, half), BF)
    point = pltpu.VMEM(p_mine.shape[1:], BF)
    pair = (ANY, shape((2 * frames, half), BF))
    rates = (VMEM, shape((8, full), F32))
    ins = dict(
        **place_ins(place),
        **any_ins(grads_mine=grads_mine, grads_other=grads_other, running=running, grad_in=grad,
                  w_mine=w_mine, w_other=w_other),
    )
    outs = dict(rates=rates)
    scratch = dict(
        **place_rooms(place, full),
        gm_v=part, go_v=part,
        padded=pltpu.VMEM((2, frames + 2 * HALO, half), F32),
        label=pltpu.VMEM((frames + 2 * HALO, LANES), jnp.int32),
        running_v=wide, grad_v=wide,
        w_v=pltpu.VMEM((2,) + w_mine.shape[1:], BF),
        turned_v=pltpu.VMEM((K * full, full), BF),
        taps=pltpu.VMEM((2, TILE, K * full), BF),
    )
    if last:
        outs["frames_mine"] = (ANY, shape((2, 1, frames, half), F32))
        outs["frames_sent"] = (ANY, shape((frames, half), F32))
    else:
        ins.update(any_ins(dilated=dilated, p_mine=p_mine, p_other=p_other))
        outs.update(grad=(ANY, shape((frames, full), F32)), mine=pair, other=pair, mid_rates=rates)
        scratch.update(mid_v=wide, pm_v=point, po_v=point, gp_v=narrow, gd_v=narrow)
    scratch["sem"] = DMA((3 + 2 + 2 + 2 + 8 * tiles,))
    return call(
        order, functools.partial(opening_kernel, unit), "opening", ins, outs, scratch
    )


def prepare_kernel(r):
    taps, full, out_half = r.w_down.shape
    code, codes = r.codebook.shape
    blocks = r.ids.shape[2]
    width = taps * code
    core = lax.axis_index(CHAN)
    copies = Copies(r.sem)
    first = [copies.start(r.ids.at[core], r.ids_v), copies.start(r.codebook, r.book_v)]
    loads = [copies.start(r.w_down.at[index], r.down_v.at[index]) for index in range(taps)]
    copies.wait(*first)
    mark = r.ids_v[...]
    total = jnp.zeros((3 * code, blocks), F32)
    step = 1024
    for start in range(0, codes, step):
        columns = r.book_v[:, start : start + step]
        unit = columns * lax.rsqrt(jnp.sum(columns * columns, axis=0, keepdims=True) + 1.0)
        parts = jnp.concatenate([part.astype(F32) for part in split(unit, 3)], axis=0).astype(BF)
        number = lax.broadcasted_iota(jnp.int32, (step, blocks), 0) + start
        total = total + dot(parts, jnp.where(number == mark, 1.0, 0.0).astype(BF))
    picked = total[:code] + total[code : 2 * code] + total[2 * code :]
    r.chosen[...] = jnp.concatenate([picked] * taps, axis=0).T
    r.ids_t[...] = jnp.broadcast_to(mark.astype(F32), (blocks, blocks)).T
    expand = jnp.concatenate([r.w_expand[...].astype(F32)] * taps, axis=0).astype(BF)
    r.back_mine[...] = dot_cols(r.out_grad[core, 0], expand)
    r.sent[full:, :] = dot_cols(r.out_grad[1 - core, 0], expand)
    fold = (
        lax.broadcasted_iota(jnp.int32, (code, width), 0)
        == lax.broadcasted_iota(jnp.int32, (code, width), 1) % code
    ).astype(BF)
    latent = dot_rows(r.w_latent[...], fold)
    group = lax.broadcasted_iota(jnp.int32, (out_half, width), 1) // code
    product = jnp.zeros((full, width), F32)
    for index in range(taps):
        copies.wait(loads[index])
        product = product + dot(r.down_v[index], jnp.where(group == index, latent, 0.0).astype(BF))
    r.sent[:full, :] = product


def run_prepare(order, w_down, w_latent, w_expand, out_grad, ids, codebook):
    taps, full, _ = w_down.shape
    width = taps * codebook.shape[0]
    blocks = ids.shape[2]
    square = (VMEM, shape((blocks, width), F32))
    return call(
        order,
        prepare_kernel,
        "prepare",
        dict(
            **any_ins(w_down=w_down, ids=ids, codebook=codebook),
            **vmem_ins(w_latent=w_latent, w_expand=w_expand, out_grad=out_grad),
        ),
        dict(
            sent=(VMEM, shape((full + blocks, width), F32)),
            chosen=square, back_mine=square,
            ids_t=(VMEM, shape((blocks, blocks), F32)),
        ),
        dict(
            down_v=pltpu.VMEM(w_down.shape, BF),
            book_v=pltpu.VMEM(codebook.shape, F32),
            ids_v=pltpu.VMEM(ids.shape[1:], jnp.int32),
            sem=DMA((taps + 2,)),
        ),
    )


def code_grad_kernel(r):
    blocks, width = r.back_mine.shape
    rows, half = r.mine.shape
    code = width // KS
    core = lax.axis_index(CHAN)
    came = r.came.shape[0] - blocks
    back = (r.back_mine[...] + r.came[came:, :]).T[:code, :]
    parts = jnp.concatenate([part.astype(F32) for part in split(back, 3)], axis=0).astype(BF)
    wide = 4
    for first in range(0, rows // code, wide):
        pieces = []
        for lane in range(0, wide * half, blocks):
            number = lax.broadcasted_iota(jnp.int32, (blocks, blocks), 1) + (first * half + lane)
            pieces.append(jnp.where(r.ids_t[...] == number.astype(F32), 1.0, 0.0).astype(BF))
        sums = dot(parts, jnp.concatenate(pieces, axis=1))
        sums = sums[:code] + sums[code : 2 * code] + sums[2 * code :]
        for index in range(wide):
            r.stage[(first + index) * code : (first + index + 1) * code, :] = sums[
                :, index * half : (index + 1) * half
            ]
    down = r.down_sum[...].astype(F32)
    codes = r.stage[...]
    r.mine[...] = jnp.where(core == 0, down, codes).astype(BF)
    r.other[...] = jnp.where(core == 0, codes, down).astype(BF)


def run_code_grad(order, ids_t, back_mine, came, down_sum, codes):
    half = down_sum.shape[1]
    rows = codes // half * (back_mine.shape[1] // KS)
    part = (VMEM, shape((rows, half), BF))
    made = call(
        order,
        code_grad_kernel,
        "code_grads",
        vmem_ins(ids_t=ids_t, back_mine=back_mine, came=came, down_sum=down_sum),
        dict(mine=part, other=part),
        dict(stage=pltpu.VMEM((rows, half), F32)),
    )
    return made["mine"], made["other"]


def down_kernel(span, r):
    taps, full, out_half = r.w_down.shape
    width = r.mine.shape[1] // 2
    code = width // taps
    copies = Copies(r.sem)
    loads = {index: copies.start(r.w_down.at[index], r.down_v.at[index - span[0]]) for index in range(*span)}
    core = lax.axis_index(CHAN)
    total = jnp.where(core == 0, r.mine[...].astype(F32), r.got[...].astype(F32))
    sums = jnp.concatenate([total[:, :width], total[:, width:]], axis=0)
    rounded = sums.astype(BF)
    fold = (
        lax.broadcasted_iota(jnp.int32, (code, width), 0)
        == lax.broadcasted_iota(jnp.int32, (code, width), 1) % code
    ).astype(BF)
    latent = dot_rows(r.w_latent[...], fold)
    group = lax.broadcasted_iota(jnp.int32, (out_half, width), 1) // code
    across = sums.T
    product = r.latent_in[...] if hasattr(r, "latent_in") else jnp.zeros((code, out_half), F32)
    outs = []
    for index in range(*span):
        slot = index % 4
        if len(outs) >= 4:
            copies.wait(outs[-4])
        spread = jnp.where(group == index, latent, 0.0).astype(BF)
        r.out_v[slot] = dot_cols(rounded, spread)
        outs.append(copies.start(r.out_v.at[slot], r.grad_down.at[index]))
        copies.wait(loads[index])
        product = product + dot(
            across[index * code : (index + 1) * code, :].astype(BF), r.down_v[index - span[0]]
        )
    r.grad_latent[...] = product
    copies.wait_all()


def run_down(order, span, mine, got, w_latent, w_down, before=None):
    taps, full, out_half = w_down.shape
    count = span[1] - span[0]
    ins = {}
    if before is not None:
        ins.update(any_ins(down_in=before["grad_down"]))
        ins.update(vmem_ins(latent_in=before["grad_latent"]))
    ins.update(vmem_ins(mine=mine, got=got, w_latent=w_latent))
    ins.update(any_ins(w_down=w_down))
    return call(
        order,
        functools.partial(down_kernel, span),
        "down_grads",
        ins,
        dict(
            grad_down=(ANY, shape(w_down.shape, F32)),
            grad_latent=(VMEM, shape(w_latent.shape, F32)),
        ),
        dict(
            down_v=pltpu.VMEM((count, full, out_half), BF),
            out_v=pltpu.VMEM((4, full, out_half), F32),
            sem=DMA((2 * count,)),
        ),
        aliases=None if before is None else {0: 0},
    )


def step_kernel(jobs, r):
    copies = Copies(r.sem) if hasattr(r, "sem") else None
    for job in jobs:
        job.load(r, copies)
    for job in jobs:
        job.run(r, copies)
    if copies is not None:
        copies.wait_all()


class Scatter:
    def __init__(self, name, kept, got, bits, large=False, unit=1, ways=1):
        self.name, self.bits, self.large, self.ways = name, bits, large, ways
        self.kept, self.got = kept, got
        self.spec = ANY if large else VMEM
        self.used = sum(array.shape[0] for array in kept)
        self.shape = (-(-self.used // unit) * unit, kept[0].shape[1])

    def ins(self):
        arrays = {f"kept{self.name}_{index}": array for index, array in enumerate(self.kept)}
        arrays.update({f"got{self.name}_{index}": array for index, array in enumerate(self.got)})
        return {name: (self.spec, array) for name, array in arrays.items()}

    def outs(self):
        part = (self.spec, shape((self.shape[0] // (2 * self.ways), self.shape[1]), BF))
        return {kind + self.name + "w" * way: part for way in range(self.ways) for kind in ("sent", "next")}

    def scratch(self):
        rooms = {"room" + self.name: pltpu.VMEM(self.shape, BF)}
        if self.large:
            rooms["other" + self.name] = pltpu.VMEM(self.shape, BF)
        return rooms

    def copies(self):
        return 2 * len(self.kept) + 2 * self.ways if self.large else 0

    def spans(self):
        start = 0
        for index, array in enumerate(self.kept):
            yield index, slice(start, start + array.shape[0])
            start += array.shape[0]

    def load(self, r, copies):
        self.loads = []
        if self.large:
            for index, rows in self.spans():
                there = pl.ds(rows.start, rows.stop - rows.start)
                for kind, room in (("kept", "room"), ("got", "other")):
                    source = getattr(r, f"{kind}{self.name}_{index}")
                    self.loads.append(copies.start(source, getattr(r, room + self.name).at[there]))

    def add(self, r, room, copies):
        for index, rows in self.spans():
            if self.large:
                copies.wait(*self.loads[2 * index : 2 * index + 2])
                kept, got = room[rows, :], getattr(r, "other" + self.name)[rows, :]
            else:
                kept = getattr(r, f"kept{self.name}_{index}")[...]
                got = getattr(r, f"got{self.name}_{index}")[...]
            room[rows, :] = (kept.astype(F32) + got.astype(F32)).astype(BF)

    def run(self, r, copies):
        room = getattr(r, "room" + self.name)
        self.add(r, room, copies)
        if room.shape[0] > self.used:
            room[self.used :, :] = jnp.zeros((room.shape[0] - self.used, room.shape[1]), BF)
        rows = room.shape[0] // (2 * self.ways)
        side = kept_side(self.bits)
        for way in range(self.ways):
            for kind, which in (("sent", 1 - side), ("next", side)):
                target = getattr(r, kind + self.name + "w" * way)
                here = pl.ds(pl.multiple_of((2 * way + which) * rows, 16), rows)
                if self.large:
                    copies.start(room.at[here], target)
                else:
                    target[...] = room[here, :]


class Reduce(Scatter):
    def outs(self):
        return {"sent" + self.name: (VMEM, shape(self.shape, BF))}

    def scratch(self):
        return {}

    def run(self, r, copies):
        self.add(r, getattr(r, "sent" + self.name), copies)


class Gather(Scatter):
    def outs(self):
        rows, columns = self.shape
        return {"sent" + self.name: (VMEM, shape((2 * rows, columns), BF))}

    def scratch(self):
        return {}

    def run(self, r, copies):
        out = getattr(r, "sent" + self.name)
        rows = out.shape[0] // 2
        side = kept_side(self.bits)
        for kind, which in (("kept", side), ("got", 1 - side)):
            here = pl.ds(pl.multiple_of(which * rows, 16), rows)
            out[here, :] = getattr(r, f"{kind}{self.name}_0")[...]


class Add:
    def __init__(self, name, value, got):
        self.name, self.value, self.got = name, value, got

    def ins(self):
        return vmem_ins(**{"value" + self.name: self.value, "came" + self.name: self.got})

    def outs(self):
        return {"total" + self.name: (VMEM, shape(self.value.shape, self.value.dtype))}

    def scratch(self):
        return {}

    def copies(self):
        return 0

    def load(self, r, copies):
        pass

    def run(self, r, copies):
        total = getattr(r, "value" + self.name)[...].astype(F32) + getattr(r, "came" + self.name)[...].astype(F32)
        getattr(r, "total" + self.name)[...] = total.astype(self.value.dtype)


def hold_kernel(r):
    pass


def run_hold(order, arrays):
    names = [f"part{index}" for index in range(len(arrays))]
    outs = {"out" + name: (ANY, shape(array.shape, array.dtype)) for name, array in zip(names, arrays)}
    made = call(
        order, hold_kernel, "hold", any_ins(**dict(zip(names, arrays))), outs, {},
        aliases={index: index for index in range(len(arrays))},
    )
    return [made["out" + name] for name in names]


def run_step(order, sums):
    jobs = [one.job() for one in sums]
    ins, outs, scratch = {}, {}, {}
    for job in jobs:
        ins.update(job.ins())
        outs.update(job.outs())
        scratch.update(job.scratch())
    copies = sum(job.copies() for job in jobs)
    if copies:
        scratch["sem"] = DMA((copies,))
    made = call(
        order,
        functools.partial(step_kernel, jobs),
        "sum_step",
        ins,
        outs,
        scratch,
        limit=VMEM_LIMIT if copies else SMALL_LIMIT,
    )
    for one in sums:
        one.take(made)


def finish_kernel(pieces, kind, r):
    conv_rows = r.conv.shape[1]
    copies = Copies(r.sem)
    loads, edges = [], []
    for index, (unit, piece) in enumerate(pieces):
        there = pl.ds(piece.place, piece.rows)
        loads.append(copies.start(getattr(r, "part" + piece.name).at[there], getattr(r, f"chunk{index}")))
    for index, (unit, piece) in enumerate(pieces):
        side = kept_side(piece.bits)
        which = side if kind == "part" else 1 - side
        rows = piece.rows
        wide = getattr(r, f"wide{index}")
        copies.wait(loads[index])
        wide[...] = getattr(r, f"chunk{index}")[...].astype(F32)
        if piece.start + piece.span + rows <= conv_rows:
            there = pl.ds(pl.multiple_of(piece.start + which * piece.span, 16), rows)
            copies.start(wide, r.conv.at[unit, there])
            continue
        for choice in range(2):
            start = piece.start + choice * piece.span
            edge = min(max(conv_rows - start, 0), rows)
            parts = []
            if edge > 0:
                parts.append((wide.at[pl.ds(0, edge)], r.conv.at[unit, pl.ds(start, edge)]))
            if edge < rows:
                target = r.point.at[unit, pl.ds(start + edge - conv_rows, rows - edge)]
                parts.append((wide.at[pl.ds(edge, rows - edge)], target))
            made = [
                pltpu.make_async_copy(source, target, r.edge_sem.at[index, number])
                for number, (source, target) in enumerate(parts)
            ]
            edges.append((which == choice, made))

            @pl.when(which == choice)
            def _():
                for copy in made:
                    copy.start()

    for chosen, made in edges:

        @pl.when(chosen)
        def _():
            for copy in made:
                copy.wait()

    copies.wait_all()


def run_finish(order, pieces, kind, arrays, before, full):
    half = arrays[0].shape[1]
    ins = {}
    if before is not None:
        ins.update(any_ins(conv_in=before["conv"], point_in=before["point"]))
    ins.update(any_ins(**{f"part{index}": array for index, array in enumerate(arrays)}))
    scratch = {}
    for index, (_, piece) in enumerate(pieces):
        scratch[f"chunk{index}"] = pltpu.VMEM((piece.rows, half), BF)
        scratch[f"wide{index}"] = pltpu.VMEM((piece.rows, half), F32)
    scratch["sem"] = DMA((2 * len(pieces),))
    scratch["edge_sem"] = DMA((len(pieces), 2))
    return call(
        order,
        functools.partial(finish_kernel, pieces, kind),
        "finish",
        ins,
        dict(
            conv=(ANY, shape((3, K * full, half), F32)),
            point=(ANY, shape((3, full, half), F32)),
        ),
        scratch,
        aliases=None if before is None else {0: 0, 1: 1},
    )


def collect_kernel(r):
    half = r.mine.shape[1]
    code = r.w_expand.shape[0]
    core = lax.axis_index(CHAN)
    own, oth = both_columns(half)
    r.rate_v[...] = jnp.zeros(r.rate_v.shape, F32)
    for index in range(7):
        rate = getattr(r, f"rate{index}")
        r.rate_v[index : index + 1, :] = jnp.sum(rate[...], axis=0, keepdims=True)
    r.mine[:8, :] = r.rate_v[:, own]
    r.other[:8, :] = r.rate_v[:, oth]
    r.other[8:, :] = jnp.zeros((r.other.shape[0] - 8, half), F32)
    blocks, width = r.mixed_mine.shape
    wide = jnp.concatenate([r.w_expand[...].astype(F32)] * (width // code), axis=0).astype(BF)
    lane = lax.broadcasted_iota(jnp.int32, (blocks, width), 1)
    total = jnp.zeros((code, r.out_grad.shape[3]), F32)
    for row, mixed in ((core, r.mixed_mine), (1 - core, r.mixed_got)):
        value = mixed[...]
        once = jnp.where(lane < code, value.astype(F32), 0.0).astype(BF)
        r.block_out[row, 0] = dot(once, wide).astype(BF)
        sums = lax.dot_general(
            value, r.out_grad[row, 0], (((0,), (0,)), ((), ())), preferred_element_type=F32
        )
        total = total + sums[:code, :]
    for index in range(total.shape[1] // half):
        r.mine[8 * (index + 1) : 8 * (index + 2), :] = total[:, index * half : (index + 1) * half]


def run_collect(order, rates, mixed_mine, mixed_got, out_grad, w_expand, half):
    part = (VMEM, shape((8 + 8 * (w_expand.shape[1] // half), half), F32))
    made = call(
        order,
        collect_kernel,
        "collect",
        vmem_ins(
            **{f"rate{index}": rate for index, rate in enumerate(rates)},
            mixed_mine=mixed_mine, mixed_got=mixed_got, out_grad=out_grad, w_expand=w_expand,
        ),
        dict(block_out=(VMEM, shape(out_grad.shape, BF)), mine=part, other=part),
        dict(rate_v=pltpu.VMEM((8, 2 * half), F32)),
        limit=SMALL_LIMIT,
    )
    return made["block_out"], made["mine"], made["other"]


def place_kernel(r):
    core = lax.axis_index(CHAN)
    copies = Copies(r.sem)
    frames = r.got.shape[0]
    moved = [
        (copies.start(r.got.at[there], r.room.at[there]), there) for _, there in tiles_of(frames)
    ]
    for number, there in moved:
        copies.wait(number)
        copies.start(r.room.at[there], r.out.at[1 - core, 0, there])
    copies.wait_all()


def run_place(order, mine, got):
    return call(
        order,
        place_kernel,
        "place_rows",
        any_ins(mine=mine, got=got),
        dict(out=(ANY, shape(mine.shape, mine.dtype))),
        dict(room=pltpu.VMEM(got.shape, got.dtype), sem=DMA((2 * (got.shape[0] // TILE),))),
        aliases={0: 0},
        limit=SMALL_LIMIT,
    )["out"]


def codebook_kernel(r):
    rows, half = r.mine.shape
    code = r.codebook.shape[0]
    core = lax.axis_index(CHAN)
    sums = jnp.where(core == 0, r.got[...].astype(F32), r.mine[...].astype(F32))
    for index in range(rows // code):
        r.total[:, index * half : (index + 1) * half] = sums[index * code : (index + 1) * code, :]
    columns = r.codebook[...]
    scale = lax.rsqrt(jnp.sum(columns * columns, axis=0, keepdims=True) + 1.0)
    unit = columns * scale
    grad = r.total[...]
    r.out[...] = scale * (grad - unit * jnp.sum(unit * grad, axis=0, keepdims=True))


def run_codebook(order, mine, got, codebook):
    return call(
        order,
        codebook_kernel,
        "codebook_grads",
        vmem_ins(mine=mine, got=got, codebook=codebook),
        dict(out=(VMEM, shape(codebook.shape, F32))),
        dict(total=pltpu.VMEM(codebook.shape, F32)),
        limit=SMALL_LIMIT,
    )["out"]


def chip_axes(count):
    bits = count.bit_length() - 1
    side = bits // 3
    return list(range(side)), list(range(side, 2 * side)), list(range(2 * side, bits))


def two_orders(count):
    x, y, z = chip_axes(count)
    back = z[::-1]
    return ((x + y + z, y + x + back), (z + y + x, back + y + x))


def first_unit(count, ways):
    return ways * 8 * count


def piece_plan(full, count):
    orders = two_orders(count)
    rows = (K + 1) * full
    cut = 3 * rows // 4
    first = {2: [], 1: [], 0: []}
    later = []
    for seq, (share, start) in enumerate(((cut // 2, 0), ((rows - cut) // 2, cut))):
        bits = (orders[seq][0][0], orders[seq][1][0])
        place = 0
        for unit in (2, 1, 0):
            first[unit].append(Piece(f"{seq}", start, share, place, bits, share))
            place += share
        ways = 2 - seq
        unit_rows = first_unit(count, ways)
        place = -(-place // unit_rows) * unit_rows
        for unit in (2, 1, 0):
            lo = (2 - unit) * share
            for way in range(ways):
                at = max(lo, way * place // ways)
                stop = min(lo + share, (way + 1) * place // ways)
                if stop > at:
                    name = f"{2 * seq + way}"
                    later.append(
                        (unit, Piece(name, start + at - lo, stop - at, at - way * place // ways, bits, share))
                    )
    return first, later


def exchange(values, count, bits):
    pairs = []
    for chip in range(count):
        for core in range(2):
            pairs.append((2 * chip + core, 2 * (chip ^ (1 << bits[core])) + core))
    return lax.ppermute(values, (DP, CHAN), pairs)


def swap(values):
    return lax.ppermute(values, CHAN, [(0, 1), (1, 0)])


class FirstStep:
    def __init__(self, name, count, cores, ways):
        self.name, self.count, self.ways = name, count, ways
        self.steps = list(zip(*cores))
        self.kept = []
        self.got = []

    def begin(self, sent, kept):
        self.kept.append(kept)
        self.got.append(exchange(sent, self.count, self.steps[0]))

    def job(self):
        unit = first_unit(self.count, self.ways)
        return Scatter("f" + self.name, self.kept, self.got, self.steps[1], True, unit, self.ways)

    def take(self, made):
        self.made = [
            (f"{2 * int(self.name) + way}", made["sentf" + self.name + "w" * way], made["nextf" + self.name + "w" * way])
            for way in range(self.ways)
        ]

    def go_on(self, name, sent, kept):
        return PartSum(name, self.count, self.steps, sent, kept)


class PartSum:
    def __init__(self, name, count, steps, sent, kept):
        self.name, self.count, self.steps = name, count, steps
        self.level = 1
        self.scattering = True
        self.kept = [kept]
        self.send(sent)

    def send(self, sent):
        self.sent = sent
        self.got = [exchange(sent, self.count, self.steps[self.level])]

    def job(self):
        if not self.scattering:
            return Gather(self.name, [self.sent], self.got, self.steps[self.level])
        if self.level + 1 < len(self.steps):
            unit = 16 << (len(self.steps) - 1 - self.level)
            return Scatter(self.name, self.kept, self.got, self.steps[self.level + 1], False, unit)
        return Reduce(self.name, self.kept, self.got, None)

    def take(self, made):
        if not self.scattering:
            self.level -= 1
        elif self.level + 1 < len(self.steps):
            self.level += 1
            self.kept = [made["next" + self.name]]
        else:
            self.scattering = False
        self.send(made["sent" + self.name])

    def ready(self):
        return not self.scattering and self.level == 0


class SmallSum:
    def __init__(self, name, mine, other, count, order):
        self.name, self.count, self.order = name, count, order
        self.value = mine
        self.got = swap(other)
        self.level = 0

    def job(self):
        return Add(self.name, self.value, self.got)

    def take(self, made):
        self.value = made["total" + self.name]
        if self.level < len(self.order):
            bit = self.order[self.level]
            self.got = exchange(self.value, self.count, (bit, bit))
        self.level += 1

    def ready(self):
        return self.level > len(self.order)


def shards(
    frames_in,
    utter_lengths,
    code_ids,
    alpha_first,
    alpha_second,
    alpha_last,
    w_dilated,
    w_point,
    w_down,
    w_latent,
    w_expand,
    codebook,
    out_grad,
):
    count = lax.axis_size(DP)
    half = frames_in.shape[3]
    full = 2 * half
    codes = codebook.shape[1]
    order = Order()

    frames_got = swap(frames_in)
    p_got = swap(w_point)
    w_mine = w_dilated.reshape(3, K * full, half)
    w_got = swap(w_mine)
    alpha_rows = jnp.concatenate([alpha_first, alpha_second, alpha_last[None]], axis=0)
    place = (utter_lengths, alpha_rows, swap(alpha_rows))

    ready = run_prepare(order, w_down, w_latent.T, w_expand, out_grad, code_ids, codebook)
    came = swap(ready["sent"])
    made = run_forward(
        order, place, frames_in, frames_got, w_mine, w_got, w_point, p_got,
        dict(
            sent=ready["sent"], came=came,
            chosen=ready["chosen"], back_mine=ready["back_mine"],
        ),
    )
    seen = [made[f"seen{u}"] for u in range(3)]
    rates = [None] * 5 + [made["rates"], made["last_rates"]]
    grads = [None, None, (made["mine"], swap(made["other"]), made["other"])]
    seen_got = [None, None, swap(seen[2])]
    running, dilated, grad = made["running"], made["dilated"], made["grad"]

    def open_unit(u, grad):
        made = run_opening(
            order, u, place, grads[u][0], grads[u][2], running, grad, dilated, w_mine, w_got, w_point, p_got
        )
        rates[u] = made["rates"]
        if u > 0:
            rates[2 + u] = made["mid_rates"]
            grads[u - 1] = (made["mine"], swap(made["other"]), made["other"])
        return made

    x, y, z = chip_axes(count)
    code_mine, code_sent = run_code_grad(
        order, ready["ids_t"], ready["back_mine"], came, made["down_sum"], codes
    )
    codes_sum = SmallSum("", code_mine, code_sent, count, z[::-1] + y + x)
    plan, later = piece_plan(full, count)
    firsts = [
        FirstStep(f"{index}", count, cores, 2 - index) for index, cores in enumerate(two_orders(count))
    ]

    def weigh(u):
        made = run_weight(
            order, u, place, seen[u], seen_got[u], grads[u][0], grads[u][1], plan[u],
            (codes_sum.value, codes_sum.got) if u > 0 else None,
        )
        if u > 0:
            codes_sum.take(made)
        for index, one in enumerate(firsts):
            one.begin(made[f"sent{index}"], made[f"kept{index}"])

    grad = open_unit(2, grad)["grad"]
    seen_got[1] = swap(seen[1])
    order.before += [seen_got[1]]
    weigh(2)
    first = [one.got[0] for one in firsts]
    grad = open_unit(1, grad)["grad"]
    seen_got[0] = swap(seen[0])
    mixed_got = swap(made["mixed"])
    order.before += first + [seen_got[0], mixed_got]
    weigh(1)
    weigh(0)
    order.before += [one.got[1] for one in firsts] + [codes_sum.got]
    last = open_unit(0, grad)
    run_step(order, firsts + [codes_sum])
    (name0, sent0, kept0), (name1, sent1, kept1) = firsts[0].made
    [(name2, sent2, kept2)] = firsts[1].made
    sums = [firsts[0].go_on(name0, sent0, kept0)]
    sent1, sent2, frames_sent = run_hold(order, [sent1, sent2, last["frames_sent"]])
    sums += [firsts[0].go_on(name1, sent1, kept1), firsts[1].go_on(name2, sent2, kept2)]

    def advance(*more):
        if not sums[0].scattering:
            order.before.append(swap(sums[0].got[0][:16]))
        run_step(order, sums[:1])
        run_step(order, sums[1:] + [one for one in more if not one.ready()])

    block_out, small_mine, small_other = run_collect(
        order, rates, made["mixed"], mixed_got, out_grad, w_expand, half
    )
    small = SmallSum("small", small_mine, small_other, count, z + y + x)
    grad_frames = run_place(order, last["frames_mine"], swap(frames_sent))
    while not (codes_sum.ready() or sums[0].ready()):
        advance(codes_sum, small)
    codes_back = swap(codes_sum.value)
    advance(small)
    grad_codebook = run_codebook(order, codes_sum.value, codes_back, codebook)
    taps = w_down.shape[0]
    advance(small)
    downs = run_down(order, (0, taps // 2), codes_sum.value, codes_back, w_latent.T, w_down)
    while not sums[0].ready():
        advance(small)
    parts, gots = [one.sent for one in sums], [one.got[0] for one in sums]
    written = run_finish(order, later, "part", parts, None, full)
    soon = [(unit, piece) for unit, piece in later if piece.name == "0"]
    written = run_finish(order, soon, "got", gots[:1], written, full)
    downs = run_down(order, (taps // 2, taps), codes_sum.value, codes_back, w_latent.T, w_down, downs)
    while not small.ready():
        run_step(order, [small])
    rest = [(unit, piece) for unit, piece in later if piece.name != "0"]
    written = run_finish(order, rest, "got", gots, written, full)
    grad_w_dilated, grad_w_point = written["conv"], written["point"]
    small = small.value
    return (
        block_out,
        grad_frames,
        small[0:3],
        small[3:6],
        small[6],
        grad_w_dilated.reshape(3, K, full, half),
        grad_w_point,
        downs["grad_down"],
        downs["grad_latent"].T,
        jnp.concatenate(
            [small[start : start + 8] for start in range(8, small.shape[0], 8)], axis=1
        ),
        grad_codebook,
    )


def solution(mesh):
    placed = (
        P(None, DP, None, CHAN),
        P(None, DP, None),
        P(None, DP, None),
        P(None, CHAN),
        P(None, CHAN),
        P(CHAN),
        P(None, None, None, CHAN),
        P(None, None, CHAN),
        P(None, None, CHAN),
        P(CHAN, None),
        P(None, CHAN),
        P(),
        P(None, DP, None, CHAN),
    )
    return jax.shard_map(
        shards,
        mesh=mesh,
        in_specs=placed,
        out_specs=(
            P(None, DP, None, CHAN),
            P(None, DP, None, CHAN),
            P(None, CHAN),
            P(None, CHAN),
            P(CHAN),
            P(None, None, None, CHAN),
            P(None, None, CHAN),
            P(None, None, CHAN),
            P(CHAN, None),
            P(None, CHAN),
            P(),
        ),
        check_vma=False,
    )
```

```python
import functools
import types
import jax
import jax.numpy as jnp
from jax import lax
from jax.experimental import pallas as pl
from jax.experimental.pallas import tpu as pltpu
from jax.sharding import PartitionSpec as P

DP = "dp"
CHAN = "chan"
K = 7
STRIDE = 8
KS = 16
DILATIONS = (1, 3, 9)
BF = jnp.bfloat16
F32 = jnp.float32
HALO = 32
TILE = 512
LANES = 128
SINE = (3.141592580569316, -5.1677069002071025, 2.550031640919103, -0.5980464504720939, 0.0772222489218058)
COSINE = (0.9999999534666402, -4.934792858671753, 4.058411914096722, -1.3318801607983635, 0.2196967977026182)
VMEM_LIMIT = 65280 * 1024
SMALL_LIMIT = 16 * 1024 * 1024
COST = dict(prepare=9, forward=36, code_grads=3, weight_grads=10, opening=15)
ANY = pl.BlockSpec(memory_space=pl.ANY)
SMEM = pl.BlockSpec(memory_space=pltpu.SMEM)
VMEM = pl.BlockSpec(memory_space=pltpu.VMEM)
DMA = pltpu.SemaphoreType.DMA


def shape(dims, kind):
    return jax.ShapeDtypeStruct(dims, kind)


class Order:
    def __init__(self):
        self.token = None
        self.before = []


def call(order, kernel, name, ins, outs, scratch, aliases=None, limit=VMEM_LIMIT):
    deps = ([] if order.token is None else [order.token]) + order.before
    order.before = []

    def body(*refs):
        refs = list(refs)
        named = dict(zip(ins, refs))
        refs = refs[len(ins) + len(deps) :]
        named.update(zip(outs, refs))
        refs[len(outs)][...] = jnp.zeros((8, LANES), F32)
        named.update(zip(scratch, refs[len(outs) + 1 :]))
        kernel(types.SimpleNamespace(**named))

    token = shape((8, LANES), F32)
    made = pl.pallas_call(
        body,
        out_shape=[out for _, out in outs.values()] + [token],
        in_specs=[spec for spec, _ in ins.values()] + [ANY] * len(deps),
        out_specs=[spec for spec, _ in outs.values()] + [VMEM],
        scratch_shapes=list(scratch.values()),
        input_output_aliases=aliases or {},
        compiler_params=pltpu.CompilerParams(vmem_limit_bytes=limit),
        cost_estimate=pl.CostEstimate(
            flops=COST.get(name, 0) << 30, bytes_accessed=COST.get(name, 0) * 3500000, transcendentals=0
        ),
        name=name,
    )(*[array for _, array in ins.values()], *deps)
    order.token = made[-1]
    return dict(zip(outs, made))


class Copies:
    def __init__(self, sem):
        self.sem = sem
        self.made = []
        self.done = set()

    def start(self, source, target):
        copy = pltpu.make_async_copy(source, target, self.sem.at[len(self.made)])
        copy.start()
        self.made.append(copy)
        return len(self.made) - 1

    def wait(self, *numbers):
        for number in numbers:
            if number not in self.done:
                self.done.add(number)
                self.made[number].wait()

    def wait_all(self):
        self.wait(*range(len(self.made)))


def dot(left, right):
    return jnp.dot(left, right, preferred_element_type=F32)


def dot_cols(left, right):
    return lax.dot_general(left, right, (((1,), (1,)), ((), ())), preferred_element_type=F32)


def dot_rows(left, right):
    return lax.dot_general(left, right, (((0,), (0,)), ((), ())), preferred_element_type=F32)


def poly(u, terms):
    total = terms[-1]
    for term in terms[-2::-1]:
        total = total * u + term
    return total


def half_turns(v, alpha):
    turns = v * (alpha * 0.3183098861837907)
    return turns - jnp.round(turns)


def snake(v, alpha):
    t = half_turns(v, alpha)
    u = t * t
    p = poly(u, SINE)
    return v + (u * (p * p)) * (1.0 / alpha)


def snake_slopes(v, alpha):
    t = half_turns(v, alpha)
    u = t * t
    sine = t * poly(u, SINE)
    double = 2.0 * sine * poly(u, COSINE)
    return sine * sine, double


def ends_of(lengths, row):
    ends = []
    total = 0
    for utt in range(lengths.shape[2]):
        total = total + lengths[row, 0, utt] * STRIDE
        ends.append(total)
    return ends


def put_labels(label_ref, ends, frames):
    t = lax.broadcasted_iota(jnp.int32, label_ref.shape, 0) - HALO
    label = jnp.zeros(label_ref.shape, jnp.int32)
    for end in ends:
        label = label + (t >= end).astype(jnp.int32)
    label_ref[...] = jnp.where((t < 0) | (t >= frames), -1, label)


def put_edges(padded_ref, frames):
    edge = jnp.zeros((HALO, padded_ref.shape[1]), F32)
    padded_ref[:HALO, :] = edge
    padded_ref[HALO + frames :, :] = edge


def tap(padded_ref, label_ref, row, rows, offset):
    here = HALO + row
    width = padded_ref.shape[1]
    same = label_ref[here + offset : here + offset + rows, :] == label_ref[here : here + rows, :]
    pieces = []
    for lane in range(0, width, LANES):
        piece = padded_ref[here + offset : here + offset + rows, lane : lane + LANES]
        pieces.append(jnp.where(same, piece, 0.0).astype(BF))
    return jnp.concatenate(pieces, axis=1)


def column_half(core, half):
    return pl.ds(pl.multiple_of(core * half, half), half)


def both_columns(half):
    core = lax.axis_index(CHAN)
    return column_half(core, half), column_half(1 - core, half)


def put_row(target, mine, other, index, own, oth):
    half = mine.shape[1]
    target[:, own] = jnp.broadcast_to(mine[index : index + 1, :], (8, half))
    target[:, oth] = jnp.broadcast_to(other[index : index + 1, :], (8, half))
    return target[0:1, :]


def split(values, terms):
    parts = []
    for _ in range(terms):
        part = values.astype(BF)
        parts.append(part)
        values = values - part.astype(F32)
    return parts


def row_sums(values):
    return jnp.sum(values.reshape(values.shape[0] // 8, 8, values.shape[1]), axis=0)


def tiles_of(frames):
    return [(slice(start, start + TILE), pl.ds(start, TILE)) for start in range(0, frames, TILE)]


def forward_kernel(r):
    frames, full = r.run_v.shape[1:]
    half = full // 2
    core = lax.axis_index(CHAN)
    own, oth = both_columns(half)
    copies = Copies(r.sem)
    tiles = tiles_of(frames)
    place = [
        copies.start(r.lengths, r.lengths_v),
        copies.start(r.alpha_mine, r.alpha_mv),
        copies.start(r.alpha_other, r.alpha_ov),
    ]
    loads = [copies.start(r.frames_in.at[core, 0], r.mine_v), copies.start(r.frames_got.at[core, 0], r.other_v)]

    def load_weights(unit):
        return [
            copies.start(r.w_mine.at[unit], r.w_v.at[unit % 2, 0]),
            copies.start(r.w_other.at[unit], r.w_v.at[unit % 2, 1]),
        ]

    weights = [load_weights(0)]
    points = [copies.start(r.p_mine, r.pm_v), copies.start(r.p_other, r.po_v)]
    weights.append(load_weights(1))
    small = [
        copies.start(source, target)
        for source, target in (
            (r.sent.at[pl.ds(0, full)], r.dm_v), (r.came.at[pl.ds(0, full)], r.do_v),
            (r.chosen, r.chosen_v), (r.back_mine, r.bm_v),
            (r.came.at[pl.ds(full, r.bo_v.shape[0])], r.bo_v),
        )
    ]
    put_edges(r.padded, frames)
    copies.wait(*place)
    put_labels(r.label, ends_of(r.lengths_v, core), frames)
    copies.wait(*loads)
    leaving = {(kind, slot): [] for kind in ("run", "mid", "seen") for slot in range(2)}

    def settle(kind, slot):
        copies.wait(*leaving[kind, slot])
        leaving[kind, slot] = []

    for unit in range(3):
        now, later = r.run_v.at[unit % 2], r.run_v.at[(unit + 1) % 2]
        mid = r.mid_v.at[unit % 2]
        seen = r.seen_v.at[unit % 2]
        rate_in = put_row(r.rate_v.at[unit], r.alpha_mv, r.alpha_ov, unit, own, oth)
        rate_mid = put_row(r.rate_v.at[3 + unit], r.alpha_mv, r.alpha_ov, 3 + unit, own, oth)
        settle("seen", unit % 2)
        for rows, there in tiles:
            if unit == 0:
                now[rows, own] = r.mine_v[rows, :].astype(F32)
                now[rows, oth] = r.other_v[rows, :].astype(F32)
                leaving["run", 0].append(copies.start(now.at[there], r.running.at[unit, there]))
            opened = snake(now[rows, :], rate_in)
            r.padded[HALO + rows.start : HALO + rows.stop, :] = opened
            seen[:full, rows] = opened.T.astype(BF)
        seen_out = getattr(r, f"seen{unit}")
        leaving["seen", unit % 2].append(
            copies.start(seen.at[pl.ds(0, full)], seen_out.at[pl.ds(0, full)])
        )
        copies.wait(*weights[unit])
        if unit == 0:
            copies.wait(*points)
        settle("mid", unit % 2)
        settle("run", (unit + 1) % 2)
        for place_of, (rows, there) in enumerate(tiles):
            taps = r.taps.at[place_of % 2]
            for index in range(K):
                offset = DILATIONS[unit] * (index - K // 2)
                taps[:, index * full : (index + 1) * full] = tap(
                    r.padded, r.label, rows.start, TILE, offset
                )
            mid[rows, own] = dot(taps[...], r.w_v[unit % 2, 0])
            mid[rows, oth] = dot(taps[...], r.w_v[unit % 2, 1])
            if unit < 2:
                leaving["mid", unit % 2].append(copies.start(mid.at[there], r.dilated.at[unit, there]))
            closed = snake(mid[rows, :], rate_mid)
            seen[full:, rows] = closed.T.astype(BF)
            closed = closed.astype(BF)
            later[rows, own] = now[rows, own] + dot(closed, r.pm_v[unit])
            later[rows, oth] = now[rows, oth] + dot(closed, r.po_v[unit])
            if unit < 2:
                leaving["run", (unit + 1) % 2].append(
                    copies.start(later.at[there], r.running.at[unit + 1, there])
                )
        leaving["seen", unit % 2].append(
            copies.start(seen.at[pl.ds(full, full)], seen_out.at[pl.ds(full, full)])
        )
        if unit == 0:
            weights.append(load_weights(2))

    running, mid = r.run_v.at[1], r.mid_v.at[0]
    blocks = frames // STRIDE
    value = put_row(r.rate_v.at[6], r.alpha_mv, r.alpha_ov, 6, own, oth)
    mid_value = r.rate_v[5, 0:1, :]
    inverse = 1.0 / value
    copies.wait(*small)
    width = r.dm_v.shape[1]
    code = width // KS
    lane = lax.broadcasted_iota(jnp.int32, (TILE, width), 1) // code
    step = lax.broadcasted_iota(jnp.int32, (TILE, width), 0) % STRIDE
    pattern = (lane % STRIDE == (step + STRIDE // 2) % STRIDE).astype(F32)
    down = r.dm_v[...] + r.do_v[...]
    down_parts = jnp.concatenate(split(down, 2), axis=1)
    sums = []
    for rows, _ in tiles:
        v = running[rows, :]
        square, double = snake_slopes(v, value)
        r.square_v[rows, :] = square
        r.double_v[rows, :] = double
        opened = (v + square * inverse).astype(BF)
        r.opened_v[rows, :] = opened
        products = dot(opened, down_parts)
        products = products[:, :width] + products[:, width:]
        products = (products * pattern).reshape(TILE // STRIDE, STRIDE, width)
        sums.append(jnp.sum(products, axis=1))
    sums = jnp.concatenate(sums, axis=0)
    block = lax.broadcasted_iota(jnp.int32, (blocks, width), 0)
    block_lane = lax.broadcasted_iota(jnp.int32, (blocks, width), 1)
    label = jnp.zeros((blocks, width), jnp.int32)
    for end in ends_of(r.lengths_v, core):
        label = label + (block * STRIDE >= end).astype(jnp.int32)

    def earlier(values):
        return pltpu.roll(values, 1, 0)

    def later_rows(values):
        return pltpu.roll(values, blocks - 1, 0)

    same_before = jnp.where((block > 0) & (earlier(label) == label), 1.0, 0.0)
    same_after = jnp.where((block < blocks - 1) & (later_rows(label) == label), 1.0, 0.0)
    early = block_lane < 4 * code
    late = block_lane >= 12 * code
    sums = jnp.where(
        early, same_before * earlier(sums), jnp.where(late, same_after * later_rows(sums), sums)
    )
    fold = (
        lax.broadcasted_iota(jnp.int32, (width, width), 0) % code
        == lax.broadcasted_iota(jnp.int32, (width, width), 1) % code
    ).astype(BF)
    latent = dot(jnp.concatenate(split(sums, 3), axis=1), jnp.concatenate([fold] * 3, axis=0))
    scale = lax.rsqrt(jnp.sum(latent * latent, axis=1, keepdims=True) * (1.0 / KS) + 1.0)
    unit_code = latent * scale
    r.mixed[...] = (unit_code + r.chosen_v[...]).astype(BF)
    back = r.bm_v[...] + r.bo_v[...]
    along = jnp.sum(unit_code * back, axis=1, keepdims=True) * (1.0 / KS)
    spread = (back - unit_code * along) * scale
    spread = jnp.where(
        early,
        later_rows(same_before * spread),
        jnp.where(late, earlier(same_after * spread), spread),
    )
    down_t_parts = split(down.T, 2)
    down_t_stack = jnp.concatenate([down_t_parts[0], down_t_parts[1], down_t_parts[0]], axis=0)
    total = jnp.zeros((8, full), F32)
    last_total = jnp.zeros((8, full), F32)
    down_total = jnp.zeros(down.shape, F32)
    for rows, there in tiles:
        own_blocks = spread[rows.start // STRIDE : rows.stop // STRIDE, :]
        wide = jnp.broadcast_to(
            own_blocks[:, None, :], (TILE // STRIDE, STRIDE, width)
        ).reshape(TILE, width) * pattern
        parts = split(wide, 2)
        sums = lax.dot_general(
            r.opened_v[rows, :],
            jnp.concatenate(parts, axis=1),
            (((0,), (0,)), ((), ())),
            preferred_element_type=F32,
        )
        down_total = down_total + (sums[:, :width] + sums[:, width:])
        grad_last = dot(jnp.concatenate([parts[0], parts[0], parts[1]], axis=1), down_t_stack)
        square = r.square_v[rows, :]
        double = r.double_v[rows, :]
        grad = grad_last * (1.0 + double)
        r.grad_v[rows, :] = grad
        copies.start(r.grad_v.at[there], r.grad.at[there])
        rate = grad_last * (running[rows, :] * double - square * inverse)
        last_total = last_total + row_sums(rate)
        total = total + closing_steps(
            r, rows, grad, mid[rows, :], mid_value, (own, oth), r.pm_v[2], r.po_v[2]
        )
        send_closing(r, copies, rows, there, own, oth)
    r.rates[...] = total * (1.0 / mid_value)
    r.last_rates[...] = last_total * inverse
    r.down_sum[:, :width] = down_total[:half, :].astype(BF)
    r.down_sum[:, width:] = down_total[half:, :].astype(BF)
    copies.wait_all()


def closing_steps(r, rows, point, mid, alpha, core_cols, p_mine, p_other):
    own, oth = core_cols
    r.gp_v[rows, :] = point.astype(BF)
    grad = dot_cols(r.gp_v[rows, own], p_mine) + dot_cols(r.gp_v[rows, oth], p_other)
    square, double = snake_slopes(mid, alpha)
    r.gd_v[rows, :] = (grad * (1.0 + double)).astype(BF)
    return row_sums(grad * (mid * double - square * (1.0 / alpha)))


def send_closing(r, copies, rows, there, own, oth):
    frames = r.gp_v.shape[0]
    after = pl.ds(frames + rows.start, TILE)
    copies.start(r.gp_v.at[there, own], r.mine.at[there])
    copies.start(r.gd_v.at[there, own], r.mine.at[after])
    copies.start(r.gp_v.at[there, oth], r.other.at[there])
    copies.start(r.gd_v.at[there, oth], r.other.at[after])


def place_ins(place):
    return {name: (ANY, array) for name, array in zip(("lengths", "alpha_mine", "alpha_other"), place)}


def place_rooms(place, full):
    lengths, alpha, _ = place
    return dict(
        lengths_v=pltpu.SMEM(lengths.shape, jnp.int32),
        alpha_mv=pltpu.VMEM(alpha.shape, F32),
        alpha_ov=pltpu.VMEM(alpha.shape, F32),
        rate_v=pltpu.VMEM((7, 8, full), F32),
    )


def any_ins(**arrays):
    return {name: (ANY, array) for name, array in arrays.items()}


def vmem_ins(**arrays):
    return {name: (VMEM, array) for name, array in arrays.items()}


def run_forward(order, place, frames_in, frames_got, w_mine, w_other, p_mine, p_other, small):
    frames, half = frames_in.shape[2:]
    full = 2 * half
    tiles = frames // TILE
    blocks = frames // STRIDE
    width = small["chosen"].shape[1]
    wide = (frames, full)
    pair = (ANY, shape((2 * frames, half), BF))
    square = pltpu.VMEM((blocks, width), F32)
    tall = pltpu.VMEM((full, width), F32)
    return call(
        order,
        forward_kernel,
        "forward",
        dict(
            **place_ins(place),
            **any_ins(frames_in=frames_in, frames_got=frames_got, w_mine=w_mine, w_other=w_other,
                      p_mine=p_mine, p_other=p_other, **small),
        ),
        dict(
            running=(ANY, shape((3,) + wide, F32)),
            dilated=(ANY, shape((2,) + wide, F32)),
            seen0=(ANY, shape((2 * full, frames), BF)),
            seen1=(ANY, shape((2 * full, frames), BF)),
            seen2=(ANY, shape((2 * full, frames), BF)),
            grad=(ANY, shape(wide, F32)),
            mixed=(VMEM, shape((blocks, width), BF)),
            down_sum=(VMEM, shape((half, 2 * width), BF)),
            last_rates=(VMEM, shape((8, full), F32)),
            mine=pair,
            other=pair,
            rates=(VMEM, shape((8, full), F32)),
        ),
        dict(
            **place_rooms(place, full),
            mine_v=pltpu.VMEM((frames, half), BF),
            other_v=pltpu.VMEM((frames, half), BF),
            run_v=pltpu.VMEM((2,) + wide, F32),
            mid_v=pltpu.VMEM((2,) + wide, F32),
            seen_v=pltpu.VMEM((2, 2 * full, frames), BF),
            padded=pltpu.VMEM((frames + 2 * HALO, full), F32),
            label=pltpu.VMEM((frames + 2 * HALO, LANES), jnp.int32),
            taps=pltpu.VMEM((2, TILE, K * full), BF),
            w_v=pltpu.VMEM((2, 2) + w_mine.shape[1:], BF),
            pm_v=pltpu.VMEM(p_mine.shape, BF),
            po_v=pltpu.VMEM(p_mine.shape, BF),
            dm_v=tall, do_v=tall, chosen_v=square, bm_v=square, bo_v=square,
            opened_v=pltpu.VMEM(wide, BF),
            square_v=pltpu.VMEM(wide, F32),
            double_v=pltpu.VMEM(wide, F32),
            grad_v=pltpu.VMEM(wide, F32),
            gp_v=pltpu.VMEM(wide, BF),
            gd_v=pltpu.VMEM(wide, BF),
            sem=DMA((3 + 2 + 6 + 2 + 5 + 5 * tiles + 6 + 5 * tiles,)),
        ),
    )


def weight_kernel(unit, pieces, r):
    frames = r.padded.shape[1] - 2 * HALO
    half = r.padded.shape[2]
    full = 2 * half
    core = lax.axis_index(CHAN)
    copies = Copies(r.sem)
    place = copies.start(r.lengths, r.lengths_v)
    grads = []
    for row, source in enumerate((r.grads_mine, r.grads_got)):
        grads.append(copies.start(source.at[pl.ds(frames, frames)], r.gd_v.at[row]))
    opened = []
    for row, source in enumerate((r.seen_mine, r.seen_got)):
        columns = pl.ds(row * frames, frames)
        opened.append(copies.start(source.at[pl.ds(0, full)], r.seen_v.at[pl.ds(0, full), columns]))
    points = []
    for row, (source, seen) in enumerate(((r.grads_mine, r.seen_mine), (r.grads_got, r.seen_got))):
        columns = pl.ds(row * frames, frames)
        points.append(copies.start(source.at[pl.ds(0, frames)], r.gp_v.at[columns]))
        points.append(copies.start(seen.at[pl.ds(full, full)], r.seen_v.at[pl.ds(full, full), columns]))
    if hasattr(r, "value"):
        beside = [copies.start(r.value, r.value_v), copies.start(r.came, r.came_v)]
    for row in range(2):
        put_edges(r.padded.at[row], frames)
    copies.wait(place)
    for row in range(2):
        put_labels(r.label.at[row], ends_of(r.lengths_v, core if row == 0 else 1 - core), frames)
    for row in range(2):
        copies.wait(grads[row])
        r.padded[row, HALO : HALO + frames, :] = r.gd_v[row].astype(F32)
    copies.wait(*opened)
    waiting = list(pieces)

    def send_pieces(rows):
        for piece in [piece for piece in waiting if piece.start + 2 * piece.rows <= rows]:
            waiting.remove(piece)
            side = kept_side(piece.bits)
            for kind, which in (("sent", 1 - side), ("kept", side)):
                here = pl.ds(pl.multiple_of(piece.start + which * piece.rows, 16), piece.rows)
                copies.start(r.out_v.at[here], getattr(r, kind + piece.name))

    for index in range(K):
        offset = -DILATIONS[unit] * (index - K // 2)
        taps = r.taps.at[index % 2]
        for row in range(2):
            for start in range(0, frames, TILE):
                taps[row * frames + start : row * frames + start + TILE, :] = tap(
                    r.padded.at[row], r.label.at[row], start, TILE, offset
                )
        r.out_v[index * full : (index + 1) * full, :] = dot(r.seen_v[:full, :], taps[...]).astype(BF)
        send_pieces((index + 1) * full)
    if hasattr(r, "value"):
        copies.wait(*beside)
        total = r.value_v[...].astype(F32) + r.came_v[...].astype(F32)
        r.value_v[...] = total.astype(BF)
        copies.start(r.value_v, r.total)
    copies.wait(*points)
    r.out_v[K * full : (K + 1) * full, :] = dot(r.seen_v[full:, :], r.gp_v[...]).astype(BF)
    send_pieces((K + 1) * full)
    copies.wait_all()


def kept_side(bits):
    bit = jnp.where(lax.axis_index(CHAN) == 0, bits[0], bits[1])
    return lax.shift_right_logical(lax.axis_index(DP), bit) & 1


class Piece:
    def __init__(self, name, start, rows, place, bits, span):
        self.name, self.start, self.rows, self.place, self.bits, self.span = name, start, rows, place, bits, span


def run_weight(order, unit, place, seen_mine, seen_got, grads_mine, grads_got, pieces, beside=None):
    frames, half = grads_mine.shape[0] // 2, grads_mine.shape[1]
    full = 2 * half
    ins = any_ins(lengths=place[0], seen_mine=seen_mine, seen_got=seen_got,
                  grads_mine=grads_mine, grads_got=grads_got)
    scratch = dict(
        lengths_v=pltpu.SMEM(place[0].shape, jnp.int32),
        seen_v=pltpu.VMEM((2 * full, 2 * frames), BF),
        gd_v=pltpu.VMEM((2, frames, half), BF),
        gp_v=pltpu.VMEM((2 * frames, half), BF),
        padded=pltpu.VMEM((2, frames + 2 * HALO, half), F32),
        label=pltpu.VMEM((2, frames + 2 * HALO, LANES), jnp.int32),
        taps=pltpu.VMEM((2, 2 * frames, half), BF),
        out_v=pltpu.VMEM(((K + 1) * full, half), BF),
        sem=DMA((12 + 2 * len(pieces),)),
    )
    outs = {
        kind + piece.name: (ANY, shape((piece.rows, half), BF))
        for piece in pieces
        for kind in ("sent", "kept")
    }
    if beside is not None:
        value, came = beside
        ins.update(any_ins(value=value, came=came))
        outs["total"] = (ANY, shape(value.shape, BF))
        scratch.update(value_v=pltpu.VMEM(value.shape, BF), came_v=pltpu.VMEM(value.shape, BF))
    return call(
        order, functools.partial(weight_kernel, unit, pieces), "weight_grads", ins, outs, scratch
    )


def opening_kernel(unit, r):
    last = unit == 0
    frames, full = r.running_v.shape
    half = full // 2
    core = lax.axis_index(CHAN)
    own, oth = both_columns(half)
    copies = Copies(r.sem)
    tiles = tiles_of(frames)
    place = [
        copies.start(r.lengths, r.lengths_v),
        copies.start(r.alpha_mine, r.alpha_mv),
        copies.start(r.alpha_other, r.alpha_ov),
    ]
    after = pl.ds(frames, frames)
    grads = [
        copies.start(r.grads_mine.at[after], r.gm_v),
        copies.start(r.grads_other.at[after], r.go_v),
    ]
    weights = [
        copies.start(r.w_mine.at[unit], r.w_v.at[0]),
        copies.start(r.w_other.at[unit], r.w_v.at[1]),
    ]
    if not last:
        points = [
            copies.start(r.p_mine.at[unit - 1], r.pm_v),
            copies.start(r.p_other.at[unit - 1], r.po_v),
        ]
    loads = []
    for _, there in tiles:
        loads.append([
            copies.start(r.running.at[unit, there], r.running_v.at[there]),
            copies.start(r.grad_in.at[there], r.grad_v.at[there]),
        ])
        if not last:
            loads[-1].append(copies.start(r.dilated.at[unit - 1, there], r.mid_v.at[there]))
    for part in range(2):
        put_edges(r.padded.at[part], frames)
    copies.wait(*place)
    put_labels(r.label, ends_of(r.lengths_v, core), frames)
    value = put_row(r.rate_v.at[0], r.alpha_mv, r.alpha_ov, unit, own, oth)
    if not last:
        mid_value = put_row(r.rate_v.at[1], r.alpha_mv, r.alpha_ov, 2 + unit, own, oth)
    for part, values in ((0, r.gm_v), (1, r.go_v)):
        copies.wait(grads[part])
        r.padded[part, HALO : HALO + frames, :] = values[...].astype(F32)
    for part in range(2):
        copies.wait(weights[part])
        for index in range(K):
            r.turned_v[(2 * index + part) * half : (2 * index + part + 1) * half, :] = r.w_v[
                part, index * full : (index + 1) * full, :
            ].T
    if not last:
        copies.wait(*points)
    total = jnp.zeros((8, full), F32)
    mid_total = jnp.zeros((8, full), F32)
    for place_of, (rows, there) in enumerate(tiles):
        taps = r.taps.at[place_of % 2]
        for index in range(K):
            offset = -DILATIONS[unit] * (index - K // 2)
            for part in range(2):
                start = (2 * index + part) * half
                taps[:, start : start + half] = tap(
                    r.padded.at[part], r.label, rows.start, TILE, offset
                )
        opened = dot(taps[...], r.turned_v[...])
        copies.wait(*loads[place_of])
        v = r.running_v[rows, :]
        square, double = snake_slopes(v, value)
        grad = r.grad_v[rows, :] + opened * (1.0 + double)
        r.grad_v[rows, :] = grad
        total = total + row_sums(opened * (v * double - square * (1.0 / value)))
        if last:
            copies.start(r.grad_v.at[there, own], r.frames_mine.at[core, 0, there])
            copies.start(r.grad_v.at[there, oth], r.frames_sent.at[there])
        else:
            copies.start(r.grad_v.at[there], r.grad.at[there])
            mid_total = mid_total + closing_steps(
                r, rows, grad, r.mid_v[rows, :], mid_value, (own, oth), r.pm_v[...], r.po_v[...]
            )
            send_closing(r, copies, rows, there, own, oth)
    r.rates[...] = total * (1.0 / value)
    if not last:
        r.mid_rates[...] = mid_total * (1.0 / mid_value)
    copies.wait_all()


def run_opening(order, unit, place, grads_mine, grads_other, running, grad, dilated, w_mine, w_other, p_mine, p_other):
    frames, full = grad.shape
    half = full // 2
    tiles = frames // TILE
    last = unit == 0
    wide = pltpu.VMEM((frames, full), F32)
    narrow = pltpu.VMEM((frames, full), BF)
    part = pltpu.VMEM((frames, half), BF)
    point = pltpu.VMEM(p_mine.shape[1:], BF)
    pair = (ANY, shape((2 * frames, half), BF))
    rates = (VMEM, shape((8, full), F32))
    ins = dict(
        **place_ins(place),
        **any_ins(grads_mine=grads_mine, grads_other=grads_other, running=running, grad_in=grad,
                  w_mine=w_mine, w_other=w_other),
    )
    outs = dict(rates=rates)
    scratch = dict(
        **place_rooms(place, full),
        gm_v=part, go_v=part,
        padded=pltpu.VMEM((2, frames + 2 * HALO, half), F32),
        label=pltpu.VMEM((frames + 2 * HALO, LANES), jnp.int32),
        running_v=wide, grad_v=wide,
        w_v=pltpu.VMEM((2,) + w_mine.shape[1:], BF),
        turned_v=pltpu.VMEM((K * full, full), BF),
        taps=pltpu.VMEM((2, TILE, K * full), BF),
    )
    if last:
        outs["frames_mine"] = (ANY, shape((2, 1, frames, half), F32))
        outs["frames_sent"] = (ANY, shape((frames, half), F32))
    else:
        ins.update(any_ins(dilated=dilated, p_mine=p_mine, p_other=p_other))
        outs.update(grad=(ANY, shape((frames, full), F32)), mine=pair, other=pair, mid_rates=rates)
        scratch.update(mid_v=wide, pm_v=point, po_v=point, gp_v=narrow, gd_v=narrow)
    scratch["sem"] = DMA((3 + 2 + 2 + 2 + 8 * tiles,))
    return call(
        order, functools.partial(opening_kernel, unit), "opening", ins, outs, scratch
    )


def prepare_kernel(r):
    taps, full, out_half = r.w_down.shape
    code, codes = r.codebook.shape
    blocks = r.ids.shape[2]
    width = taps * code
    core = lax.axis_index(CHAN)
    copies = Copies(r.sem)
    first = [copies.start(r.ids.at[core], r.ids_v), copies.start(r.codebook, r.book_v)]
    loads = [copies.start(r.w_down.at[index], r.down_v.at[index]) for index in range(taps)]
    copies.wait(*first)
    mark = r.ids_v[...]
    total = jnp.zeros((3 * code, blocks), F32)
    step = 1024
    for start in range(0, codes, step):
        columns = r.book_v[:, start : start + step]
        unit = columns * lax.rsqrt(jnp.sum(columns * columns, axis=0, keepdims=True) + 1.0)
        parts = jnp.concatenate([part.astype(F32) for part in split(unit, 3)], axis=0).astype(BF)
        number = lax.broadcasted_iota(jnp.int32, (step, blocks), 0) + start
        total = total + dot(parts, jnp.where(number == mark, 1.0, 0.0).astype(BF))
    picked = total[:code] + total[code : 2 * code] + total[2 * code :]
    r.chosen[...] = jnp.concatenate([picked] * taps, axis=0).T
    r.ids_t[...] = jnp.broadcast_to(mark.astype(F32), (blocks, blocks)).T
    expand = jnp.concatenate([r.w_expand[...].astype(F32)] * taps, axis=0).astype(BF)
    r.back_mine[...] = dot_cols(r.out_grad[core, 0], expand)
    r.sent[full:, :] = dot_cols(r.out_grad[1 - core, 0], expand)
    fold = (
        lax.broadcasted_iota(jnp.int32, (code, width), 0)
        == lax.broadcasted_iota(jnp.int32, (code, width), 1) % code
    ).astype(BF)
    latent = dot_rows(r.w_latent[...], fold)
    group = lax.broadcasted_iota(jnp.int32, (out_half, width), 1) // code
    product = jnp.zeros((full, width), F32)
    for index in range(taps):
        copies.wait(loads[index])
        product = product + dot(r.down_v[index], jnp.where(group == index, latent, 0.0).astype(BF))
    r.sent[:full, :] = product


def run_prepare(order, w_down, w_latent, w_expand, out_grad, ids, codebook):
    taps, full, _ = w_down.shape
    width = taps * codebook.shape[0]
    blocks = ids.shape[2]
    square = (VMEM, shape((blocks, width), F32))
    return call(
        order,
        prepare_kernel,
        "prepare",
        dict(
            **any_ins(w_down=w_down, ids=ids, codebook=codebook),
            **vmem_ins(w_latent=w_latent, w_expand=w_expand, out_grad=out_grad),
        ),
        dict(
            sent=(VMEM, shape((full + blocks, width), F32)),
            chosen=square, back_mine=square,
            ids_t=(VMEM, shape((blocks, blocks), F32)),
        ),
        dict(
            down_v=pltpu.VMEM(w_down.shape, BF),
            book_v=pltpu.VMEM(codebook.shape, F32),
            ids_v=pltpu.VMEM(ids.shape[1:], jnp.int32),
            sem=DMA((taps + 2,)),
        ),
    )


def code_grad_kernel(r):
    blocks, width = r.back_mine.shape
    rows, half = r.mine.shape
    code = width // KS
    core = lax.axis_index(CHAN)
    came = r.came.shape[0] - blocks
    back = (r.back_mine[...] + r.came[came:, :]).T[:code, :]
    parts = jnp.concatenate([part.astype(F32) for part in split(back, 3)], axis=0).astype(BF)
    wide = 4
    for first in range(0, rows // code, wide):
        pieces = []
        for lane in range(0, wide * half, blocks):
            number = lax.broadcasted_iota(jnp.int32, (blocks, blocks), 1) + (first * half + lane)
            pieces.append(jnp.where(r.ids_t[...] == number.astype(F32), 1.0, 0.0).astype(BF))
        sums = dot(parts, jnp.concatenate(pieces, axis=1))
        sums = sums[:code] + sums[code : 2 * code] + sums[2 * code :]
        for index in range(wide):
            r.stage[(first + index) * code : (first + index + 1) * code, :] = sums[
                :, index * half : (index + 1) * half
            ]
    down = r.down_sum[...].astype(F32)
    codes = r.stage[...]
    r.mine[...] = jnp.where(core == 0, down, codes).astype(BF)
    r.other[...] = jnp.where(core == 0, codes, down).astype(BF)


def run_code_grad(order, ids_t, back_mine, came, down_sum, codes):
    half = down_sum.shape[1]
    rows = codes // half * (back_mine.shape[1] // KS)
    part = (VMEM, shape((rows, half), BF))
    made = call(
        order,
        code_grad_kernel,
        "code_grads",
        vmem_ins(ids_t=ids_t, back_mine=back_mine, came=came, down_sum=down_sum),
        dict(mine=part, other=part),
        dict(stage=pltpu.VMEM((rows, half), F32)),
    )
    return made["mine"], made["other"]


def down_kernel(span, r):
    taps, full, out_half = r.w_down.shape
    width = r.mine.shape[1] // 2
    code = width // taps
    copies = Copies(r.sem)
    loads = {index: copies.start(r.w_down.at[index], r.down_v.at[index - span[0]]) for index in range(*span)}
    core = lax.axis_index(CHAN)
    total = jnp.where(core == 0, r.mine[...].astype(F32), r.got[...].astype(F32))
    sums = jnp.concatenate([total[:, :width], total[:, width:]], axis=0)
    rounded = sums.astype(BF)
    fold = (
        lax.broadcasted_iota(jnp.int32, (code, width), 0)
        == lax.broadcasted_iota(jnp.int32, (code, width), 1) % code
    ).astype(BF)
    latent = dot_rows(r.w_latent[...], fold)
    group = lax.broadcasted_iota(jnp.int32, (out_half, width), 1) // code
    across = sums.T
    product = r.latent_in[...] if hasattr(r, "latent_in") else jnp.zeros((code, out_half), F32)
    outs = []
    for index in range(*span):
        slot = index % 4
        if len(outs) >= 4:
            copies.wait(outs[-4])
        spread = jnp.where(group == index, latent, 0.0).astype(BF)
        r.out_v[slot] = dot_cols(rounded, spread)
        outs.append(copies.start(r.out_v.at[slot], r.grad_down.at[index]))
        copies.wait(loads[index])
        product = product + dot(
            across[index * code : (index + 1) * code, :].astype(BF), r.down_v[index - span[0]]
        )
    r.grad_latent[...] = product
    copies.wait_all()


def run_down(order, span, mine, got, w_latent, w_down, before=None):
    taps, full, out_half = w_down.shape
    count = span[1] - span[0]
    ins = {}
    if before is not None:
        ins.update(any_ins(down_in=before["grad_down"]))
        ins.update(vmem_ins(latent_in=before["grad_latent"]))
    ins.update(vmem_ins(mine=mine, got=got, w_latent=w_latent))
    ins.update(any_ins(w_down=w_down))
    return call(
        order,
        functools.partial(down_kernel, span),
        "down_grads",
        ins,
        dict(
            grad_down=(ANY, shape(w_down.shape, F32)),
            grad_latent=(VMEM, shape(w_latent.shape, F32)),
        ),
        dict(
            down_v=pltpu.VMEM((count, full, out_half), BF),
            out_v=pltpu.VMEM((4, full, out_half), F32),
            sem=DMA((2 * count,)),
        ),
        aliases=None if before is None else {0: 0},
        limit=SMALL_LIMIT if before is None else VMEM_LIMIT,
    )


def step_kernel(jobs, r):
    copies = Copies(r.sem) if hasattr(r, "sem") else None
    for job in jobs:
        job.load(r, copies)
    for job in jobs:
        job.run(r, copies)
    if copies is not None:
        copies.wait_all()


class Scatter:
    def __init__(self, name, kept, got, bits, large=False, unit=1, ways=1):
        self.name, self.bits, self.large, self.ways = name, bits, large, ways
        self.kept, self.got = kept, got
        self.spec = ANY if large else VMEM
        self.used = sum(array.shape[0] for array in kept)
        self.shape = (-(-self.used // unit) * unit, kept[0].shape[1])

    def ins(self):
        arrays = {f"kept{self.name}_{index}": array for index, array in enumerate(self.kept)}
        arrays.update({f"got{self.name}_{index}": array for index, array in enumerate(self.got)})
        return {name: (self.spec, array) for name, array in arrays.items()}

    def outs(self):
        part = (self.spec, shape((self.shape[0] // (2 * self.ways), self.shape[1]), BF))
        return {kind + self.name + "w" * way: part for way in range(self.ways) for kind in ("sent", "next")}

    def scratch(self):
        rooms = {"room" + self.name: pltpu.VMEM(self.shape, BF)}
        if self.large:
            rooms["other" + self.name] = pltpu.VMEM(self.shape, BF)
        return rooms

    def copies(self):
        return 2 * len(self.kept) + 2 * self.ways if self.large else 0

    def spans(self):
        start = 0
        for index, array in enumerate(self.kept):
            yield index, slice(start, start + array.shape[0])
            start += array.shape[0]

    def load(self, r, copies):
        self.loads = []
        if self.large:
            for index, rows in self.spans():
                there = pl.ds(rows.start, rows.stop - rows.start)
                for kind, room in (("kept", "room"), ("got", "other")):
                    source = getattr(r, f"{kind}{self.name}_{index}")
                    self.loads.append(copies.start(source, getattr(r, room + self.name).at[there]))

    def add(self, r, room, copies):
        for index, rows in self.spans():
            if self.large:
                copies.wait(*self.loads[2 * index : 2 * index + 2])
                kept, got = room[rows, :], getattr(r, "other" + self.name)[rows, :]
            else:
                kept = getattr(r, f"kept{self.name}_{index}")[...]
                got = getattr(r, f"got{self.name}_{index}")[...]
            room[rows, :] = (kept.astype(F32) + got.astype(F32)).astype(BF)

    def run(self, r, copies):
        room = getattr(r, "room" + self.name)
        self.add(r, room, copies)
        if room.shape[0] > self.used:
            room[self.used :, :] = jnp.zeros((room.shape[0] - self.used, room.shape[1]), BF)
        rows = room.shape[0] // (2 * self.ways)
        side = kept_side(self.bits)
        for way in range(self.ways):
            for kind, which in (("sent", 1 - side), ("next", side)):
                target = getattr(r, kind + self.name + "w" * way)
                here = pl.ds(pl.multiple_of((2 * way + which) * rows, 16), rows)
                if self.large:
                    copies.start(room.at[here], target)
                else:
                    target[...] = room[here, :]


class Reduce(Scatter):
    def outs(self):
        return {"sent" + self.name: (VMEM, shape(self.shape, BF))}

    def scratch(self):
        return {}

    def run(self, r, copies):
        self.add(r, getattr(r, "sent" + self.name), copies)


class Gather(Scatter):
    def outs(self):
        rows, columns = self.shape
        return {"sent" + self.name: (VMEM, shape((2 * rows, columns), BF))}

    def scratch(self):
        return {}

    def run(self, r, copies):
        out = getattr(r, "sent" + self.name)
        rows = out.shape[0] // 2
        side = kept_side(self.bits)
        for kind, which in (("kept", side), ("got", 1 - side)):
            here = pl.ds(pl.multiple_of(which * rows, 16), rows)
            out[here, :] = getattr(r, f"{kind}{self.name}_0")[...]


class Add:
    def __init__(self, name, value, got):
        self.name, self.value, self.got = name, value, got

    def ins(self):
        return vmem_ins(**{"value" + self.name: self.value, "came" + self.name: self.got})

    def outs(self):
        return {"total" + self.name: (VMEM, shape(self.value.shape, self.value.dtype))}

    def scratch(self):
        return {}

    def copies(self):
        return 0

    def load(self, r, copies):
        pass

    def run(self, r, copies):
        total = getattr(r, "value" + self.name)[...].astype(F32) + getattr(r, "came" + self.name)[...].astype(F32)
        getattr(r, "total" + self.name)[...] = total.astype(self.value.dtype)


def hold_kernel(r):
    pass


def run_hold(order, arrays):
    names = [f"part{index}" for index in range(len(arrays))]
    outs = {"out" + name: (ANY, shape(array.shape, array.dtype)) for name, array in zip(names, arrays)}
    made = call(
        order, hold_kernel, "hold", any_ins(**dict(zip(names, arrays))), outs, {},
        aliases={index: index for index in range(len(arrays))},
    )
    return [made["out" + name] for name in names]


def run_step(order, sums):
    jobs = [one.job() for one in sums]
    ins, outs, scratch = {}, {}, {}
    for job in jobs:
        ins.update(job.ins())
        outs.update(job.outs())
        scratch.update(job.scratch())
    copies = sum(job.copies() for job in jobs)
    if copies:
        scratch["sem"] = DMA((copies,))
    made = call(
        order,
        functools.partial(step_kernel, jobs),
        "sum_step",
        ins,
        outs,
        scratch,
        limit=VMEM_LIMIT if copies else SMALL_LIMIT,
    )
    for one in sums:
        one.take(made)


def finish_kernel(pieces, kind, r):
    conv_rows = r.conv.shape[1]
    copies = Copies(r.sem)
    loads, edges = [], []
    for index, (unit, piece) in enumerate(pieces):
        there = pl.ds(piece.place, piece.rows)
        loads.append(copies.start(getattr(r, "part" + piece.name).at[there], getattr(r, f"chunk{index}")))
    for index, (unit, piece) in enumerate(pieces):
        side = kept_side(piece.bits)
        which = side if kind == "part" else 1 - side
        rows = piece.rows
        wide = getattr(r, f"wide{index}")
        copies.wait(loads[index])
        wide[...] = getattr(r, f"chunk{index}")[...].astype(F32)
        if piece.start + piece.span + rows <= conv_rows:
            there = pl.ds(pl.multiple_of(piece.start + which * piece.span, 16), rows)
            copies.start(wide, r.conv.at[unit, there])
            continue
        for choice in range(2):
            start = piece.start + choice * piece.span
            edge = min(max(conv_rows - start, 0), rows)
            parts = []
            if edge > 0:
                parts.append((wide.at[pl.ds(0, edge)], r.conv.at[unit, pl.ds(start, edge)]))
            if edge < rows:
                target = r.point.at[unit, pl.ds(start + edge - conv_rows, rows - edge)]
                parts.append((wide.at[pl.ds(edge, rows - edge)], target))
            made = [
                pltpu.make_async_copy(source, target, r.edge_sem.at[index, number])
                for number, (source, target) in enumerate(parts)
            ]
            edges.append((which == choice, made))

            @pl.when(which == choice)
            def _():
                for copy in made:
                    copy.start()

    for chosen, made in edges:

        @pl.when(chosen)
        def _():
            for copy in made:
                copy.wait()

    copies.wait_all()


def run_finish(order, pieces, kind, arrays, before, full):
    half = arrays[0].shape[1]
    ins = {}
    if before is not None:
        ins.update(any_ins(conv_in=before["conv"], point_in=before["point"]))
    ins.update(any_ins(**{f"part{index}": array for index, array in enumerate(arrays)}))
    scratch = {}
    for index, (_, piece) in enumerate(pieces):
        scratch[f"chunk{index}"] = pltpu.VMEM((piece.rows, half), BF)
        scratch[f"wide{index}"] = pltpu.VMEM((piece.rows, half), F32)
    scratch["sem"] = DMA((2 * len(pieces),))
    scratch["edge_sem"] = DMA((len(pieces), 2))
    return call(
        order,
        functools.partial(finish_kernel, pieces, kind),
        "finish",
        ins,
        dict(
            conv=(ANY, shape((3, K * full, half), F32)),
            point=(ANY, shape((3, full, half), F32)),
        ),
        scratch,
        aliases=None if before is None else {0: 0, 1: 1},
    )


def collect_kernel(r):
    half = r.mine.shape[1]
    code = r.w_expand.shape[0]
    core = lax.axis_index(CHAN)
    own, oth = both_columns(half)
    r.rate_v[...] = jnp.zeros(r.rate_v.shape, F32)
    for index in range(7):
        rate = getattr(r, f"rate{index}")
        r.rate_v[index : index + 1, :] = jnp.sum(rate[...], axis=0, keepdims=True)
    r.mine[:8, :] = r.rate_v[:, own]
    r.other[:8, :] = r.rate_v[:, oth]
    r.other[8:, :] = jnp.zeros((r.other.shape[0] - 8, half), F32)
    blocks, width = r.mixed_mine.shape
    wide = jnp.concatenate([r.w_expand[...].astype(F32)] * (width // code), axis=0).astype(BF)
    lane = lax.broadcasted_iota(jnp.int32, (blocks, width), 1)
    total = jnp.zeros((code, r.out_grad.shape[3]), F32)
    for row, mixed in ((core, r.mixed_mine), (1 - core, r.mixed_got)):
        value = mixed[...]
        once = jnp.where(lane < code, value.astype(F32), 0.0).astype(BF)
        r.block_out[row, 0] = dot(once, wide).astype(BF)
        sums = lax.dot_general(
            value, r.out_grad[row, 0], (((0,), (0,)), ((), ())), preferred_element_type=F32
        )
        total = total + sums[:code, :]
    for index in range(total.shape[1] // half):
        r.mine[8 * (index + 1) : 8 * (index + 2), :] = total[:, index * half : (index + 1) * half]


def run_collect(order, rates, mixed_mine, mixed_got, out_grad, w_expand, half):
    part = (VMEM, shape((8 + 8 * (w_expand.shape[1] // half), half), F32))
    made = call(
        order,
        collect_kernel,
        "collect",
        vmem_ins(
            **{f"rate{index}": rate for index, rate in enumerate(rates)},
            mixed_mine=mixed_mine, mixed_got=mixed_got, out_grad=out_grad, w_expand=w_expand,
        ),
        dict(block_out=(VMEM, shape(out_grad.shape, BF)), mine=part, other=part),
        dict(rate_v=pltpu.VMEM((8, 2 * half), F32)),
        limit=SMALL_LIMIT,
    )
    return made["block_out"], made["mine"], made["other"]


def place_kernel(r):
    core = lax.axis_index(CHAN)
    copies = Copies(r.sem)
    frames = r.got.shape[0]
    moved = [
        (copies.start(r.got.at[there], r.room.at[there]), there) for _, there in tiles_of(frames)
    ]
    for number, there in moved:
        copies.wait(number)
        copies.start(r.room.at[there], r.out.at[1 - core, 0, there])
    copies.wait_all()


def run_place(order, mine, got):
    return call(
        order,
        place_kernel,
        "place_rows",
        any_ins(mine=mine, got=got),
        dict(out=(ANY, shape(mine.shape, mine.dtype))),
        dict(room=pltpu.VMEM(got.shape, got.dtype), sem=DMA((2 * (got.shape[0] // TILE),))),
        aliases={0: 0},
        limit=SMALL_LIMIT,
    )["out"]


def codebook_kernel(r):
    rows, half = r.mine.shape
    code = r.codebook.shape[0]
    core = lax.axis_index(CHAN)
    sums = jnp.where(core == 0, r.got[...].astype(F32), r.mine[...].astype(F32))
    for index in range(rows // code):
        r.total[:, index * half : (index + 1) * half] = sums[index * code : (index + 1) * code, :]
    columns = r.codebook[...]
    scale = lax.rsqrt(jnp.sum(columns * columns, axis=0, keepdims=True) + 1.0)
    unit = columns * scale
    grad = r.total[...]
    r.out[...] = scale * (grad - unit * jnp.sum(unit * grad, axis=0, keepdims=True))


def run_codebook(order, mine, got, codebook):
    return call(
        order,
        codebook_kernel,
        "codebook_grads",
        vmem_ins(mine=mine, got=got, codebook=codebook),
        dict(out=(VMEM, shape(codebook.shape, F32))),
        dict(total=pltpu.VMEM(codebook.shape, F32)),
        limit=SMALL_LIMIT,
    )["out"]


def chip_axes(count):
    bits = count.bit_length() - 1
    side = bits // 3
    return list(range(side)), list(range(side, 2 * side)), list(range(2 * side, bits))


def two_orders(count):
    x, y, z = chip_axes(count)
    back = z[::-1]
    return ((x + y + z, y + x + back), (z + y + x, back + y + x))


def first_unit(count, ways):
    return ways * 8 * count


def piece_plan(full, count):
    orders = two_orders(count)
    rows = (K + 1) * full
    cut = 3 * rows // 4
    first = {2: [], 1: [], 0: []}
    later = []
    for seq, (share, start) in enumerate(((cut // 2, 0), ((rows - cut) // 2, cut))):
        bits = (orders[seq][0][0], orders[seq][1][0])
        place = 0
        for unit in (2, 1, 0):
            first[unit].append(Piece(f"{seq}", start, share, place, bits, share))
            place += share
        ways = 2 - seq
        unit_rows = first_unit(count, ways)
        place = -(-place // unit_rows) * unit_rows
        for unit in (2, 1, 0):
            lo = (2 - unit) * share
            for way in range(ways):
                at = max(lo, way * place // ways)
                stop = min(lo + share, (way + 1) * place // ways)
                if stop > at:
                    name = f"{2 * seq + way}"
                    later.append(
                        (unit, Piece(name, start + at - lo, stop - at, at - way * place // ways, bits, share))
                    )
    return first, later


def exchange(values, count, bits):
    pairs = []
    for chip in range(count):
        for core in range(2):
            pairs.append((2 * chip + core, 2 * (chip ^ (1 << bits[core])) + core))
    return lax.ppermute(values, (DP, CHAN), pairs)


def swap(values):
    return lax.ppermute(values, CHAN, [(0, 1), (1, 0)])


class FirstStep:
    def __init__(self, name, count, cores, ways):
        self.name, self.count, self.ways = name, count, ways
        self.steps = list(zip(*cores))
        self.kept = []
        self.got = []

    def begin(self, sent, kept):
        self.kept.append(kept)
        self.got.append(exchange(sent, self.count, self.steps[0]))

    def job(self):
        unit = first_unit(self.count, self.ways)
        return Scatter("f" + self.name, self.kept, self.got, self.steps[1], True, unit, self.ways)

    def take(self, made):
        self.made = [
            (f"{2 * int(self.name) + way}", made["sentf" + self.name + "w" * way], made["nextf" + self.name + "w" * way])
            for way in range(self.ways)
        ]

    def go_on(self, name, sent, kept):
        return PartSum(name, self.count, self.steps, sent, kept)


class PartSum:
    def __init__(self, name, count, steps, sent, kept):
        self.name, self.count, self.steps = name, count, steps
        self.level = 1
        self.scattering = True
        self.kept = [kept]
        self.send(sent)

    def send(self, sent):
        self.sent = sent
        self.got = [exchange(sent, self.count, self.steps[self.level])]

    def job(self):
        if not self.scattering:
            return Gather(self.name, [self.sent], self.got, self.steps[self.level])
        if self.level + 1 < len(self.steps):
            unit = 16 << (len(self.steps) - 1 - self.level)
            return Scatter(self.name, self.kept, self.got, self.steps[self.level + 1], False, unit)
        return Reduce(self.name, self.kept, self.got, None)

    def take(self, made):
        if not self.scattering:
            self.level -= 1
        elif self.level + 1 < len(self.steps):
            self.level += 1
            self.kept = [made["next" + self.name]]
        else:
            self.scattering = False
        self.send(made["sent" + self.name])

    def ready(self):
        return not self.scattering and self.level == 0


class SmallSum:
    def __init__(self, name, mine, other, count, order):
        self.name, self.count, self.order = name, count, order
        self.value = mine
        self.got = swap(other)
        self.level = 0

    def job(self):
        return Add(self.name, self.value, self.got)

    def take(self, made):
        self.value = made["total" + self.name]
        if self.level < len(self.order):
            bit = self.order[self.level]
            self.got = exchange(self.value, self.count, (bit, bit))
        self.level += 1

    def ready(self):
        return self.level > len(self.order)


def shards(
    frames_in,
    utter_lengths,
    code_ids,
    alpha_first,
    alpha_second,
    alpha_last,
    w_dilated,
    w_point,
    w_down,
    w_latent,
    w_expand,
    codebook,
    out_grad,
):
    count = lax.axis_size(DP)
    half = frames_in.shape[3]
    full = 2 * half
    codes = codebook.shape[1]
    order = Order()

    frames_got = swap(frames_in)
    p_got = swap(w_point)
    w_mine = w_dilated.reshape(3, K * full, half)
    w_got = swap(w_mine)
    alpha_rows = jnp.concatenate([alpha_first, alpha_second, alpha_last[None]], axis=0)
    place = (utter_lengths, alpha_rows, swap(alpha_rows))

    ready = run_prepare(order, w_down, w_latent.T, w_expand, out_grad, code_ids, codebook)
    came = swap(ready["sent"])
    made = run_forward(
        order, place, frames_in, frames_got, w_mine, w_got, w_point, p_got,
        dict(
            sent=ready["sent"], came=came,
            chosen=ready["chosen"], back_mine=ready["back_mine"],
        ),
    )
    seen = [made[f"seen{u}"] for u in range(3)]
    rates = [None] * 5 + [made["rates"], made["last_rates"]]
    grads = [None, None, (made["mine"], swap(made["other"]), made["other"])]
    seen_got = [None, None, swap(seen[2])]
    running, dilated, grad = made["running"], made["dilated"], made["grad"]

    def open_unit(u, grad):
        made = run_opening(
            order, u, place, grads[u][0], grads[u][2], running, grad, dilated, w_mine, w_got, w_point, p_got
        )
        rates[u] = made["rates"]
        if u > 0:
            rates[2 + u] = made["mid_rates"]
            grads[u - 1] = (made["mine"], swap(made["other"]), made["other"])
        return made

    x, y, z = chip_axes(count)
    code_mine, code_sent = run_code_grad(
        order, ready["ids_t"], ready["back_mine"], came, made["down_sum"], codes
    )
    codes_sum = SmallSum("", code_mine, code_sent, count, z[::-1] + y + x)
    plan, later = piece_plan(full, count)
    firsts = [
        FirstStep(f"{index}", count, cores, 2 - index) for index, cores in enumerate(two_orders(count))
    ]

    def weigh(u):
        made = run_weight(
            order, u, place, seen[u], seen_got[u], grads[u][0], grads[u][1], plan[u],
            (codes_sum.value, codes_sum.got) if u > 0 else None,
        )
        if u > 0:
            codes_sum.take(made)
        for index, one in enumerate(firsts):
            one.begin(made[f"sent{index}"], made[f"kept{index}"])

    grad = open_unit(2, grad)["grad"]
    seen_got[1] = swap(seen[1])
    order.before += [seen_got[1]]
    weigh(2)
    first = [one.got[0] for one in firsts]
    grad = open_unit(1, grad)["grad"]
    seen_got[0] = swap(seen[0])
    mixed_got = swap(made["mixed"])
    order.before += first + [seen_got[0], mixed_got]
    weigh(1)
    weigh(0)
    order.before += [one.got[1] for one in firsts] + [codes_sum.got]
    last = open_unit(0, grad)
    run_step(order, firsts + [codes_sum])
    (name0, sent0, kept0), (name1, sent1, kept1) = firsts[0].made
    [(name2, sent2, kept2)] = firsts[1].made
    sums = [firsts[0].go_on(name0, sent0, kept0)]
    sent1, sent2, frames_sent = run_hold(order, [sent1, sent2, last["frames_sent"]])
    sums += [firsts[0].go_on(name1, sent1, kept1), firsts[1].go_on(name2, sent2, kept2)]

    def advance(*more, between=None):
        if not sums[0].scattering:
            order.before.append(swap(sums[0].got[0][:16]))
        run_step(order, sums[:1])
        made = between() if between else None
        run_step(order, sums[1:] + [one for one in more if not one.ready()])
        return made

    block_out, small_mine, small_other = run_collect(
        order, rates, made["mixed"], mixed_got, out_grad, w_expand, half
    )
    small = SmallSum("small", small_mine, small_other, count, z + y + x)
    grad_frames = run_place(order, last["frames_mine"], swap(frames_sent))
    while not (codes_sum.ready() or sums[0].ready()):
        advance(codes_sum, small)
    codes_back = swap(codes_sum.value)
    advance(small)
    grad_codebook = run_codebook(order, codes_sum.value, codes_back, codebook)
    taps = w_down.shape[0]
    downs = advance(
        small,
        between=lambda: run_down(order, (0, taps // 2), codes_sum.value, codes_back, w_latent.T, w_down),
    )
    while not sums[0].ready():
        advance(small)
    parts, gots = [one.sent for one in sums], [one.got[0] for one in sums]
    written = run_finish(order, later, "part", parts, None, full)
    soon = [(unit, piece) for unit, piece in later if piece.name == "0"]
    written = run_finish(order, soon, "got", gots[:1], written, full)
    downs = run_down(order, (taps // 2, taps), codes_sum.value, codes_back, w_latent.T, w_down, downs)
    while not small.ready():
        run_step(order, [small])
    rest = [(unit, piece) for unit, piece in later if piece.name != "0"]
    written = run_finish(order, rest, "got", gots, written, full)
    grad_w_dilated, grad_w_point = written["conv"], written["point"]
    small = small.value
    return (
        block_out,
        grad_frames,
        small[0:3],
        small[3:6],
        small[6],
        grad_w_dilated.reshape(3, K, full, half),
        grad_w_point,
        downs["grad_down"],
        downs["grad_latent"].T,
        jnp.concatenate(
            [small[start : start + 8] for start in range(8, small.shape[0], 8)], axis=1
        ),
        grad_codebook,
    )


def solution(mesh):
    placed = (
        P(None, DP, None, CHAN),
        P(None, DP, None),
        P(None, DP, None),
        P(None, CHAN),
        P(None, CHAN),
        P(CHAN),
        P(None, None, None, CHAN),
        P(None, None, CHAN),
        P(None, None, CHAN),
        P(CHAN, None),
        P(None, CHAN),
        P(),
        P(None, DP, None, CHAN),
    )
    return jax.shard_map(
        shards,
        mesh=mesh,
        in_specs=placed,
        out_specs=(
            P(None, DP, None, CHAN),
            P(None, DP, None, CHAN),
            P(None, CHAN),
            P(None, CHAN),
            P(CHAN),
            P(None, None, None, CHAN),
            P(None, None, CHAN),
            P(None, None, CHAN),
            P(CHAN, None),
            P(None, CHAN),
            P(),
        ),
        check_vma=False,
    )
```
